256 devices in a mesh: dp: 16 (over x_hi, y, core), tile: 16 (over x_lo, z).
Axes of the slice: x: 4 (x_hi: 2, x_lo: 2; x = x_hi * 2 + x_lo), y: 4, z: 8, core: 2. Of those that a mesh axis runs over, the one named last changes fastest.
Arguments:
- fields_in: bfloat16 [16, 16, 2, 32, 32, 256], P('dp', 'tile'), may hold values from -6 to 6
- state_start: float32 [16, 16, 32, 32, 256], P('dp', 'tile'), may hold values from -0.9 to 0.9
- state_adjoint: float32 [16, 16, 32, 32, 256], P('dp', 'tile'), may hold values from -12 to 12
- output_grad: bfloat16 [16, 16, 2, 8, 1024], P('dp', 'tile'), may hold values from -12 to 12
- conv_weight: bfloat16 [9, 256, 256], replicated, may hold values from -0.125 to 0.125
- w_update: bfloat16 [512, 256], replicated, may hold values from -0.25 to 0.25
- w_reset: bfloat16 [512, 256], replicated, may hold values from -0.25 to 0.25
- w_candidate: bfloat16 [512, 256], replicated, may hold values from -0.25 to 0.25
- head_weight: bfloat16 [8, 256], replicated, may hold values from -0.375 to 0.375
- neighbor_tile: int32 [16, 4], replicated, may hold values from 0 to 15, as said below
- seam_turns: int32 [16, 4], replicated, may hold values from 0 to 2, as said below
Outputs:
- grad_fields: bfloat16 [16, 16, 2, 32, 32, 256], P('dp', 'tile')
- grad_state: float32 [16, 16, 32, 32, 256], P('dp', 'tile')
- grad_conv: float32 [9, 256, 256], P(None, 'tile')
- grad_update: float32 [512, 256], P(None, 'tile')
- grad_reset: float32 [512, 256], P(None, 'tile')
- grad_candidate: float32 [512, 256], P(None, 'tile')
- grad_head: float32 [8, 256], P(None, 'tile')
The draws below stay inside these ranges and needn't reach their ends.
Inputs may be any that keep to these rules, and one draw needn't show every extreme that they name: The tiles form a closed belt: side 1 of tile s meets side 3 of tile (s + 1) mod 16. The tiles are paired as mates (2 m + o, 2 m + 1 + o) mod 16 for one o in 0, 1; sides 0 and 2 of a tile meet sides 0 or 2 of itself or of its mate. Gluing is mutual: if side k of s meets side j of t = neighbor_tile[s, k], then neighbor_tile[t, j] = s and the side of t that meets s is j. The rotation code of the seam described with neighbor_tile: side k of tile s meets side (k + 2 - seam_turns[s, k]) mod 4 of its neighbour.
All inputs are finite; a program needn't handle non-finite values.
Results may differ from the reference program's by a relative error of at most 0.007.
Values may be sent and summed in bfloat16 or wider, within the bound.
No kernel may reach another device: no remote copies, remote signals or barrier semaphores. Data moves between devices by JAX's collectives and lax.ppermute only.
A program may use at most 128 MiB of HBM per device.

```python
import math
import jax
import jax.numpy as jnp
from jax import lax

C = 256
VARS = 8
SIDE = 32
STEPS = 2
TILES = 16
BATCH = 16
CELLS = 1024


def belt_plan(key):
    offset = jax.random.randint(jax.random.fold_in(key, 5), (), 0, 2).astype(jnp.int32)
    pairs = TILES // 2
    kinds = jax.random.randint(jax.random.fold_in(key, 6), (pairs,), 0, 5).astype(jnp.int32)
    chosen = jax.random.randint(jax.random.fold_in(key, 7), (), 0, pairs).astype(jnp.int32)
    slots = jnp.arange(pairs, dtype=jnp.int32)
    kinds = jnp.where(slots == chosen, 1, kinds)
    kinds = jnp.where(slots == (chosen + 1) % pairs, 0, kinds).astype(jnp.int32)
    tiles = jnp.arange(TILES, dtype=jnp.int32)
    shifted = (tiles - offset) % TILES
    mate = jnp.where(shifted % 2 == 0, (tiles + 1) % TILES, (tiles - 1 + TILES) % TILES).astype(jnp.int32)
    kind = kinds[shifted // 2]
    after = (tiles + 1) % TILES
    before = (tiles - 1 + TILES) % TILES
    top_mate = (kind == 0) | (kind == 1) | (kind == 3)
    bottom_mate = (kind == 0) | (kind == 1) | (kind == 4)
    top_tile = jnp.where(top_mate, mate, tiles).astype(jnp.int32)
    bottom_tile = jnp.where(bottom_mate, mate, tiles).astype(jnp.int32)
    neighbor = jnp.stack([top_tile, after, bottom_tile, before], axis=1).astype(jnp.int32)
    half = jnp.where((kind == 1) | (kind == 2), 0, 2).astype(jnp.int32)
    zero = jnp.zeros_like(half)
    turns = jnp.stack([half, zero, half, zero], axis=1).astype(jnp.int32)
    return (neighbor, turns)


def draw_neighbor_tile(key, part):
    neighbor, turns = belt_plan(key)
    return neighbor


def draw_seam_turns(key, part):
    neighbor, turns = belt_plan(key)
    return turns


def level_of(key, dims, shards, smallest, top_value):
    def one(axis_at, shards_of):
        draws = jax.random.uniform(jax.random.fold_in(jax.random.fold_in(key, 6), axis_at), (shards_of,), jnp.float32, smallest / len(shards), top_value / len(shards))
        return jnp.repeat(jnp.exp(draws), dims[axis_at] // shards_of).reshape((-1,) + (1,) * (len(dims) - axis_at - 1))

    loudness = one(*shards[0])
    for cut in shards[1:]:
        loudness = loudness * one(*cut)
    return loudness


def scatter_about(rng, dims, scale, limit, cuts=(), kind=jnp.bfloat16):
    entries = jax.random.normal(rng, dims, jnp.float32) * scale
    if len(cuts) > 0:
        entries = level_of(rng, dims, cuts, -0.22, 0.18) * entries
    return jnp.clip(entries, min=-limit, max=limit).astype(kind)


def setup_inputs(seed: int = 0) -> dict:
    splits = jax.random.split(jax.random.key(seed), 12)
    fields_in = scatter_about(splits[0], (BATCH, TILES, STEPS, SIDE, SIDE, C), 1.0, 6.0, ((0, 16), (1, 16)))
    state_start = jnp.clip(jax.random.uniform(splits[1], (BATCH, TILES, SIDE, SIDE, C), jnp.float32, -0.9, 0.9) * level_of(splits[1], (BATCH, TILES, SIDE, SIDE, C), ((0, 16), (1, 16)), -0.4, 0.0), -0.9, 0.9)
    state_adjoint = scatter_about(splits[2], (BATCH, TILES, SIDE, SIDE, C), 2.0, 12.0, ((0, 16), (1, 16)), jnp.float32)
    output_grad = scatter_about(splits[3], (BATCH, TILES, STEPS, VARS, CELLS), 2.0, 12.0, ((0, 16), (1, 16)))
    conv_weight = scatter_about(splits[4], (9, C, C), (9 * C) ** -0.5, 0.125)
    w_update = scatter_about(splits[5], (2 * C, C), (2 * C) ** -0.5, 0.25)
    w_reset = scatter_about(splits[6], (2 * C, C), (2 * C) ** -0.5, 0.25)
    w_candidate = scatter_about(splits[7], (2 * C, C), (2 * C) ** -0.5, 0.25)
    head_weight = scatter_about(splits[8], (VARS, C), C ** -0.5, 0.375)
    neighbor_tile = draw_neighbor_tile(jax.random.fold_in(splits[11], 71), 0)
    seam_turns = draw_seam_turns(jax.random.fold_in(splits[11], 71), 0)
    return dict(fields_in=fields_in, state_start=state_start, state_adjoint=state_adjoint, output_grad=output_grad, conv_weight=conv_weight, w_update=w_update, w_reset=w_reset, w_candidate=w_candidate, head_weight=head_weight, neighbor_tile=neighbor_tile, seam_turns=seam_turns)


CUBIC = 0.044715
ROOT = math.sqrt(2.0 / math.pi)

def edges_of(field):
    top = field[..., 0, :, :]
    right = field[..., :, -1, :]
    bottom = jnp.flip(field[..., -1, :, :], axis=-2)
    left = jnp.flip(field[..., :, 0, :], axis=-2)
    return jnp.stack([top, right, bottom, left], axis=-3)

def add_edges(field, extra):
    field = field.at[..., 0, :, :].add(extra[..., 0, :, :])
    field = field.at[..., :, -1, :].add(extra[..., 1, :, :])
    field = field.at[..., -1, :, :].add(jnp.flip(extra[..., 2, :, :], axis=-2))
    field = field.at[..., :, 0, :].add(jnp.flip(extra[..., 3, :, :], axis=-2))
    return field

def pad_with(field, halo):
    left = jnp.flip(halo[:, 3], axis=1)[:, :, None, :]
    right = halo[:, 1][:, :, None, :]
    middle = jnp.concatenate([left, field, right], axis=2)
    corner = jnp.zeros_like(halo[:, 0, :1, :])
    top = jnp.concatenate([corner, halo[:, 0], corner], axis=1)[:, None]
    bottom = jnp.concatenate([corner, jnp.flip(halo[:, 2], axis=1), corner], axis=1)[:, None]
    return jnp.concatenate([top, middle, bottom], axis=1)

def cycle_of(grad_pad):
    top = grad_pad[:, 0, 1:-1]
    right = grad_pad[:, 1:-1, -1]
    bottom = jnp.flip(grad_pad[:, -1, 1:-1], axis=1)
    left = jnp.flip(grad_pad[:, 1:-1, 0], axis=1)
    return jnp.stack([top, right, bottom, left], axis=1)

def conv_pre(padded, conv_weight):
    side = padded.shape[1] - 2
    width = padded.shape[-1]
    result = jnp.zeros((padded.shape[0] * side * side, conv_weight.shape[2]), jnp.float32)
    for tap in range(9):
        window = padded[:, tap // 3:tap // 3 + side, tap % 3:tap % 3 + side, :].reshape(-1, width)
        result = result + jnp.dot(window, conv_weight[tap], preferred_element_type=jnp.float32)
    return result

def local_backward(fields, halos, state, adjoint, output_grad, weights):
    conv_weight, w_update, w_reset, w_candidate, head_weight = weights
    tiles_here = fields.shape[0]
    steps = fields.shape[1]
    side = fields.shape[2]
    width = fields.shape[-1]
    hidden = state.reshape(-1, width)
    saved = []
    for step in range(steps):
        padded = pad_with(fields[:, step], halos[:, step])
        raw_conv = conv_pre(padded, conv_weight)
        bend = jnp.tanh(ROOT * (raw_conv + CUBIC * raw_conv * raw_conv * raw_conv))
        feature = (0.5 * raw_conv * (1.0 + bend)).astype(jnp.bfloat16)
        joined = jnp.concatenate([feature, hidden.astype(jnp.bfloat16)], axis=1)
        update = jax.nn.sigmoid(jnp.dot(joined, w_update, preferred_element_type=jnp.float32))
        reset = jax.nn.sigmoid(jnp.dot(joined, w_reset, preferred_element_type=jnp.float32))
        gated = (reset * hidden).astype(jnp.bfloat16)
        joined_gate = jnp.concatenate([feature, gated], axis=1)
        candidate = jnp.tanh(jnp.dot(joined_gate, w_candidate, preferred_element_type=jnp.float32))
        following = hidden + update * (candidate - hidden)
        saved.append((padded, raw_conv, bend, joined, update, reset, joined_gate, candidate, hidden, following))
        hidden = following
    carried = adjoint.reshape(-1, width)
    conv_grads = [jnp.zeros(conv_weight.shape[1:], jnp.float32) for tap in range(9)]
    grad_update = jnp.zeros(w_update.shape, jnp.float32)
    grad_reset = jnp.zeros(w_reset.shape, jnp.float32)
    grad_candidate = jnp.zeros(w_candidate.shape, jnp.float32)
    grad_head = jnp.zeros(head_weight.shape, jnp.float32)
    grad_middles = [None] * steps
    cycles = [None] * steps
    for step in reversed(range(steps)):
        padded, raw_conv, bend, joined, update, reset, joined_gate, candidate, hidden, following = saved[step]
        grad_out = jnp.transpose(output_grad[:, step], (1, 0, 2)).reshape(output_grad.shape[2], -1)
        grad_head = grad_head + jnp.dot(grad_out, following.astype(jnp.bfloat16), preferred_element_type=jnp.float32)
        overall = carried + jnp.dot(grad_out.T, head_weight, preferred_element_type=jnp.float32)
        part_cand = (overall * update * (1.0 - candidate * candidate)).astype(jnp.bfloat16)
        part_update = (overall * (candidate - hidden) * update * (1.0 - update)).astype(jnp.bfloat16)
        back_cand = jnp.dot(part_cand, w_candidate.T, preferred_element_type=jnp.float32)
        grad_gated = back_cand[:, width:]
        part_reset = (grad_gated * hidden * reset * (1.0 - reset)).astype(jnp.bfloat16)
        back_joined = jnp.dot(part_update, w_update.T, preferred_element_type=jnp.float32) + jnp.dot(part_reset, w_reset.T, preferred_element_type=jnp.float32)
        carried = overall * (1.0 - update) + grad_gated * reset + back_joined[:, width:]
        grad_feature = back_cand[:, :width] + back_joined[:, :width]
        slope = 0.5 * (1.0 + bend) + 0.5 * raw_conv * (1.0 - bend * bend) * ROOT * (1.0 + 3.0 * CUBIC * raw_conv * raw_conv)
        part_conv = (grad_feature * slope).astype(jnp.bfloat16)
        grad_candidate = grad_candidate + jnp.dot(joined_gate.T, part_cand, preferred_element_type=jnp.float32)
        grad_update = grad_update + jnp.dot(joined.T, part_update, preferred_element_type=jnp.float32)
        grad_reset = grad_reset + jnp.dot(joined.T, part_reset, preferred_element_type=jnp.float32)
        grad_pad = jnp.zeros(padded.shape, jnp.float32)
        for tap in range(9):
            row_at = tap // 3
            col_at = tap % 3
            window = padded[:, row_at:row_at + side, col_at:col_at + side, :].reshape(-1, width)
            conv_grads[tap] = conv_grads[tap] + jnp.dot(window.T, part_conv, preferred_element_type=jnp.float32)
            spread = jnp.dot(part_conv, conv_weight[tap].T, preferred_element_type=jnp.float32)
            grad_pad = grad_pad.at[:, row_at:row_at + side, col_at:col_at + side, :].add(spread.reshape(tiles_here, side, side, width))
        grad_middles[step] = grad_pad[:, 1:-1, 1:-1]
        cycles[step] = cycle_of(grad_pad).astype(jnp.bfloat16)
    grads = (jnp.stack(conv_grads, axis=0), grad_update, grad_reset, grad_candidate, grad_head)
    return (jnp.stack(grad_middles, axis=1), jnp.stack(cycles, axis=1), carried.reshape(state.shape), grads)

def partner_pick(array, neighbor_tile, partner_side):
    moved = jnp.transpose(array, (1, 3, 0, 2, 4, 5))
    picked = moved[neighbor_tile, partner_side]
    return jnp.flip(jnp.transpose(picked, (2, 0, 3, 1, 4, 5)), axis=-2)

def reference(fields_in, state_start, state_adjoint, output_grad, conv_weight, w_update, w_reset, w_candidate, head_weight, neighbor_tile, seam_turns):
    weights = (conv_weight, w_update, w_reset, w_candidate, head_weight)
    partner_side = (jnp.arange(4, dtype=jnp.int32)[None, :] + 2 - seam_turns) % 4
    halos = partner_pick(edges_of(fields_in), neighbor_tile, partner_side)

    def one_member(sums, member):
        field, halo, start, adjoint, grad_out = member
        grad_middle, cycle, grad_start, grads = local_backward(field, halo, start, adjoint, grad_out, weights)
        sums = tuple((left + right for left, right in zip(sums, grads)))
        return (sums, (grad_middle, cycle, grad_start))
    initial = (jnp.zeros(conv_weight.shape, jnp.float32), jnp.zeros(w_update.shape, jnp.float32), jnp.zeros(w_reset.shape, jnp.float32), jnp.zeros(w_candidate.shape, jnp.float32), jnp.zeros(head_weight.shape, jnp.float32))
    sums, (grad_middle, cycles, grad_start) = lax.scan(one_member, initial, (fields_in, halos, state_start, state_adjoint, output_grad))
    extra = partner_pick(cycles, neighbor_tile, partner_side).astype(jnp.float32)
    grad_fields = add_edges(grad_middle, extra).astype(jnp.bfloat16)
    return (grad_fields, grad_start, sums[0], sums[1], sums[2], sums[3], sums[4])
```

```python
import math

import jax
import jax.numpy as jnp
from jax import lax
from jax.experimental import pallas as pl
from jax.experimental.pallas import tpu as pltpu
from jax.sharding import Mesh
from jax.sharding import PartitionSpec as P

CUBIC = 0.044715
ROOT = math.sqrt(2.0 / math.pi)
BF = jnp.bfloat16
F32 = jnp.float32
SIDE = 32
CELLS = SIDE * SIDE
C = 256
STEPS = 2
CHUNK = 256
VMEM_LIMIT = 60 * 1024 * 1024


def mm(a, b):
    return lax.dot_general(a, b, (((1,), (0,)), ((), ())), preferred_element_type=F32)


def mm_nt(a, b):
    return lax.dot_general(a, b, (((1,), (1,)), ((), ())), preferred_element_type=F32)


def mm_tn(a, b):
    return lax.dot_general(a, b, (((0,), (0,)), ((), ())), preferred_element_type=F32)


def one_hot(cond):
    return jnp.where(cond, 1.0, 0.0).astype(BF)


def iota(shape, dim):
    return lax.broadcasted_iota(jnp.int32, shape, dim)


def column_pick(first_col):
    rows = iota((SIDE, CELLS), 0)
    cells = iota((SIDE, CELLS), 1)
    return one_hot(cells == rows * SIDE + first_col)


def edges_kernel(fields_ref, to_next_ref, to_prev_ref):
    left = column_pick(0)
    right = column_pick(SIDE - 1)
    for step in range(STEPS):
        flat = fields_ref[step].reshape(CELLS, C)
        to_next_ref[step, 0] = mm(right, flat).astype(BF)
        to_prev_ref[step, 0] = mm(left, flat).astype(BF)
        for ref in (to_next_ref, to_prev_ref):
            ref[step, 1] = fields_ref[step, 0]
            ref[step, 2] = fields_ref[step, SIDE - 1]


def seam_rows(info_ref, own_top, own_bottom, from_prev, from_next):
    stacked = jnp.concatenate(
        [own_top, own_bottom, from_prev[1], from_prev[2], from_next[1], from_next[2]], axis=0
    )
    rows = iota((2 * SIDE, 6 * SIDE), 0)
    cols = iota((2 * SIDE, 6 * SIDE), 1)
    top_base, top_sign, bottom_base, bottom_sign = (info_ref[i] for i in range(4))
    wanted = jnp.where(
        rows < SIDE, top_base + top_sign * rows, bottom_base + bottom_sign * (rows - SIDE)
    )
    return mm(one_hot(cols == wanted), stacked)


def store_shifts(ref, step, low, high, middle, left, right):
    col = iota((SIDE, SIDE, C), 1)
    before = jnp.where(col == 0, left[:, None, :], pltpu.roll(middle, 1, axis=1))
    after = jnp.where(col == SIDE - 1, right[:, None, :], pltpu.roll(middle, SIDE - 1, axis=1))
    body = pl.ds(SIDE, CELLS)
    ref[step, body, 0:C] = before.reshape(CELLS, C).astype(BF)
    ref[step, body, C : 2 * C] = middle.reshape(CELLS, C).astype(BF)
    ref[step, body, 2 * C : 3 * C] = after.reshape(CELLS, C).astype(BF)
    col = iota((SIDE, C), 0)
    for at, line in ((0, low), (SIDE + CELLS, high)):
        row = pl.ds(at, SIDE)
        ref[step, row, 0:C] = jnp.where(col == 0, 0.0, pltpu.roll(line, 1, axis=0)).astype(BF)
        ref[step, row, C : 2 * C] = line.astype(BF)
        ref[step, row, 2 * C : 3 * C] = jnp.where(
            col == SIDE - 1, 0.0, pltpu.roll(line, SIDE - 1, axis=0)
        ).astype(BF)


def main_kernel(
    info_ref,
    fields_ref,
    prev_ref,
    next_ref,
    state_ref,
    adjoint_ref,
    grad_out_ref,
    conv_ref,
    update_ref,
    reset_ref,
    candidate_ref,
    head_ref,
    grad_state_ref,
    part_conv_ref,
    to_next_ref,
    to_prev_ref,
    keep_ref,
    send_ref,
    windows,
    joined,
    gated_all,
    parts,
    last_state,
):
    for step in range(STEPS):
        seams = seam_rows(
            info_ref, fields_ref[step, 0], fields_ref[step, SIDE - 1], prev_ref[step], next_ref[step]
        )
        store_shifts(
            windows,
            step,
            seams[:SIDE],
            seams[SIDE:],
            fields_ref[step].astype(F32),
            prev_ref[step, 0].astype(F32),
            next_ref[step, 0].astype(F32),
        )

    def chunk(index, _):
        start = pl.multiple_of(index * CHUNK, CHUNK)
        rows = pl.ds(start, CHUNK)
        hidden = state_ref[rows, :]
        saved = []
        for step in range(STEPS):
            raw = jnp.zeros((CHUNK, C), F32)
            for p in range(3):
                window = windows[step, pl.ds(start + p * SIDE, CHUNK), :]
                raw = raw + mm(window, conv_ref[pl.ds(3 * C * p, 3 * C), :])
            bend = jnp.tanh(raw * (ROOT + (ROOT * CUBIC) * (raw * raw)))
            feature = (0.5 * raw * (1.0 + bend)).astype(BF)
            joined[step, rows, 0:C] = feature
            joined[step, rows, C : 2 * C] = hidden.astype(BF)
            both = joined[step, rows, :]
            update = 0.5 * jnp.tanh(0.5 * mm(both, update_ref[...])) + 0.5
            reset = 0.5 * jnp.tanh(0.5 * mm(both, reset_ref[...])) + 0.5
            gated = (reset * hidden).astype(BF)
            gated_all[step, rows, :] = gated
            candidate = jnp.tanh(
                mm(feature, candidate_ref[0:C, :]) + mm(gated, candidate_ref[C : 2 * C, :])
            )
            following = hidden + update * (candidate - hidden)
            saved.append((raw, bend, update, reset, candidate, hidden))
            hidden = following
        last_state[rows, :] = hidden.astype(BF)
        carried = adjoint_ref[rows, :]
        for step in reversed(range(STEPS)):
            raw, bend, update, reset, candidate, hidden = saved[step]
            total = carried + mm_tn(grad_out_ref[step, :, rows], head_ref[...])
            keep = 1.0 - update
            scaled = total * update
            part_cand = (scaled * (1.0 - candidate * candidate)).astype(BF)
            part_update = (scaled * (candidate - hidden) * keep).astype(BF)
            grad_gated = mm_nt(part_cand, candidate_ref[C : 2 * C, :])
            part_reset = (grad_gated * hidden * reset * (1.0 - reset)).astype(BF)
            parts[step, rows, 0:C] = part_cand
            parts[step, rows, C : 2 * C] = part_update
            parts[step, rows, 2 * C : 3 * C] = part_reset
            carried = (
                total * keep
                + grad_gated * reset
                + mm_nt(part_update, update_ref[C : 2 * C, :])
                + mm_nt(part_reset, reset_ref[C : 2 * C, :])
            )
            grad_feature = (
                mm_nt(part_cand, candidate_ref[0:C, :])
                + mm_nt(part_update, update_ref[0:C, :])
                + mm_nt(part_reset, reset_ref[0:C, :])
            )
            slope = 0.5 * (1.0 + bend) + (0.5 * ROOT) * raw * (1.0 - bend * bend) * (
                1.0 + (3.0 * CUBIC) * (raw * raw)
            )
            part_conv_ref[step, rows, :] = (grad_feature * slope).astype(BF)
        grad_state_ref[rows, :] = carried
        return 0

    lax.fori_loop(0, CELLS // CHUNK, chunk, 0)

    core = info_ref[4]

    def share(block, value):
        value = value.reshape(16, 16, C)
        rows = pl.ds((block % 8) * 16, 16)

        @pl.when(core == block // 8)
        def _():
            keep_ref[:, rows, :] = value

        @pl.when(core != block // 8)
        def _():
            send_ref[:, rows, :] = value.astype(BF)

    def over_steps(one):
        return one(0) + one(1)

    for gate in range(2):
        lanes = slice(C * (gate + 1), C * (gate + 2))
        grad = over_steps(lambda s: mm_tn(parts[s, :, lanes], joined[s]))
        share(9 + 2 * gate, grad[:, :C])
        share(10 + 2 * gate, grad[:, C:])
    share(13, over_steps(lambda s: mm_tn(parts[s, :, 0:C], joined[s, :, 0:C])))
    share(14, over_steps(lambda s: mm_tn(parts[s, :, 0:C], gated_all[s])))
    grad_head = mm(grad_out_ref[0], joined[1, :, C : 2 * C]) + mm(grad_out_ref[1], last_state[...])
    grad_head = jnp.concatenate([grad_head, jnp.zeros((C - 8, C), F32)], axis=0)
    share(15, grad_head.T)
    for p in range(3):
        grad = over_steps(
            lambda s: mm_tn(part_conv_ref[s], windows[s, pl.ds(p * SIDE, CELLS), :])
        )
        for q in range(3):
            share(3 * p + q, grad[:, q * C : (q + 1) * C].T)

    picks = []
    row = iota((SIDE, CELLS), 0)
    cell = iota((SIDE, CELLS), 1)
    for col in (0, SIDE - 1):
        for p in range(3):
            at = row + 1 - p
            picks.append(one_hot((cell == at * SIDE + col) & (at >= 0) & (at < SIDE)))
    for line in (0, SIDE - 1):
        for q in range(3):
            at = row + 1 - q
            picks.append(one_hot((cell == line * SIDE + at) & (at >= 0) & (at < SIDE)))
    picks = jnp.concatenate(picks, axis=0)
    taps = [0, 3, 6, 2, 5, 8, 0, 1, 2, 6, 7, 8]
    for step in range(STEPS):
        picked = mm(picks, part_conv_ref[step]).astype(BF)
        outside = []
        for side in range(4):
            total = jnp.zeros((SIDE, C), F32)
            for k in range(3 * side, 3 * side + 3):
                total = total + mm_nt(
                    picked[k * SIDE : (k + 1) * SIDE], conv_ref[taps[k] * C : (taps[k] + 1) * C, :]
                )
            outside.append(total.astype(BF))
        to_next_ref[step, 0] = outside[1]
        to_prev_ref[step, 0] = outside[0]
        for ref in (to_next_ref, to_prev_ref):
            ref[step, 1] = outside[2]
            ref[step, 2] = outside[3]


def fields_kernel(
    info_ref,
    part_conv_ref,
    own_ref,
    prev_ref,
    next_ref,
    conv_ref,
    grad_fields_ref,
    shifted,
):
    zero = jnp.zeros((SIDE, C), F32)
    for step in range(STEPS):
        store_shifts(
            shifted,
            step,
            zero,
            zero,
            part_conv_ref[step].astype(F32).reshape(SIDE, SIDE, C),
            zero,
            zero,
        )
        seams = seam_rows(info_ref, own_ref[step, 1], own_ref[step, 2], prev_ref[step], next_ref[step])
        left = prev_ref[step, 0].astype(F32)
        right = next_ref[step, 0].astype(F32)
        for part in range(4):
            at = part * 8
            grad = jnp.zeros((CHUNK, C), F32)
            for p in range(3):
                for q in range(3):
                    lanes = slice((2 - q) * C, (3 - q) * C)
                    window = shifted[step, pl.ds((at + 2 - p) * SIDE, CHUNK), lanes]
                    tap = 3 * p + q
                    grad = grad + mm_nt(window, conv_ref[tap * C : (tap + 1) * C, :])
            grad = grad.reshape(8, SIDE, C)
            col = iota((8, SIDE, C), 1)
            row = iota((8, SIDE, C), 0)
            grad = grad + jnp.where(col == 0, left[at : at + 8][:, None, :], 0.0)
            grad = grad + jnp.where(col == SIDE - 1, right[at : at + 8][:, None, :], 0.0)
            if part == 0:
                grad = grad + jnp.where(row == 0, seams[:SIDE][None], 0.0)
            if part == 3:
                grad = grad + jnp.where(row == 7, seams[SIDE:][None], 0.0)
            grad_fields_ref[step, at : at + 8] = grad.astype(BF)


def in_vmem():
    return pl.BlockSpec(memory_space=pltpu.VMEM)


def in_smem():
    return pl.BlockSpec(memory_space=pltpu.SMEM)


def params():
    return pltpu.CompilerParams(vmem_limit_bytes=VMEM_LIMIT)


def shape(dims, kind=BF):
    return jax.ShapeDtypeStruct(dims, kind)


EDGE = (STEPS, 3, SIDE, C)


def edges_call(fields):
    return pl.pallas_call(
        edges_kernel,
        out_shape=(shape(EDGE), shape(EDGE)),
        in_specs=[in_vmem()],
        out_specs=(in_vmem(), in_vmem()),
        compiler_params=params(),
        name="edges",
    )(fields)


def main_call(info, fields, prev, following, state, adjoint, grad_out, conv, update, reset, cand, head):
    return pl.pallas_call(
        main_kernel,
        out_shape=(
            shape((CELLS, C), F32),
            shape((STEPS, CELLS, C)),
            shape(EDGE),
            shape(EDGE),
            shape((16, 128, C), F32),
            shape((16, 128, C)),
        ),
        in_specs=[in_smem()] + [in_vmem()] * 11,
        out_specs=tuple([in_vmem()] * 6),
        scratch_shapes=[
            pltpu.VMEM((STEPS, CELLS + 2 * SIDE, 3 * C), BF),
            pltpu.VMEM((STEPS, CELLS, 2 * C), BF),
            pltpu.VMEM((STEPS, CELLS, C), BF),
            pltpu.VMEM((STEPS, CELLS, 3 * C), BF),
            pltpu.VMEM((CELLS, C), BF),
        ],
        compiler_params=params(),
        name="steps",
    )(info, fields, prev, following, state, adjoint, grad_out, conv, update, reset, cand, head)


def fields_call(info, part_conv, own, prev, following, conv):
    return pl.pallas_call(
        fields_kernel,
        out_shape=shape((STEPS, SIDE, SIDE, C)),
        in_specs=[in_smem()] + [in_vmem()] * 5,
        out_specs=in_vmem(),
        scratch_shapes=[pltpu.VMEM((STEPS, CELLS + 2 * SIDE, 3 * C), BF)],
        compiler_params=params(),
        cost_estimate=pl.CostEstimate(
            flops=2 * STEPS * CELLS * C * C * 9, bytes_accessed=4 << 20, transcendentals=0
        ),
        name="fields",
    )(info, part_conv, own, prev, following, conv)


def seam_info(tile, core, neighbor_tile, seam_turns):
    partner = lax.dynamic_slice_in_dim(neighbor_tile, tile, 1, 0)[0]
    turns = lax.dynamic_slice_in_dim(seam_turns, tile, 1, 0)[0]
    words = []
    for side in (0, 2):
        other = (side + 2 - turns[side]) % 4
        place = jnp.where(
            partner[side] == tile, 0, jnp.where(partner[side] == (tile + 15) % 16, 1, 2)
        )
        flip = other == side
        base = (2 * place + other // 2) * SIDE
        words.append(jnp.where(flip, base + SIDE - 1, base))
        words.append(jnp.where(flip, -1, 1))
    return jnp.stack(words + [core, core, core, core]).astype(jnp.int32)


RING = [(i, (i + 1) % 16) for i in range(16)]
BACK = [((i + 1) % 16, i) for i in range(16)]


def reduce_weights(keep, send):
    y = lax.axis_index("y")
    got = lax.ppermute(send, "core", [(0, 1), (1, 0)])
    held = (keep + got.astype(F32)).reshape(16, 4, 2, 16, C)
    up = [(i, (i + 1) % 4) for i in range(4)]
    down = [((i + 1) % 4, i) for i in range(4)]

    def at(offset):
        return lax.dynamic_index_in_dim(held, (y + offset) % 4, 1, keepdims=False)

    far = at(2).astype(BF)
    from_low = lax.ppermute(far[:, 0], "y", up).astype(F32)
    from_high = lax.ppermute(far[:, 1], "y", down).astype(F32)
    above, below = at(1), at(3)
    above = jnp.stack([above[:, 0] + from_low, above[:, 1]], axis=1).astype(BF)
    below = jnp.stack([below[:, 0], below[:, 1] + from_high], axis=1).astype(BF)
    from_low = lax.ppermute(above, "y", up).astype(F32)
    from_high = lax.ppermute(below, "y", down).astype(F32)
    mine = (at(0) + from_low + from_high).astype(BF).reshape(16, 32, C)
    mine = lax.all_to_all(mine, ("x_lo", "z"), 0, 0, tiled=True)
    mine = jnp.sum(mine.astype(F32), axis=0)
    spread = jnp.broadcast_to(mine[None], (16, 32, C))
    whole = lax.all_to_all(spread, ("x_hi", "y", "core"), 0, 0, tiled=True)
    whole = whole.reshape(2, 4, 2, 32, C)
    whole = whole[0] + whole[1]
    return jnp.transpose(whole, (1, 0, 2, 3)).reshape(16, 16, C)


def body(
    fields_in,
    state_start,
    state_adjoint,
    output_grad,
    conv_weight,
    w_update,
    w_reset,
    w_candidate,
    head_weight,
    neighbor_tile,
    seam_turns,
):
    tile = lax.axis_index(("x_lo", "z"))
    core = lax.axis_index("core")
    info = seam_info(tile, core, neighbor_tile, seam_turns)
    fields = fields_in[0, 0]
    conv = conv_weight.reshape(9 * C, C)
    to_next, to_prev = edges_call(fields)
    prev = lax.ppermute(to_next, ("x_lo", "z"), RING)
    following = lax.ppermute(to_prev, ("x_lo", "z"), BACK)
    grad_state, part_conv, out_next, out_prev, keep, send = main_call(
        info,
        fields,
        prev,
        following,
        state_start.reshape(CELLS, C),
        state_adjoint.reshape(CELLS, C),
        output_grad[0, 0],
        conv,
        w_update,
        w_reset,
        w_candidate,
        head_weight,
    )
    prev = lax.ppermute(out_next, ("x_lo", "z"), RING)
    following = lax.ppermute(out_prev, ("x_lo", "z"), BACK)
    grad_fields = fields_call(info, part_conv, out_next, prev, following, conv)
    total = reduce_weights(keep, send)

    def gate(first):
        return jnp.concatenate([total[first], total[first + 1]], axis=1).T

    return (
        grad_fields[None, None],
        grad_state.reshape(1, 1, SIDE, SIDE, C),
        total[:9],
        gate(9),
        gate(11),
        gate(13),
        total[15, :, :8].T,
    )


def solution(mesh):
    cube = Mesh(mesh.devices.reshape(2, 4, 2, 2, 8), ("x_hi", "y", "core", "x_lo", "z"))
    dp = ("x_hi", "y", "core")
    tile = ("x_lo", "z")
    return jax.shard_map(
        body,
        mesh=cube,
        in_specs=(
            P(dp, tile, None, None, None, None),
            P(dp, tile, None, None, None),
            P(dp, tile, None, None, None),
            P(dp, tile, None, None, None),
            P(),
            P(),
            P(),
            P(),
            P(),
            P(),
            P(),
        ),
        out_specs=(
            P(dp, tile, None, None, None, None),
            P(dp, tile, None, None, None),
            P(None, tile, None),
            P(None, tile),
            P(None, tile),
            P(None, tile),
            P(None, tile),
        ),
        check_vma=False,
    )
```

```python
import math

import jax
import jax.numpy as jnp
from jax import lax
from jax.experimental import pallas as pl
from jax.experimental.pallas import tpu as pltpu
from jax.sharding import Mesh
from jax.sharding import PartitionSpec as P

CUBIC = 0.044715
ROOT = math.sqrt(2.0 / math.pi)
BF = jnp.bfloat16
F32 = jnp.float32
SIDE = 32
CELLS = SIDE * SIDE
C = 256
STEPS = 2
CHUNK = 512
VMEM_LIMIT = 60 * 1024 * 1024


def mm(a, b):
    return lax.dot_general(a, b, (((1,), (0,)), ((), ())), preferred_element_type=F32)


def mm_nt(a, b):
    return lax.dot_general(a, b, (((1,), (1,)), ((), ())), preferred_element_type=F32)


def mm_tn(a, b):
    return lax.dot_general(a, b, (((0,), (0,)), ((), ())), preferred_element_type=F32)


def one_hot(cond):
    return jnp.where(cond, 1.0, 0.0).astype(BF)


def iota(shape, dim):
    return lax.broadcasted_iota(jnp.int32, shape, dim)


def edges_kernel(fields_ref, to_next_ref, to_prev_ref):
    for step in range(STEPS):
        to_next_ref[step, 0] = fields_ref[step, :, SIDE - 1, :]
        to_prev_ref[step, 0] = fields_ref[step, :, 0, :]
        for ref in (to_next_ref, to_prev_ref):
            ref[step, 1] = fields_ref[step, 0]
            ref[step, 2] = fields_ref[step, SIDE - 1]


def seam_of(info_ref, belt_ref, turns_ref, side):
    tile = info_ref[0]
    partner = belt_ref[side, tile]
    other = lax.rem(side + 2 - turns_ref[side, tile], 4)
    before = lax.rem(tile + 15, 16)
    place = jnp.where(partner == tile, 0, jnp.where(partner == before, 1, 2))
    base = (2 * place + jnp.where(other == 2, 1, 0)) * SIDE
    flip = other == side
    return jnp.where(flip, base + SIDE - 1, base), jnp.where(flip, -1, 1)


def seam_rows(info_ref, belt_ref, turns_ref, own_top, own_bottom, from_prev, from_next):
    stacked = jnp.concatenate(
        [own_top, own_bottom, from_prev[1], from_prev[2], from_next[1], from_next[2]], axis=0
    )
    rows = iota((2 * SIDE, 6 * SIDE), 0)
    cols = iota((2 * SIDE, 6 * SIDE), 1)
    top_base, top_sign = seam_of(info_ref, belt_ref, turns_ref, 0)
    bottom_base, bottom_sign = seam_of(info_ref, belt_ref, turns_ref, 2)
    wanted = jnp.where(
        rows < SIDE, top_base + top_sign * rows, bottom_base + bottom_sign * (rows - SIDE)
    )
    return mm(one_hot(cols == wanted), stacked)


def store_shifts(ref, step, low, high, middle, left, right):
    col = iota((SIDE, SIDE, C), 1)
    before = jnp.where(col == 0, left[:, None, :], pltpu.roll(middle, 1, axis=1))
    after = jnp.where(col == SIDE - 1, right[:, None, :], pltpu.roll(middle, SIDE - 1, axis=1))
    body = pl.ds(SIDE, CELLS)
    ref[step, body, 0:C] = before.reshape(CELLS, C).astype(BF)
    ref[step, body, C : 2 * C] = middle.reshape(CELLS, C).astype(BF)
    ref[step, body, 2 * C : 3 * C] = after.reshape(CELLS, C).astype(BF)
    col = iota((SIDE, C), 0)
    for at, line in ((0, low), (SIDE + CELLS, high)):
        row = pl.ds(at, SIDE)
        ref[step, row, 0:C] = jnp.where(col == 0, 0.0, pltpu.roll(line, 1, axis=0)).astype(BF)
        ref[step, row, C : 2 * C] = line.astype(BF)
        ref[step, row, 2 * C : 3 * C] = jnp.where(
            col == SIDE - 1, 0.0, pltpu.roll(line, SIDE - 1, axis=0)
        ).astype(BF)


def main_kernel(
    info_ref,
    belt_ref,
    turns_ref,
    *refs,
):
    sources, refs = refs[:11], refs[11:]
    grad_state_out, part_conv_out, to_next_ref, to_prev_ref, keep_out, send_out = refs[:6]
    held, refs = refs[6:17], refs[17:]
    (
        windows,
        joined,
        gated_all,
        parts_t,
        part_conv,
        part_conv_t,
        last_state,
        grad_state,
        shares,
        in_sems,
        out_sems,
    ) = refs
    loads = [
        pltpu.make_async_copy(source, target, in_sems.at[k])
        for k, (source, target) in enumerate(zip(sources, held))
    ]
    for load in loads:
        load.start()
    (
        fields_ref,
        prev_ref,
        next_ref,
        conv_ref,
        state_ref,
        update_ref,
        reset_ref,
        candidate_ref,
        adjoint_ref,
        grad_out_ref,
        head_ref,
    ) = held
    for load in loads[:3]:
        load.wait()
    for step in range(STEPS):
        seams = seam_rows(
            info_ref,
            belt_ref,
            turns_ref,
            fields_ref[step, 0],
            fields_ref[step, SIDE - 1],
            prev_ref[step],
            next_ref[step],
        )
        store_shifts(
            windows,
            step,
            seams[:SIDE],
            seams[SIDE:],
            fields_ref[step].astype(F32),
            prev_ref[step, 0].astype(F32),
            next_ref[step, 0].astype(F32),
        )
    for load in loads[3:]:
        load.wait()

    def chunk(start):
        rows = pl.ds(start, CHUNK)
        hidden = state_ref[rows, :]
        saved = []
        for step in range(STEPS):
            raw = jnp.zeros((CHUNK, C), F32)
            for p in range(3):
                window = windows[step, pl.ds(start + p * SIDE, CHUNK), :]
                raw = raw + mm(window, conv_ref[pl.ds(3 * C * p, 3 * C), :])
            bend = jnp.tanh(raw * (ROOT + (ROOT * CUBIC) * (raw * raw)))
            feature = (0.5 * raw * (1.0 + bend)).astype(BF)
            joined[step, rows, 0:C] = feature
            joined[step, rows, C : 2 * C] = hidden.astype(BF)
            both = joined[step, rows, :]
            update = 0.5 * jnp.tanh(0.5 * mm(both, update_ref[...])) + 0.5
            reset = 0.5 * jnp.tanh(0.5 * mm(both, reset_ref[...])) + 0.5
            gated = (reset * hidden).astype(BF)
            gated_all[step, rows, :] = gated
            candidate = jnp.tanh(
                mm(feature, candidate_ref[0:C, :]) + mm(gated, candidate_ref[C : 2 * C, :])
            )
            following = hidden + update * (candidate - hidden)
            saved.append((raw, bend, update, reset, candidate, hidden))
            hidden = following
        last_state[rows, :] = hidden.astype(BF)
        carried = adjoint_ref[rows, :]
        for step in reversed(range(STEPS)):
            raw, bend, update, reset, candidate, hidden = saved[step]
            total = carried + mm_tn(grad_out_ref[step, :, rows], head_ref[...])
            keep = 1.0 - update
            scaled = total * update
            part_cand = (scaled * (1.0 - candidate * candidate)).astype(BF)
            part_update = (scaled * (candidate - hidden) * keep).astype(BF)
            grad_gated = mm_nt(part_cand, candidate_ref[C : 2 * C, :])
            part_reset = (grad_gated * hidden * reset * (1.0 - reset)).astype(BF)
            parts_t[step, 0:C, rows] = part_cand.T
            parts_t[step, C : 2 * C, rows] = part_update.T
            parts_t[step, 2 * C : 3 * C, rows] = part_reset.T
            carried = (
                total * keep
                + grad_gated * reset
                + mm_nt(part_update, update_ref[C : 2 * C, :])
                + mm_nt(part_reset, reset_ref[C : 2 * C, :])
            )
            grad_feature = (
                mm_nt(part_cand, candidate_ref[0:C, :])
                + mm_nt(part_update, update_ref[0:C, :])
                + mm_nt(part_reset, reset_ref[0:C, :])
            )
            slope = 0.5 * (1.0 + bend) + (0.5 * ROOT) * raw * (1.0 - bend * bend) * (
                1.0 + (3.0 * CUBIC) * (raw * raw)
            )
            grad_raw = (grad_feature * slope).astype(BF)
            part_conv[step, rows, :] = grad_raw
            part_conv_t[step, :, rows] = grad_raw.T
        grad_state[rows, :] = carried

    for index in range(CELLS // CHUNK):
        chunk(index * CHUNK)
    stores = [
        pltpu.make_async_copy(grad_state, grad_state_out, out_sems.at[16]),
        pltpu.make_async_copy(part_conv, part_conv_out, out_sems.at[17]),
    ]
    for store in stores:
        store.start()

    picks = []
    row = iota((SIDE, CELLS), 0)
    cell = iota((SIDE, CELLS), 1)
    for col in (0, SIDE - 1):
        for p in range(3):
            at = row + 1 - p
            picks.append(one_hot((cell == at * SIDE + col) & (at >= 0) & (at < SIDE)))
    for line in (0, SIDE - 1):
        for q in range(3):
            at = row + 1 - q
            picks.append(one_hot((cell == line * SIDE + at) & (at >= 0) & (at < SIDE)))
    picks = jnp.concatenate(picks, axis=0)
    taps = [0, 3, 6, 2, 5, 8, 0, 1, 2, 6, 7, 8]
    for step in range(STEPS):
        picked = mm(picks, part_conv[step]).astype(BF)
        outside = []
        for side in range(4):
            total = jnp.zeros((SIDE, C), F32)
            for k in range(3 * side, 3 * side + 3):
                total = total + mm_nt(
                    picked[k * SIDE : (k + 1) * SIDE], conv_ref[taps[k] * C : (taps[k] + 1) * C, :]
                )
            outside.append(total.astype(BF))
        to_next_ref[step, 0] = outside[1]
        to_prev_ref[step, 0] = outside[0]
        for ref in (to_next_ref, to_prev_ref):
            ref[step, 1] = outside[2]
            ref[step, 2] = outside[3]

    core = info_ref[1]

    def share(block, value):
        shares[block] = value.reshape(16, 16, C)
        kept = pltpu.make_async_copy(shares.at[block], keep_out.at[block % 8], out_sems.at[block])
        sent = pltpu.make_async_copy(shares.at[block], send_out.at[block % 8], out_sems.at[block])
        pl.when(core == block // 8)(kept.start)
        pl.when(core != block // 8)(sent.start)
        stores.append(kept)

    def over_steps(one):
        return one(0) + one(1)

    for gate in range(2):
        lanes = slice(C * (gate + 1), C * (gate + 2))
        grad = over_steps(lambda s: mm(parts_t[s, lanes, :], joined[s])).astype(BF)
        share(9 + 2 * gate, grad[:, :C])
        share(10 + 2 * gate, grad[:, C:])
    share(13, over_steps(lambda s: mm(parts_t[s, 0:C, :], joined[s, :, 0:C])).astype(BF))
    share(14, over_steps(lambda s: mm(parts_t[s, 0:C, :], gated_all[s])).astype(BF))
    grad_head = mm(grad_out_ref[0], joined[1, :, C : 2 * C]) + mm(grad_out_ref[1], last_state[...])
    grad_head = jnp.concatenate([grad_head, jnp.zeros((C - 8, C), F32)], axis=0)
    share(15, grad_head.T.astype(BF))
    for p in range(3):
        grad = over_steps(
            lambda s: mm(part_conv_t[s], windows[s, pl.ds(p * SIDE, CELLS), :])
        ).astype(BF)
        for q in range(3):
            share(3 * p + q, grad[:, q * C : (q + 1) * C].T)
    for store in stores:
        store.wait()


def fields_kernel(
    info_ref,
    belt_ref,
    turns_ref,
    part_conv_ref,
    own_ref,
    prev_ref,
    next_ref,
    conv_ref,
    grad_fields_ref,
    shifted,
):
    zero = jnp.zeros((SIDE, C), F32)
    for step in range(STEPS):
        store_shifts(
            shifted,
            step,
            zero,
            zero,
            part_conv_ref[step].astype(F32).reshape(SIDE, SIDE, C),
            zero,
            zero,
        )
        seams = seam_rows(
            info_ref,
            belt_ref,
            turns_ref,
            own_ref[step, 1],
            own_ref[step, 2],
            prev_ref[step],
            next_ref[step],
        )
        left = prev_ref[step, 0].astype(F32)
        right = next_ref[step, 0].astype(F32)
        for part in range(4):
            at = part * 8
            grad = jnp.zeros((8 * SIDE, C), F32)
            for p in range(3):
                for q in range(3):
                    lanes = slice((2 - q) * C, (3 - q) * C)
                    window = shifted[step, pl.ds((at + 2 - p) * SIDE, 8 * SIDE), lanes]
                    tap = 3 * p + q
                    grad = grad + mm_nt(window, conv_ref[tap * C : (tap + 1) * C, :])
            grad = grad.reshape(8, SIDE, C)
            col = iota((8, SIDE, C), 1)
            row = iota((8, SIDE, C), 0)
            grad = grad + jnp.where(col == 0, left[at : at + 8][:, None, :], 0.0)
            grad = grad + jnp.where(col == SIDE - 1, right[at : at + 8][:, None, :], 0.0)
            if part == 0:
                grad = grad + jnp.where(row == 0, seams[:SIDE][None], 0.0)
            if part == 3:
                grad = grad + jnp.where(row == 7, seams[SIDE:][None], 0.0)
            grad_fields_ref[step, at : at + 8] = grad.astype(BF)


def in_vmem():
    return pl.BlockSpec(memory_space=pltpu.VMEM)


def in_smem():
    return pl.BlockSpec(memory_space=pltpu.SMEM)


def params():
    return pltpu.CompilerParams(vmem_limit_bytes=VMEM_LIMIT)


def shape(dims, kind=BF):
    return jax.ShapeDtypeStruct(dims, kind)


EDGE = (STEPS, 3, SIDE, C)


def edges_call(fields):
    return pl.pallas_call(
        edges_kernel,
        out_shape=(shape(EDGE), shape(EDGE)),
        in_specs=[in_vmem()],
        out_specs=(in_vmem(), in_vmem()),
        compiler_params=params(),
        name="edges",
    )(fields)


def main_call(*args):
    anywhere = pl.BlockSpec(memory_space=pl.ANY)
    return pl.pallas_call(
        main_kernel,
        out_shape=(
            shape((CELLS, C), F32),
            shape((STEPS, CELLS, C)),
            shape(EDGE),
            shape(EDGE),
            shape((8, 16, 16, C)),
            shape((8, 16, 16, C)),
        ),
        in_specs=[in_smem()] * 3 + [anywhere] * 11,
        out_specs=(anywhere, anywhere, in_vmem(), in_vmem(), anywhere, anywhere),
        scratch_shapes=[pltpu.VMEM(arg.shape, arg.dtype) for arg in args[3:]]
        + [
            pltpu.VMEM((STEPS, CELLS + 2 * SIDE, 3 * C), BF),
            pltpu.VMEM((STEPS, CELLS, 2 * C), BF),
            pltpu.VMEM((STEPS, CELLS, C), BF),
            pltpu.VMEM((STEPS, 3 * C, CELLS), BF),
            pltpu.VMEM((STEPS, CELLS, C), BF),
            pltpu.VMEM((STEPS, C, CELLS), BF),
            pltpu.VMEM((CELLS, C), BF),
            pltpu.VMEM((CELLS, C), F32),
            pltpu.VMEM((16, 16, 16, C), BF),
            pltpu.SemaphoreType.DMA((11,)),
            pltpu.SemaphoreType.DMA((18,)),
        ],
        compiler_params=params(),
        name="steps",
    )(*args)


def fields_call(*args):
    return pl.pallas_call(
        fields_kernel,
        out_shape=shape((STEPS, SIDE, SIDE, C)),
        in_specs=[in_smem()] * 3 + [in_vmem()] * 5,
        out_specs=in_vmem(),
        scratch_shapes=[pltpu.VMEM((STEPS, CELLS + 2 * SIDE, 3 * C), BF)],
        compiler_params=params(),
        cost_estimate=pl.CostEstimate(
            flops=2 * STEPS * CELLS * C * C * 9, bytes_accessed=4 << 20, transcendentals=0
        ),
        name="fields",
    )(*args)


RING = [(i, (i + 1) % 16) for i in range(16)]
BACK = [((i + 1) % 16, i) for i in range(16)]


def finish_kernel(whole_ref, conv_ref, update_ref, reset_ref, candidate_ref, head_ref):
    def block(k):
        return whole_ref[((k // 4) % 2) * 8 + (k % 4) * 2 + k // 8].astype(F32)

    for tap in range(9):
        conv_ref[tap] = block(tap)
    for ref, first in ((update_ref, 9), (reset_ref, 11), (candidate_ref, 13)):
        ref[:, 0:C] = block(first)
        ref[:, C : 2 * C] = block(first + 1)
    head_ref[...] = block(15).T[:8]


def finish_call(whole):
    gate = shape((16, 2 * C), F32)
    return pl.pallas_call(
        finish_kernel,
        out_shape=(shape((9, 16, C), F32), gate, gate, gate, shape((8, 16), F32)),
        in_specs=[in_vmem()],
        out_specs=tuple([in_vmem()] * 5),
        compiler_params=params(),
        name="finish",
    )(whole)


def added(pieces):
    total = pieces[0].astype(F32)
    for k in range(1, pieces.shape[0]):
        total = total + pieces[k].astype(F32)
    return total


def body(
    fields_in,
    state_start,
    state_adjoint,
    output_grad,
    conv_weight,
    w_update,
    w_reset,
    w_candidate,
    head_weight,
    neighbor_tile,
    seam_turns,
):
    dp = ("x_hi", "y", "core")
    belt = ("x_lo", "z")
    info = jnp.stack([lax.axis_index(belt), lax.axis_index("core")]).astype(jnp.int32)
    seams = (info, neighbor_tile.T, seam_turns.T)
    fields = fields_in[0, 0]
    conv = conv_weight.reshape(9 * C, C)
    to_next, to_prev = edges_call(fields)
    prev = lax.ppermute(to_next, belt, RING)
    following = lax.ppermute(to_prev, belt, BACK)
    grad_state, part_conv, out_next, out_prev, keep, send = main_call(
        *seams,
        fields,
        prev,
        following,
        conv,
        state_start.reshape(CELLS, C),
        w_update,
        w_reset,
        w_candidate,
        state_adjoint.reshape(CELLS, C),
        output_grad[0, 0],
        head_weight,
    )
    got = lax.ppermute(send, "core", [(0, 1), (1, 0)])
    held = (keep.astype(F32) + got.astype(F32)).astype(BF)
    held = lax.all_to_all(held, ("x_hi", "y"), 0, 0, tiled=True)
    held = added(held).astype(BF)
    prev = lax.ppermute(out_next, belt, RING)
    following = lax.ppermute(out_prev, belt, BACK)
    held, prev, following = lax.optimization_barrier((held, prev, following))
    grad_fields = fields_call(*seams, part_conv, out_next, prev, following, conv)
    held = lax.all_to_all(held, belt, 0, 0, tiled=True)
    held = added(held).astype(BF)
    held, grad_fields = lax.optimization_barrier((held, grad_fields))
    whole = jnp.broadcast_to(held[None], (16, 16, C))
    whole = lax.all_to_all(whole, dp, 0, 0, tiled=True)
    grad_conv, grad_update, grad_reset, grad_candidate, grad_head = finish_call(whole)
    return (
        grad_fields[None, None],
        grad_state.reshape(1, 1, SIDE, SIDE, C),
        grad_conv,
        grad_update.T,
        grad_reset.T,
        grad_candidate.T,
        grad_head,
    )


def solution(mesh):
    cube = Mesh(mesh.devices.reshape(2, 4, 2, 2, 8), ("x_hi", "y", "core", "x_lo", "z"))
    dp = ("x_hi", "y", "core")
    tile = ("x_lo", "z")
    return jax.shard_map(
        body,
        mesh=cube,
        in_specs=(
            P(dp, tile, None, None, None, None),
            P(dp, tile, None, None, None),
            P(dp, tile, None, None, None),
            P(dp, tile, None, None, None),
            P(),
            P(),
            P(),
            P(),
            P(),
            P(),
            P(),
        ),
        out_specs=(
            P(dp, tile, None, None, None, None),
            P(dp, tile, None, None, None),
            P(None, tile, None),
            P(None, tile),
            P(None, tile),
            P(None, tile),
            P(None, tile),
        ),
        check_vma=False,
    )
```

```python
import math

import jax
import jax.numpy as jnp
from jax import lax
from jax.experimental import pallas as pl
from jax.experimental.pallas import tpu as pltpu
from jax.sharding import Mesh
from jax.sharding import PartitionSpec as P

CUBIC = 0.044715
ROOT = math.sqrt(2.0 / math.pi)
BF = jnp.bfloat16
F32 = jnp.float32
SIDE = 32
CELLS = SIDE * SIDE
C = 256
STEPS = 2
CHUNK = 512


def mm(a, b):
    return lax.dot_general(a, b, (((1,), (0,)), ((), ())), preferred_element_type=F32)


def mm_nt(a, b):
    return lax.dot_general(a, b, (((1,), (1,)), ((), ())), preferred_element_type=F32)


def mm_tn(a, b):
    return lax.dot_general(a, b, (((0,), (0,)), ((), ())), preferred_element_type=F32)


def one_hot(cond):
    return jnp.where(cond, 1.0, 0.0).astype(BF)


def iota(shape, dim):
    return lax.broadcasted_iota(jnp.int32, shape, dim)


def edges_kernel(fields_ref, to_next_ref, to_prev_ref):
    for step in range(STEPS):
        to_next_ref[step, 0] = fields_ref[step, :, SIDE - 1, :]
        to_prev_ref[step, 0] = fields_ref[step, :, 0, :]
        for ref in (to_next_ref, to_prev_ref):
            ref[step, 1] = fields_ref[step, 0]
            ref[step, 2] = fields_ref[step, SIDE - 1]


def seam_of(info_ref, belt_ref, turns_ref, side):
    tile = info_ref[0]
    partner = belt_ref[side, tile]
    other = lax.rem(side + 2 - turns_ref[side, tile], 4)
    before = lax.rem(tile + 15, 16)
    place = jnp.where(partner == tile, 0, jnp.where(partner == before, 1, 2))
    base = (2 * place + jnp.where(other == 2, 1, 0)) * SIDE
    flip = other == side
    return jnp.where(flip, base + SIDE - 1, base), jnp.where(flip, -1, 1)


def seam_rows(info_ref, belt_ref, turns_ref, own_top, own_bottom, from_prev, from_next):
    stacked = jnp.concatenate(
        [own_top, own_bottom, from_prev[1], from_prev[2], from_next[1], from_next[2]], axis=0
    )
    rows = iota((2 * SIDE, 6 * SIDE), 0)
    cols = iota((2 * SIDE, 6 * SIDE), 1)
    top_base, top_sign = seam_of(info_ref, belt_ref, turns_ref, 0)
    bottom_base, bottom_sign = seam_of(info_ref, belt_ref, turns_ref, 2)
    wanted = jnp.where(
        rows < SIDE, top_base + top_sign * rows, bottom_base + bottom_sign * (rows - SIDE)
    )
    return mm(one_hot(cols == wanted), stacked)


def line_shifts(line):
    at = iota((SIDE, C), 0)
    before = jnp.where(at == 0, 0.0, pltpu.roll(line, 1, axis=0))
    after = jnp.where(at == SIDE - 1, 0.0, pltpu.roll(line, SIDE - 1, axis=0))
    return jnp.concatenate([before, line, after], axis=1).astype(BF)


def store_shifts(ref, step, low, high, middle, left, right):
    col = iota((SIDE, SIDE, C), 1)
    before = jnp.where(col == 0, left[:, None, :], pltpu.roll(middle, 1, axis=1))
    after = jnp.where(col == SIDE - 1, right[:, None, :], pltpu.roll(middle, SIDE - 1, axis=1))
    body = pl.ds(SIDE, CELLS)
    ref[step, body, 0:C] = before.reshape(CELLS, C).astype(BF)
    ref[step, body, C : 2 * C] = middle.reshape(CELLS, C).astype(BF)
    ref[step, body, 2 * C : 3 * C] = after.reshape(CELLS, C).astype(BF)
    ref[step, pl.ds(0, SIDE), :] = line_shifts(low)
    ref[step, pl.ds(SIDE + CELLS, SIDE), :] = line_shifts(high)


def early_kernel(fields_in, conv_in, raw_out, fields_ref, conv_ref, windows, raw_ref, sems):
    loads = [
        pltpu.make_async_copy(fields_in, fields_ref, sems.at[0]),
        pltpu.make_async_copy(conv_in, conv_ref, sems.at[1]),
    ]
    for load in loads:
        load.start()
    loads[0].wait()
    zero = jnp.zeros((SIDE, C), F32)
    stores = []
    for step in range(STEPS):
        store_shifts(windows, step, zero, zero, fields_ref[step].astype(F32), zero, zero)
        if step == 0:
            loads[1].wait()
        for start in range(0, CELLS, CHUNK):
            raw = jnp.zeros((CHUNK, C), F32)
            for p in range(3):
                window = windows[step, pl.ds(start + p * SIDE, CHUNK), :]
                raw = raw + mm(window, conv_ref[pl.ds(3 * C * p, 3 * C), :])
            raw_ref[step, pl.ds(start, CHUNK), :] = raw
        stores.append(pltpu.make_async_copy(raw_ref.at[step], raw_out.at[step], sems.at[2 + step]))
        stores[step].start()
    for store in stores:
        store.wait()


def main_kernel(
    info_ref,
    belt_ref,
    turns_ref,
    *refs,
):
    sources, refs = refs[:12], refs[12:]
    grad_state_out, part_conv_out, to_next_ref, to_prev_ref, keep_out, send_out = refs[:6]
    held, refs = refs[6:18], refs[18:]
    (
        windows,
        joined,
        gated_all,
        parts_t,
        part_conv,
        part_conv_t,
        last_state,
        grad_state,
        shares,
        in_sems,
        out_sems,
    ) = refs
    loads = [
        pltpu.make_async_copy(source, target, in_sems.at[k])
        for k, (source, target) in enumerate(zip(sources, held))
    ]
    for load in loads:
        load.start()
    (
        fields_ref,
        prev_ref,
        next_ref,
        conv_ref,
        raw_ref,
        state_ref,
        update_ref,
        reset_ref,
        candidate_ref,
        adjoint_ref,
        grad_out_ref,
        head_ref,
    ) = held
    for load in loads[:3]:
        load.wait()
    tops, bottoms, lefts, rights = [], [], [], []
    for step in range(STEPS):
        seams = seam_rows(
            info_ref,
            belt_ref,
            turns_ref,
            fields_ref[step, 0],
            fields_ref[step, SIDE - 1],
            prev_ref[step],
            next_ref[step],
        )
        left = prev_ref[step, 0].astype(F32)
        right = next_ref[step, 0].astype(F32)
        store_shifts(
            windows,
            step,
            seams[:SIDE],
            seams[SIDE:],
            fields_ref[step].astype(F32),
            left,
            right,
        )
        tops.append(line_shifts(seams[:SIDE]))
        bottoms.append(line_shifts(seams[SIDE:]))
        lefts.append(line_shifts(left))
        rights.append(line_shifts(right))
    for load in loads[3:5]:
        load.wait()

    def taps_of(lines, taps):
        lines = jnp.concatenate(lines, axis=0)
        total = jnp.zeros((STEPS * SIDE, C), F32)
        for k, tap in enumerate(taps):
            total = total + mm(lines[:, k * C : (k + 1) * C], conv_ref[pl.ds(tap * C, C), :])
        return total

    top = taps_of(tops, (0, 1, 2))
    bottom = taps_of(bottoms, (6, 7, 8))
    left = taps_of(lefts, (0, 3, 6))
    right = taps_of(rights, (2, 5, 8))
    place = iota((SIDE, 8, C), 1)
    for step in range(STEPS):
        lines = slice(step * SIDE, (step + 1) * SIDE)
        raw_ref[step, 0, :, :] += top[lines]
        raw_ref[step, SIDE - 1, :, :] += bottom[lines]
        raw_ref[step, :, 0:8, :] += jnp.where(place == 0, left[lines][:, None, :], 0.0)
        raw_ref[step, :, SIDE - 8 : SIDE, :] += jnp.where(place == 7, right[lines][:, None, :], 0.0)
    for load in loads[5:]:
        load.wait()

    def chunk(start):
        rows = pl.ds(start, CHUNK)
        hidden = state_ref[rows, :]
        saved = []
        for step in range(STEPS):
            raw = raw_ref[step, pl.ds(start // SIDE, CHUNK // SIDE), :, :].reshape(CHUNK, C)
            bend = jnp.tanh(raw * (ROOT + (ROOT * CUBIC) * (raw * raw)))
            feature = (0.5 * raw * (1.0 + bend)).astype(BF)
            joined[step, rows, 0:C] = feature
            joined[step, rows, C : 2 * C] = hidden.astype(BF)
            both = joined[step, rows, :]
            update = 0.5 * jnp.tanh(0.5 * mm(both, update_ref[...])) + 0.5
            reset = 0.5 * jnp.tanh(0.5 * mm(both, reset_ref[...])) + 0.5
            gated = (reset * hidden).astype(BF)
            gated_all[step, rows, :] = gated
            candidate = jnp.tanh(
                mm(feature, candidate_ref[0:C, :]) + mm(gated, candidate_ref[C : 2 * C, :])
            )
            following = hidden + update * (candidate - hidden)
            saved.append((raw, bend, update, reset, candidate, hidden))
            hidden = following
        last_state[rows, :] = hidden.astype(BF)
        carried = adjoint_ref[rows, :]
        for step in reversed(range(STEPS)):
            raw, bend, update, reset, candidate, hidden = saved[step]
            total = carried + mm_tn(grad_out_ref[step, :, rows], head_ref[...])
            keep = 1.0 - update
            scaled = total * update
            part_cand = (scaled * (1.0 - candidate * candidate)).astype(BF)
            part_update = (scaled * (candidate - hidden) * keep).astype(BF)
            grad_gated = mm_nt(part_cand, candidate_ref[C : 2 * C, :])
            part_reset = (grad_gated * hidden * reset * (1.0 - reset)).astype(BF)
            parts_t[step, 0:C, rows] = part_cand.T
            parts_t[step, C : 2 * C, rows] = part_update.T
            parts_t[step, 2 * C : 3 * C, rows] = part_reset.T
            carried = (
                total * keep
                + grad_gated * reset
                + mm_nt(part_update, update_ref[C : 2 * C, :])
                + mm_nt(part_reset, reset_ref[C : 2 * C, :])
            )
            grad_feature = (
                mm_nt(part_cand, candidate_ref[0:C, :])
                + mm_nt(part_update, update_ref[0:C, :])
                + mm_nt(part_reset, reset_ref[0:C, :])
            )
            slope = 0.5 * (1.0 + bend) + (0.5 * ROOT) * raw * (1.0 - bend * bend) * (
                1.0 + (3.0 * CUBIC) * (raw * raw)
            )
            grad_raw = (grad_feature * slope).astype(BF)
            part_conv[step, rows, :] = grad_raw
            part_conv_t[step, :, rows] = grad_raw.T
        grad_state[rows, :] = carried

    for index in range(CELLS // CHUNK):
        chunk(index * CHUNK)
    stores = [
        pltpu.make_async_copy(grad_state, grad_state_out, out_sems.at[16]),
        pltpu.make_async_copy(part_conv, part_conv_out, out_sems.at[17]),
    ]
    for store in stores:
        store.start()

    picks = []
    row = iota((SIDE, CELLS), 0)
    cell = iota((SIDE, CELLS), 1)
    for col in (0, SIDE - 1):
        for p in range(3):
            at = row + 1 - p
            picks.append(one_hot((cell == at * SIDE + col) & (at >= 0) & (at < SIDE)))
    for line in (0, SIDE - 1):
        for q in range(3):
            at = row + 1 - q
            picks.append(one_hot((cell == line * SIDE + at) & (at >= 0) & (at < SIDE)))
    picks = jnp.concatenate(picks, axis=0)
    taps = [0, 3, 6, 2, 5, 8, 0, 1, 2, 6, 7, 8]
    for step in range(STEPS):
        picked = mm(picks, part_conv[step]).astype(BF)
        outside = []
        for side in range(4):
            total = jnp.zeros((SIDE, C), F32)
            for k in range(3 * side, 3 * side + 3):
                total = total + mm_nt(
                    picked[k * SIDE : (k + 1) * SIDE], conv_ref[taps[k] * C : (taps[k] + 1) * C, :]
                )
            outside.append(total.astype(BF))
        to_next_ref[step, 0] = outside[1]
        to_prev_ref[step, 0] = outside[0]
        for ref in (to_next_ref, to_prev_ref):
            ref[step, 1] = outside[2]
            ref[step, 2] = outside[3]

    core = info_ref[1]

    def share(block, value):
        shares[block] = value.reshape(16, 16, C)
        kept = pltpu.make_async_copy(shares.at[block], keep_out.at[block % 8], out_sems.at[block])
        sent = pltpu.make_async_copy(shares.at[block], send_out.at[block % 8], out_sems.at[block])
        pl.when(core == block // 8)(kept.start)
        pl.when(core != block // 8)(sent.start)
        stores.append(kept)

    def over_steps(one):
        return one(0) + one(1)

    for gate in range(2):
        lanes = slice(C * (gate + 1), C * (gate + 2))
        grad = over_steps(lambda s: mm(parts_t[s, lanes, :], joined[s])).astype(BF)
        share(9 + 2 * gate, grad[:, :C])
        share(10 + 2 * gate, grad[:, C:])
    share(13, over_steps(lambda s: mm(parts_t[s, 0:C, :], joined[s, :, 0:C])).astype(BF))
    share(14, over_steps(lambda s: mm(parts_t[s, 0:C, :], gated_all[s])).astype(BF))
    grad_head = mm(grad_out_ref[0], joined[1, :, C : 2 * C]) + mm(grad_out_ref[1], last_state[...])
    grad_head = jnp.concatenate([grad_head, jnp.zeros((C - 8, C), F32)], axis=0)
    share(15, grad_head.T.astype(BF))
    for p in range(3):
        grad = over_steps(
            lambda s: mm(part_conv_t[s], windows[s, pl.ds(p * SIDE, CELLS), :])
        ).astype(BF)
        for q in range(3):
            share(3 * p + q, grad[:, q * C : (q + 1) * C].T)
    for store in stores:
        store.wait()


def fields_kernel(
    info_ref,
    belt_ref,
    turns_ref,
    part_conv_ref,
    own_ref,
    prev_ref,
    next_ref,
    conv_ref,
    grad_fields_ref,
    shifted,
):
    zero = jnp.zeros((SIDE, C), F32)
    for step in range(STEPS):
        store_shifts(
            shifted,
            step,
            zero,
            zero,
            part_conv_ref[step].astype(F32).reshape(SIDE, SIDE, C),
            zero,
            zero,
        )
        seams = seam_rows(
            info_ref,
            belt_ref,
            turns_ref,
            own_ref[step, 1],
            own_ref[step, 2],
            prev_ref[step],
            next_ref[step],
        )
        left = prev_ref[step, 0].astype(F32)
        right = next_ref[step, 0].astype(F32)
        for part in range(4):
            at = part * 8
            grad = jnp.zeros((8 * SIDE, C), F32)
            for p in range(3):
                for q in range(3):
                    lanes = slice((2 - q) * C, (3 - q) * C)
                    window = shifted[step, pl.ds((at + 2 - p) * SIDE, 8 * SIDE), lanes]
                    tap = 3 * p + q
                    grad = grad + mm_nt(window, conv_ref[tap * C : (tap + 1) * C, :])
            grad = grad.reshape(8, SIDE, C)
            col = iota((8, SIDE, C), 1)
            row = iota((8, SIDE, C), 0)
            grad = grad + jnp.where(col == 0, left[at : at + 8][:, None, :], 0.0)
            grad = grad + jnp.where(col == SIDE - 1, right[at : at + 8][:, None, :], 0.0)
            if part == 0:
                grad = grad + jnp.where(row == 0, seams[:SIDE][None], 0.0)
            if part == 3:
                grad = grad + jnp.where(row == 7, seams[SIDE:][None], 0.0)
            grad_fields_ref[step, at : at + 8] = grad.astype(BF)


def in_vmem():
    return pl.BlockSpec(memory_space=pltpu.VMEM)


def in_smem():
    return pl.BlockSpec(memory_space=pltpu.SMEM)


def params(mebibytes=60):
    return pltpu.CompilerParams(vmem_limit_bytes=mebibytes << 20)


def shape(dims, kind=BF):
    return jax.ShapeDtypeStruct(dims, kind)


EDGE = (STEPS, 3, SIDE, C)


def edges_call(fields):
    return pl.pallas_call(
        edges_kernel,
        out_shape=(shape(EDGE), shape(EDGE)),
        in_specs=[in_vmem()],
        out_specs=(in_vmem(), in_vmem()),
        compiler_params=params(8),
        name="edges",
    )(fields)


def early_call(fields, conv):
    anywhere = pl.BlockSpec(memory_space=pl.ANY)
    raw = (STEPS, CELLS, C)
    return pl.pallas_call(
        early_kernel,
        out_shape=shape(raw, F32),
        in_specs=[anywhere] * 2,
        out_specs=anywhere,
        scratch_shapes=[
            pltpu.VMEM(fields.shape, BF),
            pltpu.VMEM(conv.shape, BF),
            pltpu.VMEM((STEPS, CELLS + 2 * SIDE, 3 * C), BF),
            pltpu.VMEM(raw, F32),
            pltpu.SemaphoreType.DMA((4,)),
        ],
        compiler_params=params(),
        cost_estimate=pl.CostEstimate(
            flops=2 * STEPS * CELLS * C * C * 9, bytes_accessed=5 << 20, transcendentals=0
        ),
        name="early",
    )(fields, conv)


def main_call(*args):
    anywhere = pl.BlockSpec(memory_space=pl.ANY)
    return pl.pallas_call(
        main_kernel,
        out_shape=(
            shape((CELLS, C), F32),
            shape((STEPS, CELLS, C)),
            shape(EDGE),
            shape(EDGE),
            shape((8, 16, 16, C)),
            shape((8, 16, 16, C)),
        ),
        in_specs=[in_smem()] * 3 + [anywhere] * 12,
        out_specs=(anywhere, anywhere, in_vmem(), in_vmem(), anywhere, anywhere),
        scratch_shapes=[pltpu.VMEM(arg.shape, arg.dtype) for arg in args[3:]]
        + [
            pltpu.VMEM((STEPS, CELLS + 2 * SIDE, 3 * C), BF),
            pltpu.VMEM((STEPS, CELLS, 2 * C), BF),
            pltpu.VMEM((STEPS, CELLS, C), BF),
            pltpu.VMEM((STEPS, 3 * C, CELLS), BF),
            pltpu.VMEM((STEPS, CELLS, C), BF),
            pltpu.VMEM((STEPS, C, CELLS), BF),
            pltpu.VMEM((CELLS, C), BF),
            pltpu.VMEM((CELLS, C), F32),
            pltpu.VMEM((16, 16, 16, C), BF),
            pltpu.SemaphoreType.DMA((12,)),
            pltpu.SemaphoreType.DMA((18,)),
        ],
        compiler_params=params(),
        name="steps",
    )(*args)


def fields_call(*args):
    return pl.pallas_call(
        fields_kernel,
        out_shape=shape((STEPS, SIDE, SIDE, C)),
        in_specs=[in_smem()] * 3 + [in_vmem()] * 5,
        out_specs=in_vmem(),
        scratch_shapes=[pltpu.VMEM((STEPS, CELLS + 2 * SIDE, 3 * C), BF)],
        compiler_params=params(20),
        cost_estimate=pl.CostEstimate(
            flops=2 * STEPS * CELLS * C * C * 9, bytes_accessed=4 << 20, transcendentals=0
        ),
        name="fields",
    )(*args)


RING = [(i, (i + 1) % 16) for i in range(16)]
BACK = [((i + 1) % 16, i) for i in range(16)]


def finish_kernel(whole_ref, conv_ref, update_ref, reset_ref, candidate_ref, head_ref):
    def block(k):
        return whole_ref[((k // 4) % 2) * 8 + (k % 4) * 2 + k // 8].astype(F32)

    for tap in range(9):
        conv_ref[tap] = block(tap)
    for ref, first in ((update_ref, 9), (reset_ref, 11), (candidate_ref, 13)):
        ref[:, 0:C] = block(first)
        ref[:, C : 2 * C] = block(first + 1)
    head_ref[...] = block(15).T[:8]


def finish_call(whole):
    gate = shape((16, 2 * C), F32)
    return pl.pallas_call(
        finish_kernel,
        out_shape=(shape((9, 16, C), F32), gate, gate, gate, shape((8, 16), F32)),
        in_specs=[in_vmem()],
        out_specs=tuple([in_vmem()] * 5),
        compiler_params=params(8),
        name="finish",
    )(whole)


def added(pieces):
    total = pieces[0].astype(F32)
    for k in range(1, pieces.shape[0]):
        total = total + pieces[k].astype(F32)
    return total


def body(
    fields_in,
    state_start,
    state_adjoint,
    output_grad,
    conv_weight,
    w_update,
    w_reset,
    w_candidate,
    head_weight,
    neighbor_tile,
    seam_turns,
):
    dp = ("x_hi", "y", "core")
    belt = ("x_lo", "z")
    info = jnp.stack([lax.axis_index(belt), lax.axis_index("core")]).astype(jnp.int32)
    seams = (info, neighbor_tile.T, seam_turns.T)
    fields = fields_in[0, 0]
    conv = conv_weight.reshape(9 * C, C)
    to_next, to_prev = edges_call(fields)
    prev = lax.ppermute(to_next, belt, RING)
    following = lax.ppermute(to_prev, belt, BACK)
    raw = early_call(fields, conv).reshape(STEPS, SIDE, SIDE, C)
    grad_state, part_conv, out_next, out_prev, keep, send = main_call(
        *seams,
        fields,
        prev,
        following,
        conv,
        raw,
        state_start.reshape(CELLS, C),
        w_update,
        w_reset,
        w_candidate,
        state_adjoint.reshape(CELLS, C),
        output_grad[0, 0],
        head_weight,
    )
    got = lax.ppermute(send, "core", [(0, 1), (1, 0)])
    held = (keep.astype(F32) + got.astype(F32)).astype(BF)
    held = lax.all_to_all(held, ("x_hi", "y"), 0, 0, tiled=True)
    held = added(held).astype(BF)
    prev = lax.ppermute(out_next, belt, RING)
    following = lax.ppermute(out_prev, belt, BACK)
    held, prev, following = lax.optimization_barrier((held, prev, following))
    grad_fields = fields_call(*seams, part_conv, out_next, prev, following, conv)
    held = lax.all_to_all(held, belt, 0, 0, tiled=True)
    held = added(held).astype(BF)
    held, grad_fields = lax.optimization_barrier((held, grad_fields))
    whole = jnp.broadcast_to(held[None], (16, 16, C))
    whole = lax.all_to_all(whole, dp, 0, 0, tiled=True)
    grad_conv, grad_update, grad_reset, grad_candidate, grad_head = finish_call(whole)
    return (
        grad_fields[None, None],
        grad_state.reshape(1, 1, SIDE, SIDE, C),
        grad_conv,
        grad_update.T,
        grad_reset.T,
        grad_candidate.T,
        grad_head,
    )


def solution(mesh):
    cube = Mesh(mesh.devices.reshape(2, 4, 2, 2, 8), ("x_hi", "y", "core", "x_lo", "z"))
    dp = ("x_hi", "y", "core")
    tile = ("x_lo", "z")
    return jax.shard_map(
        body,
        mesh=cube,
        in_specs=(
            P(dp, tile, None, None, None, None),
            P(dp, tile, None, None, None),
            P(dp, tile, None, None, None),
            P(dp, tile, None, None, None),
            P(),
            P(),
            P(),
            P(),
            P(),
            P(),
            P(),
        ),
        out_specs=(
            P(dp, tile, None, None, None, None),
            P(dp, tile, None, None, None),
            P(None, tile, None),
            P(None, tile),
            P(None, tile),
            P(None, tile),
            P(None, tile),
        ),
        check_vma=False,
    )
```

```python
import math

import jax
import jax.numpy as jnp
from jax import lax
from jax.experimental import pallas as pl
from jax.experimental.pallas import tpu as pltpu
from jax.sharding import Mesh
from jax.sharding import PartitionSpec as P

CUBIC = 0.044715
ROOT = math.sqrt(2.0 / math.pi)
BF = jnp.bfloat16
F32 = jnp.float32
SIDE = 32
CELLS = SIDE * SIDE
C = 256
STEPS = 2
CHUNK = 512


def mm(a, b):
    return lax.dot_general(a, b, (((1,), (0,)), ((), ())), preferred_element_type=F32)


def mm_nt(a, b):
    return lax.dot_general(a, b, (((1,), (1,)), ((), ())), preferred_element_type=F32)


def mm_tn(a, b):
    return lax.dot_general(a, b, (((0,), (0,)), ((), ())), preferred_element_type=F32)


def one_hot(cond):
    return jnp.where(cond, 1.0, 0.0).astype(BF)


def iota(shape, dim):
    return lax.broadcasted_iota(jnp.int32, shape, dim)


def edges_kernel(fields_ref, to_next_ref, to_prev_ref):
    for step in range(STEPS):
        to_next_ref[step, 0] = fields_ref[step, :, SIDE - 1, :]
        to_prev_ref[step, 0] = fields_ref[step, :, 0, :]
        for ref in (to_next_ref, to_prev_ref):
            ref[step, 1] = fields_ref[step, 0]
            ref[step, 2] = fields_ref[step, SIDE - 1]


def seam_of(belt_ref, turns_ref, side):
    tile = lax.axis_index(("x_lo", "z"))
    partner = belt_ref[side, tile]
    other = lax.rem(side + 2 - turns_ref[side, tile], 4)
    before = lax.rem(tile + 15, 16)
    place = jnp.where(partner == tile, 0, jnp.where(partner == before, 1, 2))
    base = (2 * place + jnp.where(other == 2, 1, 0)) * SIDE
    flip = other == side
    return jnp.where(flip, base + SIDE - 1, base), jnp.where(flip, -1, 1)


def seam_rows(belt_ref, turns_ref, own_top, own_bottom, from_prev, from_next):
    stacked = jnp.concatenate(
        [own_top, own_bottom, from_prev[1], from_prev[2], from_next[1], from_next[2]], axis=0
    )
    rows = iota((2 * SIDE, 6 * SIDE), 0)
    cols = iota((2 * SIDE, 6 * SIDE), 1)
    top_base, top_sign = seam_of(belt_ref, turns_ref, 0)
    bottom_base, bottom_sign = seam_of(belt_ref, turns_ref, 2)
    wanted = jnp.where(
        rows < SIDE, top_base + top_sign * rows, bottom_base + bottom_sign * (rows - SIDE)
    )
    return mm(one_hot(cols == wanted), stacked)


def line_shifts(line):
    at = iota((SIDE, C), 0)
    before = jnp.where(at == 0, 0.0, pltpu.roll(line, 1, axis=0))
    after = jnp.where(at == SIDE - 1, 0.0, pltpu.roll(line, SIDE - 1, axis=0))
    return jnp.concatenate([before, line, after], axis=1).astype(BF)


def store_shifts(ref, step, low, high, middle, left, right):
    col = iota((SIDE, SIDE, C), 1)
    before = jnp.where(col == 0, left[:, None, :], pltpu.roll(middle, 1, axis=1))
    after = jnp.where(col == SIDE - 1, right[:, None, :], pltpu.roll(middle, SIDE - 1, axis=1))
    body = pl.ds(SIDE, CELLS)
    ref[step, body, 0:C] = before.reshape(CELLS, C).astype(BF)
    ref[step, body, C : 2 * C] = middle.reshape(CELLS, C).astype(BF)
    ref[step, body, 2 * C : 3 * C] = after.reshape(CELLS, C).astype(BF)
    ref[step, pl.ds(0, SIDE), :] = line_shifts(low)
    ref[step, pl.ds(SIDE + CELLS, SIDE), :] = line_shifts(high)


def early_kernel(fields_in, conv_in, raw_out, fields_ref, conv_ref, windows, raw_ref, sems):
    loads = [
        pltpu.make_async_copy(fields_in, fields_ref, sems.at[0]),
        pltpu.make_async_copy(conv_in, conv_ref, sems.at[1]),
    ]
    for load in loads:
        load.start()
    loads[0].wait()
    zero = jnp.zeros((SIDE, C), F32)
    stores = []
    for step in range(STEPS):
        store_shifts(windows, step, zero, zero, fields_ref[step].astype(F32), zero, zero)
        if step == 0:
            loads[1].wait()
        for start in range(0, CELLS, CHUNK):
            raw = jnp.zeros((CHUNK, C), F32)
            for p in range(3):
                window = windows[step, pl.ds(start + p * SIDE, CHUNK), :]
                raw = raw + mm(window, conv_ref[pl.ds(3 * C * p, 3 * C), :])
            raw_ref[step, pl.ds(start, CHUNK), :] = raw
        stores.append(pltpu.make_async_copy(raw_ref.at[step], raw_out.at[step], sems.at[2 + step]))
        stores[step].start()
    for store in stores:
        store.wait()


def main_kernel(
    belt_ref,
    turns_ref,
    *refs,
):
    sources, refs = refs[:12], refs[12:]
    grad_state_out, part_conv_out, keep_out, send_out = refs[:4]
    held, refs = refs[4:16], refs[16:]
    (
        windows,
        joined,
        gated_all,
        parts_t,
        part_conv,
        part_conv_t,
        last_state,
        grad_state,
        shares,
        in_sems,
        out_sems,
    ) = refs
    loads = [
        pltpu.make_async_copy(source, target, in_sems.at[k])
        for k, (source, target) in enumerate(zip(sources, held))
    ]
    for load in loads:
        load.start()
    (
        fields_ref,
        prev_ref,
        next_ref,
        conv_ref,
        raw_ref,
        state_ref,
        update_ref,
        reset_ref,
        candidate_ref,
        adjoint_ref,
        grad_out_ref,
        head_ref,
    ) = held
    for load in loads[:3]:
        load.wait()
    tops, bottoms, lefts, rights = [], [], [], []
    for step in range(STEPS):
        seams = seam_rows(
            belt_ref,
            turns_ref,
            fields_ref[step, 0],
            fields_ref[step, SIDE - 1],
            prev_ref[step],
            next_ref[step],
        )
        left = prev_ref[step, 0].astype(F32)
        right = next_ref[step, 0].astype(F32)
        store_shifts(
            windows,
            step,
            seams[:SIDE],
            seams[SIDE:],
            fields_ref[step].astype(F32),
            left,
            right,
        )
        tops.append(line_shifts(seams[:SIDE]))
        bottoms.append(line_shifts(seams[SIDE:]))
        lefts.append(line_shifts(left))
        rights.append(line_shifts(right))
    for load in loads[3:5]:
        load.wait()

    def taps_of(lines, taps):
        lines = jnp.concatenate(lines, axis=0)
        total = jnp.zeros((STEPS * SIDE, C), F32)
        for k, tap in enumerate(taps):
            total = total + mm(lines[:, k * C : (k + 1) * C], conv_ref[pl.ds(tap * C, C), :])
        return total

    top = taps_of(tops, (0, 1, 2))
    bottom = taps_of(bottoms, (6, 7, 8))
    left = taps_of(lefts, (0, 3, 6))
    right = taps_of(rights, (2, 5, 8))
    place = iota((SIDE, 8, C), 1)
    for step in range(STEPS):
        lines = slice(step * SIDE, (step + 1) * SIDE)
        raw_ref[step, 0, :, :] += top[lines]
        raw_ref[step, SIDE - 1, :, :] += bottom[lines]
        raw_ref[step, :, 0:8, :] += jnp.where(place == 0, left[lines][:, None, :], 0.0)
        raw_ref[step, :, SIDE - 8 : SIDE, :] += jnp.where(place == 7, right[lines][:, None, :], 0.0)
    for load in loads[5:]:
        load.wait()

    def chunk(start):
        rows = pl.ds(start, CHUNK)
        hidden = state_ref[rows, :]
        saved = []
        for step in range(STEPS):
            raw = raw_ref[step, pl.ds(start // SIDE, CHUNK // SIDE), :, :].reshape(CHUNK, C)
            bend = jnp.tanh(raw * (ROOT + (ROOT * CUBIC) * (raw * raw)))
            feature = (0.5 * raw * (1.0 + bend)).astype(BF)
            joined[step, rows, 0:C] = feature
            joined[step, rows, C : 2 * C] = hidden.astype(BF)
            both = joined[step, rows, :]
            update = 0.5 * jnp.tanh(0.5 * mm(both, update_ref[...])) + 0.5
            reset = 0.5 * jnp.tanh(0.5 * mm(both, reset_ref[...])) + 0.5
            gated = (reset * hidden).astype(BF)
            gated_all[step, rows, :] = gated
            candidate = jnp.tanh(
                mm(feature, candidate_ref[0:C, :]) + mm(gated, candidate_ref[C : 2 * C, :])
            )
            following = hidden + update * (candidate - hidden)
            saved.append((raw, bend, update, reset, candidate, hidden))
            hidden = following
        last_state[rows, :] = hidden.astype(BF)
        carried = adjoint_ref[rows, :]
        for step in reversed(range(STEPS)):
            raw, bend, update, reset, candidate, hidden = saved[step]
            total = carried + mm_tn(grad_out_ref[step, :, rows], head_ref[...])
            keep = 1.0 - update
            scaled = total * update
            part_cand = (scaled * (1.0 - candidate * candidate)).astype(BF)
            part_update = (scaled * (candidate - hidden) * keep).astype(BF)
            grad_gated = mm_nt(part_cand, candidate_ref[C : 2 * C, :])
            part_reset = (grad_gated * hidden * reset * (1.0 - reset)).astype(BF)
            parts_t[step, 0:C, rows] = part_cand.T
            parts_t[step, C : 2 * C, rows] = part_update.T
            parts_t[step, 2 * C : 3 * C, rows] = part_reset.T
            carried = (
                total * keep
                + grad_gated * reset
                + mm_nt(part_update, update_ref[C : 2 * C, :])
                + mm_nt(part_reset, reset_ref[C : 2 * C, :])
            )
            grad_feature = (
                mm_nt(part_cand, candidate_ref[0:C, :])
                + mm_nt(part_update, update_ref[0:C, :])
                + mm_nt(part_reset, reset_ref[0:C, :])
            )
            slope = 0.5 * (1.0 + bend) + (0.5 * ROOT) * raw * (1.0 - bend * bend) * (
                1.0 + (3.0 * CUBIC) * (raw * raw)
            )
            grad_raw = (grad_feature * slope).astype(BF)
            part_conv[step, rows, :] = grad_raw
            part_conv_t[step, :, rows] = grad_raw.T
        grad_state[rows, :] = carried

    for index in range(CELLS // CHUNK):
        chunk(index * CHUNK)
    stores = [
        pltpu.make_async_copy(grad_state, grad_state_out, out_sems.at[16]),
        pltpu.make_async_copy(part_conv, part_conv_out, out_sems.at[17]),
    ]
    for store in stores:
        store.start()

    core = lax.axis_index("core")

    def share(block, value):
        shares[block] = value.reshape(16, 16, C)
        kept = pltpu.make_async_copy(shares.at[block], keep_out.at[block % 8], out_sems.at[block])
        sent = pltpu.make_async_copy(shares.at[block], send_out.at[block % 8], out_sems.at[block])
        pl.when(core == block // 8)(kept.start)
        pl.when(core != block // 8)(sent.start)
        stores.append(kept)

    def over_steps(one):
        return one(0) + one(1)

    for gate in range(2):
        lanes = slice(C * (gate + 1), C * (gate + 2))
        grad = over_steps(lambda s: mm(parts_t[s, lanes, :], joined[s])).astype(BF)
        share(9 + 2 * gate, grad[:, :C])
        share(10 + 2 * gate, grad[:, C:])
    share(13, over_steps(lambda s: mm(parts_t[s, 0:C, :], joined[s, :, 0:C])).astype(BF))
    share(14, over_steps(lambda s: mm(parts_t[s, 0:C, :], gated_all[s])).astype(BF))
    grad_head = mm(grad_out_ref[0], joined[1, :, C : 2 * C]) + mm(grad_out_ref[1], last_state[...])
    grad_head = jnp.concatenate([grad_head, jnp.zeros((C - 8, C), F32)], axis=0)
    share(15, grad_head.T.astype(BF))
    for p in range(3):
        grad = over_steps(
            lambda s: mm(part_conv_t[s], windows[s, pl.ds(p * SIDE, CELLS), :])
        ).astype(BF)
        for q in range(3):
            share(3 * p + q, grad[:, q * C : (q + 1) * C].T)
    for store in stores:
        store.wait()


def outside_kernel(part_conv_ref, conv_ref, to_next_ref, to_prev_ref):
    picks = []
    row = iota((SIDE, CELLS), 0)
    cell = iota((SIDE, CELLS), 1)
    for col in (0, SIDE - 1):
        for p in range(3):
            at = row + 1 - p
            picks.append(one_hot((cell == at * SIDE + col) & (at >= 0) & (at < SIDE)))
    for line in (0, SIDE - 1):
        for q in range(3):
            at = row + 1 - q
            picks.append(one_hot((cell == line * SIDE + at) & (at >= 0) & (at < SIDE)))
    picks = jnp.concatenate(picks, axis=0)
    taps = [0, 3, 6, 2, 5, 8, 0, 1, 2, 6, 7, 8]
    for step in range(STEPS):
        picked = mm(picks, part_conv_ref[step]).astype(BF)
        outside = []
        for side in range(4):
            total = jnp.zeros((SIDE, C), F32)
            for k in range(3 * side, 3 * side + 3):
                total = total + mm_nt(
                    picked[k * SIDE : (k + 1) * SIDE], conv_ref[taps[k] * C : (taps[k] + 1) * C, :]
                )
            outside.append(total.astype(BF))
        to_next_ref[step, 0] = outside[1]
        to_prev_ref[step, 0] = outside[0]
        for ref in (to_next_ref, to_prev_ref):
            ref[step, 1] = outside[2]
            ref[step, 2] = outside[3]


def fields_kernel(
    belt_ref,
    turns_ref,
    part_conv_ref,
    own_ref,
    prev_ref,
    next_ref,
    conv_ref,
    grad_fields_ref,
    shifted,
):
    zero = jnp.zeros((SIDE, C), F32)
    for step in range(STEPS):
        store_shifts(
            shifted,
            step,
            zero,
            zero,
            part_conv_ref[step].astype(F32).reshape(SIDE, SIDE, C),
            zero,
            zero,
        )
        seams = seam_rows(
            belt_ref,
            turns_ref,
            own_ref[step, 1],
            own_ref[step, 2],
            prev_ref[step],
            next_ref[step],
        )
        left = prev_ref[step, 0].astype(F32)
        right = next_ref[step, 0].astype(F32)
        for part in range(4):
            at = part * 8
            grad = jnp.zeros((8 * SIDE, C), F32)
            for p in range(3):
                for q in range(3):
                    lanes = slice((2 - q) * C, (3 - q) * C)
                    window = shifted[step, pl.ds((at + 2 - p) * SIDE, 8 * SIDE), lanes]
                    tap = 3 * p + q
                    grad = grad + mm_nt(window, conv_ref[tap * C : (tap + 1) * C, :])
            grad = grad.reshape(8, SIDE, C)
            col = iota((8, SIDE, C), 1)
            row = iota((8, SIDE, C), 0)
            grad = grad + jnp.where(col == 0, left[at : at + 8][:, None, :], 0.0)
            grad = grad + jnp.where(col == SIDE - 1, right[at : at + 8][:, None, :], 0.0)
            if part == 0:
                grad = grad + jnp.where(row == 0, seams[:SIDE][None], 0.0)
            if part == 3:
                grad = grad + jnp.where(row == 7, seams[SIDE:][None], 0.0)
            grad_fields_ref[step, at : at + 8] = grad.astype(BF)


def in_vmem():
    return pl.BlockSpec(memory_space=pltpu.VMEM)


def in_smem():
    return pl.BlockSpec(memory_space=pltpu.SMEM)


def params(mebibytes=60):
    return pltpu.CompilerParams(vmem_limit_bytes=mebibytes << 20)


def shape(dims, kind=BF):
    return jax.ShapeDtypeStruct(dims, kind)


EDGE = (STEPS, 3, SIDE, C)


def edges_call(fields):
    return pl.pallas_call(
        edges_kernel,
        out_shape=(shape(EDGE), shape(EDGE)),
        in_specs=[in_vmem()],
        out_specs=(in_vmem(), in_vmem()),
        compiler_params=params(8),
        name="edges",
    )(fields)


def early_call(fields, conv):
    anywhere = pl.BlockSpec(memory_space=pl.ANY)
    raw = (STEPS, CELLS, C)
    return pl.pallas_call(
        early_kernel,
        out_shape=shape(raw, F32),
        in_specs=[anywhere] * 2,
        out_specs=anywhere,
        scratch_shapes=[
            pltpu.VMEM(fields.shape, BF),
            pltpu.VMEM(conv.shape, BF),
            pltpu.VMEM((STEPS, CELLS + 2 * SIDE, 3 * C), BF),
            pltpu.VMEM(raw, F32),
            pltpu.SemaphoreType.DMA((4,)),
        ],
        compiler_params=params(),
        cost_estimate=pl.CostEstimate(
            flops=2 * STEPS * CELLS * C * C * 9, bytes_accessed=5 << 20, transcendentals=0
        ),
        name="early",
    )(fields, conv)


def main_call(*args):
    anywhere = pl.BlockSpec(memory_space=pl.ANY)
    return pl.pallas_call(
        main_kernel,
        out_shape=(
            shape((CELLS, C), F32),
            shape((STEPS, CELLS, C)),
            shape((8, 16, 16, C)),
            shape((8, 16, 16, C)),
        ),
        in_specs=[in_smem()] * 2 + [anywhere] * 12,
        out_specs=(anywhere,) * 4,
        scratch_shapes=[pltpu.VMEM(arg.shape, arg.dtype) for arg in args[2:]]
        + [
            pltpu.VMEM((STEPS, CELLS + 2 * SIDE, 3 * C), BF),
            pltpu.VMEM((STEPS, CELLS, 2 * C), BF),
            pltpu.VMEM((STEPS, CELLS, C), BF),
            pltpu.VMEM((STEPS, 3 * C, CELLS), BF),
            pltpu.VMEM((STEPS, CELLS, C), BF),
            pltpu.VMEM((STEPS, C, CELLS), BF),
            pltpu.VMEM((CELLS, C), BF),
            pltpu.VMEM((CELLS, C), F32),
            pltpu.VMEM((16, 16, 16, C), BF),
            pltpu.SemaphoreType.DMA((12,)),
            pltpu.SemaphoreType.DMA((18,)),
        ],
        compiler_params=params(),
        name="steps",
    )(*args)


def outside_call(part_conv, conv):
    return pl.pallas_call(
        outside_kernel,
        out_shape=(shape(EDGE), shape(EDGE)),
        in_specs=[in_vmem()] * 2,
        out_specs=(in_vmem(), in_vmem()),
        compiler_params=params(16),
        cost_estimate=pl.CostEstimate(flops=1 << 30, bytes_accessed=3 << 20, transcendentals=0),
        name="outside",
    )(part_conv, conv)


def pair_kernel(left_ref, right_ref, out_ref):
    out_ref[...] = (left_ref[...].astype(F32) + right_ref[...].astype(F32)).astype(BF)


def pair_call(left, right):
    block = pl.BlockSpec((2, 16, 16, C), lambda i: (i, 0, 0, 0))
    return pl.pallas_call(
        pair_kernel,
        out_shape=shape(left.shape),
        grid=(4,),
        in_specs=[block, block],
        out_specs=block,
        compiler_params=params(8),
        name="pair",
    )(left, right)


def added_kernel(pieces_ref, out_ref):
    total = pieces_ref[0].astype(F32)
    for k in range(1, 8):
        total = total + pieces_ref[k].astype(F32)
    out_ref[...] = total.astype(BF)


def added_call(pieces):
    return pl.pallas_call(
        added_kernel,
        out_shape=shape((16, 16, C)),
        grid=(2,),
        in_specs=[pl.BlockSpec((8, 8, 16, C), lambda i: (0, i, 0, 0))],
        out_specs=pl.BlockSpec((8, 16, C), lambda i: (i, 0, 0)),
        compiler_params=params(8),
        name="added",
    )(pieces)


def fields_call(*args):
    return pl.pallas_call(
        fields_kernel,
        out_shape=shape((STEPS, SIDE, SIDE, C)),
        in_specs=[in_smem()] * 2 + [in_vmem()] * 5,
        out_specs=in_vmem(),
        scratch_shapes=[pltpu.VMEM((STEPS, CELLS + 2 * SIDE, 3 * C), BF)],
        compiler_params=params(20),
        cost_estimate=pl.CostEstimate(
            flops=2 * STEPS * CELLS * C * C * 9, bytes_accessed=4 << 20, transcendentals=0
        ),
        name="fields",
    )(*args)


RING = [(i, (i + 1) % 16) for i in range(16)]
BACK = [((i + 1) % 16, i) for i in range(16)]


def finish_kernel(whole_ref, conv_ref, update_ref, reset_ref, candidate_ref, head_ref):
    def block(k):
        return whole_ref[((k // 4) % 2) * 8 + (k % 4) * 2 + k // 8].astype(F32)

    for tap in range(9):
        conv_ref[tap] = block(tap)
    for ref, first in ((update_ref, 9), (reset_ref, 11), (candidate_ref, 13)):
        ref[:, 0:C] = block(first)
        ref[:, C : 2 * C] = block(first + 1)
    head_ref[...] = block(15).T[:8]


def finish_call(whole):
    gate = shape((16, 2 * C), F32)
    return pl.pallas_call(
        finish_kernel,
        out_shape=(shape((9, 16, C), F32), gate, gate, gate, shape((8, 16), F32)),
        in_specs=[in_vmem()],
        out_specs=tuple([in_vmem()] * 5),
        compiler_params=params(8),
        name="finish",
    )(whole)


def added(pieces):
    total = pieces[0].astype(F32)
    for k in range(1, pieces.shape[0]):
        total = total + pieces[k].astype(F32)
    return total


def body(
    fields_in,
    state_start,
    state_adjoint,
    output_grad,
    conv_weight,
    w_update,
    w_reset,
    w_candidate,
    head_weight,
    neighbor_tile,
    seam_turns,
):
    dp = ("x_hi", "y", "core")
    belt = ("x_lo", "z")
    seams = (neighbor_tile.T, seam_turns.T)
    fields = fields_in[0, 0]
    conv = conv_weight.reshape(9 * C, C)
    to_next, to_prev = edges_call(fields)
    prev = lax.ppermute(to_next, belt, RING)
    following = lax.ppermute(to_prev, belt, BACK)
    raw = early_call(fields, conv).reshape(STEPS, SIDE, SIDE, C)
    grad_state, part_conv, keep, send = main_call(
        *seams,
        fields,
        prev,
        following,
        conv,
        raw,
        state_start.reshape(CELLS, C),
        w_update,
        w_reset,
        w_candidate,
        state_adjoint.reshape(CELLS, C),
        output_grad[0, 0],
        head_weight,
    )
    got = lax.ppermute(send, "core", [(0, 1), (1, 0)])
    held = pair_call(keep, got)
    held = lax.all_to_all(held, ("x_hi", "y"), 0, 0, tiled=True)
    out_next, out_prev = outside_call(part_conv, conv)
    prev = lax.ppermute(out_next, belt, RING)
    following = lax.ppermute(out_prev, belt, BACK)
    held, prev, following = lax.optimization_barrier((held, prev, following))
    held = added_call(held)
    grad_fields = fields_call(*seams, part_conv, out_next, prev, following, conv)
    held = lax.all_to_all(held, belt, 0, 0, tiled=True)
    held = added(held).astype(BF)
    held, grad_fields = lax.optimization_barrier((held, grad_fields))
    whole = jnp.broadcast_to(held[None], (16, 16, C))
    whole = lax.all_to_all(whole, dp, 0, 0, tiled=True)
    grad_conv, grad_update, grad_reset, grad_candidate, grad_head = finish_call(whole)
    return (
        grad_fields[None, None],
        grad_state.reshape(1, 1, SIDE, SIDE, C),
        grad_conv,
        grad_update.T,
        grad_reset.T,
        grad_candidate.T,
        grad_head,
    )


def solution(mesh):
    cube = Mesh(mesh.devices.reshape(2, 4, 2, 2, 8), ("x_hi", "y", "core", "x_lo", "z"))
    dp = ("x_hi", "y", "core")
    tile = ("x_lo", "z")
    return jax.shard_map(
        body,
        mesh=cube,
        in_specs=(
            P(dp, tile, None, None, None, None),
            P(dp, tile, None, None, None),
            P(dp, tile, None, None, None),
            P(dp, tile, None, None, None),
            P(),
            P(),
            P(),
            P(),
            P(),
            P(),
            P(),
        ),
        out_specs=(
            P(dp, tile, None, None, None, None),
            P(dp, tile, None, None, None),
            P(None, tile, None),
            P(None, tile),
            P(None, tile),
            P(None, tile),
            P(None, tile),
        ),
        check_vma=False,
    )
```

```python
import math

import jax
import jax.numpy as jnp
import numpy as np
from jax import lax
from jax.experimental import pallas as pl
from jax.experimental.pallas import tpu as pltpu
from jax.sharding import Mesh
from jax.sharding import PartitionSpec as P

CUBIC = 0.044715
ROOT = math.sqrt(2.0 / math.pi)
BF = jnp.bfloat16
F32 = jnp.float32
SIDE = 32
CELLS = SIDE * SIDE
C = 256
STEPS = 2
CHUNK = 512


def mm(a, b):
    return lax.dot_general(a, b, (((1,), (0,)), ((), ())), preferred_element_type=F32)


def mm_nt(a, b):
    return lax.dot_general(a, b, (((1,), (1,)), ((), ())), preferred_element_type=F32)


def mm_tn(a, b):
    return lax.dot_general(a, b, (((0,), (0,)), ((), ())), preferred_element_type=F32)


def one_hot(cond):
    return jnp.where(cond, 1.0, 0.0).astype(BF)


def iota(shape, dim):
    return lax.broadcasted_iota(jnp.int32, shape, dim)


def edges_kernel(fields_ref, to_next_ref, to_prev_ref):
    for step in range(STEPS):
        to_next_ref[step, 0] = fields_ref[step, :, SIDE - 1, :]
        to_prev_ref[step, 0] = fields_ref[step, :, 0, :]
        for ref in (to_next_ref, to_prev_ref):
            ref[step, 1] = fields_ref[step, 0]
            ref[step, 2] = fields_ref[step, SIDE - 1]


def seam_of(belt_ref, turns_ref, side):
    tile = lax.axis_index(("x_lo", "z"))
    partner = belt_ref[side, tile]
    other = lax.rem(side + 2 - turns_ref[side, tile], 4)
    before = lax.rem(tile + 15, 16)
    place = jnp.where(partner == tile, 0, jnp.where(partner == before, 1, 2))
    base = (2 * place + jnp.where(other == 2, 1, 0)) * SIDE
    flip = other == side
    return jnp.where(flip, base + SIDE - 1, base), jnp.where(flip, -1, 1)


def seam_rows(belt_ref, turns_ref, own_top, own_bottom, from_prev, from_next):
    stacked = jnp.concatenate(
        [own_top, own_bottom, from_prev[1], from_prev[2], from_next[1], from_next[2]], axis=0
    )
    rows = iota((2 * SIDE, 6 * SIDE), 0)
    cols = iota((2 * SIDE, 6 * SIDE), 1)
    top_base, top_sign = seam_of(belt_ref, turns_ref, 0)
    bottom_base, bottom_sign = seam_of(belt_ref, turns_ref, 2)
    wanted = jnp.where(
        rows < SIDE, top_base + top_sign * rows, bottom_base + bottom_sign * (rows - SIDE)
    )
    return mm(one_hot(cols == wanted), stacked)


def line_shifts(line):
    at = iota((SIDE, C), 0)
    before = jnp.where(at == 0, 0.0, pltpu.roll(line, 1, axis=0))
    after = jnp.where(at == SIDE - 1, 0.0, pltpu.roll(line, SIDE - 1, axis=0))
    return jnp.concatenate([before, line, after], axis=1).astype(BF)


def store_shifts(ref, step, low, high, middle, left, right):
    col = iota((SIDE, SIDE, C), 1)
    before = jnp.where(col == 0, left[:, None, :], pltpu.roll(middle, 1, axis=1))
    after = jnp.where(col == SIDE - 1, right[:, None, :], pltpu.roll(middle, SIDE - 1, axis=1))
    body = pl.ds(SIDE, CELLS)
    ref[step, body, 0:C] = before.reshape(CELLS, C).astype(BF)
    ref[step, body, C : 2 * C] = middle.reshape(CELLS, C).astype(BF)
    ref[step, body, 2 * C : 3 * C] = after.reshape(CELLS, C).astype(BF)
    ref[step, pl.ds(0, SIDE), :] = line_shifts(low)
    ref[step, pl.ds(SIDE + CELLS, SIDE), :] = line_shifts(high)


def early_kernel(fields_in, conv_in, raw_out, fields_ref, conv_ref, windows, raw_ref, sems):
    loads = [
        pltpu.make_async_copy(fields_in.at[0], fields_ref.at[0], sems.at[0]),
        pltpu.make_async_copy(fields_in.at[1], fields_ref.at[1], sems.at[1]),
        pltpu.make_async_copy(conv_in, conv_ref, sems.at[2]),
    ]
    for load in loads:
        load.start()
    zero = jnp.zeros((SIDE, C), F32)
    stores = []
    loads[0].wait()
    store_shifts(windows, 0, zero, zero, fields_ref[0].astype(F32), zero, zero)
    loads[1].wait()
    loads[2].wait()
    for step in range(STEPS):
        if step == 0:
            store_shifts(windows, 1, zero, zero, fields_ref[1].astype(F32), zero, zero)
        for start in range(0, CELLS, CHUNK):
            raw = jnp.zeros((CHUNK, C), F32)
            for p in range(3):
                window = windows[step, pl.ds(start + p * SIDE, CHUNK), :]
                raw = raw + mm(window, conv_ref[pl.ds(3 * C * p, 3 * C), :])
            rows = pl.ds(start, CHUNK)
            raw_ref[step, rows, :] = raw
            at = (step, rows)
            sem = sems.at[3 + step * (CELLS // CHUNK) + start // CHUNK]
            stores.append(pltpu.make_async_copy(raw_ref.at[at], raw_out.at[at], sem))
            stores[-1].start()
    for store in stores:
        store.wait()


def main_kernel(
    belt_ref,
    turns_ref,
    *refs,
):
    sources, refs = refs[:12], refs[12:]
    grad_state_out, part_conv_out, keep_out, send_out = refs[:4]
    held, refs = refs[4:16], refs[16:]
    (
        windows,
        joined,
        gated_all,
        parts_t,
        part_conv,
        part_conv_t,
        last_state,
        grad_state,
        shares,
        in_sems,
        out_sems,
    ) = refs
    loads = [
        pltpu.make_async_copy(source, target, in_sems.at[k])
        for k, (source, target) in enumerate(zip(sources, held))
    ]
    for load in loads[:9]:
        load.start()
    (
        fields_ref,
        prev_ref,
        next_ref,
        conv_ref,
        raw_ref,
        state_ref,
        update_ref,
        reset_ref,
        candidate_ref,
        adjoint_ref,
        grad_out_ref,
        head_ref,
    ) = held
    for load in loads[:3]:
        load.wait()
    tops, bottoms, lefts, rights = [], [], [], []
    for step in range(STEPS):
        seams = seam_rows(
            belt_ref,
            turns_ref,
            fields_ref[step, 0],
            fields_ref[step, SIDE - 1],
            prev_ref[step],
            next_ref[step],
        )
        left = prev_ref[step, 0].astype(F32)
        right = next_ref[step, 0].astype(F32)
        store_shifts(
            windows,
            step,
            seams[:SIDE],
            seams[SIDE:],
            fields_ref[step].astype(F32),
            left,
            right,
        )
        tops.append(line_shifts(seams[:SIDE]))
        bottoms.append(line_shifts(seams[SIDE:]))
        lefts.append(line_shifts(left))
        rights.append(line_shifts(right))
    for load in loads[3:5]:
        load.wait()

    def taps_of(lines, taps):
        lines = jnp.concatenate(lines, axis=0)
        total = jnp.zeros((STEPS * SIDE, C), F32)
        for k, tap in enumerate(taps):
            total = total + mm(lines[:, k * C : (k + 1) * C], conv_ref[pl.ds(tap * C, C), :])
        return total

    top = taps_of(tops, (0, 1, 2))
    bottom = taps_of(bottoms, (6, 7, 8))
    left = taps_of(lefts, (0, 3, 6))
    right = taps_of(rights, (2, 5, 8))
    place = iota((SIDE, 8, C), 1)
    for step in range(STEPS):
        lines = slice(step * SIDE, (step + 1) * SIDE)
        raw_ref[step, 0, :, :] += top[lines]
        raw_ref[step, SIDE - 1, :, :] += bottom[lines]
        raw_ref[step, :, 0:8, :] += jnp.where(place == 0, left[lines][:, None, :], 0.0)
        raw_ref[step, :, SIDE - 8 : SIDE, :] += jnp.where(place == 7, right[lines][:, None, :], 0.0)
    for load in loads[5:9]:
        load.wait()
    for load in loads[9:]:
        load.start()

    def chunk(start):
        rows = pl.ds(start, CHUNK)
        hidden = state_ref[rows, :]
        saved = []
        for step in range(STEPS):
            raw = raw_ref[step, pl.ds(start // SIDE, CHUNK // SIDE), :, :].reshape(CHUNK, C)
            bend = jnp.tanh(raw * (ROOT + (ROOT * CUBIC) * (raw * raw)))
            feature = (0.5 * raw * (1.0 + bend)).astype(BF)
            joined[step, rows, 0:C] = feature
            joined[step, rows, C : 2 * C] = hidden.astype(BF)
            both = joined[step, rows, :]
            update = 0.5 * jnp.tanh(0.5 * mm(both, update_ref[...])) + 0.5
            reset = 0.5 * jnp.tanh(0.5 * mm(both, reset_ref[...])) + 0.5
            gated = (reset * hidden).astype(BF)
            gated_all[step, rows, :] = gated
            candidate = jnp.tanh(
                mm(feature, candidate_ref[0:C, :]) + mm(gated, candidate_ref[C : 2 * C, :])
            )
            following = hidden + update * (candidate - hidden)
            saved.append((raw, bend, update, reset, candidate, hidden))
            hidden = following
        last_state[rows, :] = hidden.astype(BF)
        if start == 0:
            for load in loads[9:]:
                load.wait()
        carried = adjoint_ref[rows, :]
        for step in reversed(range(STEPS)):
            raw, bend, update, reset, candidate, hidden = saved[step]
            total = carried + mm_tn(grad_out_ref[step, :, rows], head_ref[...])
            keep = 1.0 - update
            scaled = total * update
            part_cand = (scaled * (1.0 - candidate * candidate)).astype(BF)
            part_update = (scaled * (candidate - hidden) * keep).astype(BF)
            grad_gated = mm_nt(part_cand, candidate_ref[C : 2 * C, :])
            part_reset = (grad_gated * hidden * reset * (1.0 - reset)).astype(BF)
            parts_t[step, 0:C, rows] = part_cand.T
            parts_t[step, C : 2 * C, rows] = part_update.T
            parts_t[step, 2 * C : 3 * C, rows] = part_reset.T
            carried = (
                total * keep
                + grad_gated * reset
                + mm_nt(part_update, update_ref[C : 2 * C, :])
                + mm_nt(part_reset, reset_ref[C : 2 * C, :])
            )
            grad_feature = (
                mm_nt(part_cand, candidate_ref[0:C, :])
                + mm_nt(part_update, update_ref[0:C, :])
                + mm_nt(part_reset, reset_ref[0:C, :])
            )
            slope = 0.5 * (1.0 + bend) + (0.5 * ROOT) * raw * (1.0 - bend * bend) * (
                1.0 + (3.0 * CUBIC) * (raw * raw)
            )
            grad_raw = (grad_feature * slope).astype(BF)
            part_conv[step, rows, :] = grad_raw
            part_conv_t[step, :, rows] = grad_raw.T
        grad_state[rows, :] = carried

    for index in range(CELLS // CHUNK):
        chunk(index * CHUNK)
    stores = [
        pltpu.make_async_copy(grad_state, grad_state_out, out_sems.at[16]),
        pltpu.make_async_copy(part_conv, part_conv_out, out_sems.at[17]),
    ]
    for store in stores:
        store.start()

    core = lax.axis_index("core")

    def share(block, value):
        shares[block] = value.reshape(16, 16, C)
        x_hi, y = block % 8 // 4, block % 4
        if block < 8:
            pieces = [(slice(0, 16), y, x_hi * 16)]
        else:
            pieces = [(slice(k * 8, k * 8 + 8), 2 * x_hi + k, y * 8) for k in range(2)]
        for lines, place, first in pieces:
            count = lines.stop - lines.start
            where = (place, pl.ds(first, count))
            sem = out_sems.at[block]
            kept = pltpu.make_async_copy(shares.at[block, lines], keep_out.at[where], sem)
            sent = pltpu.make_async_copy(shares.at[block, lines], send_out.at[where], sem)
            pl.when(core == block // 8)(kept.start)
            pl.when(core != block // 8)(sent.start)
            stores.append(kept)

    def over_steps(one):
        return one(0) + one(1)

    for gate in range(2):
        lanes = slice(C * (gate + 1), C * (gate + 2))
        grad = over_steps(lambda s: mm(parts_t[s, lanes, :], joined[s])).astype(BF)
        share(9 + 2 * gate, grad[:, :C])
        share(10 + 2 * gate, grad[:, C:])
    share(13, over_steps(lambda s: mm(parts_t[s, 0:C, :], joined[s, :, 0:C])).astype(BF))
    share(14, over_steps(lambda s: mm(parts_t[s, 0:C, :], gated_all[s])).astype(BF))
    grad_head = mm(grad_out_ref[0], joined[1, :, C : 2 * C]) + mm(grad_out_ref[1], last_state[...])
    grad_head = jnp.concatenate([grad_head, jnp.zeros((C - 8, C), F32)], axis=0)
    share(15, grad_head.T.astype(BF))
    for p in range(3):
        grad = over_steps(
            lambda s: mm(part_conv_t[s], windows[s, pl.ds(p * SIDE, CELLS), :])
        ).astype(BF)
        for q in range(3):
            share(3 * p + q, grad[:, q * C : (q + 1) * C].T)
    for store in stores:
        store.wait()


def outside_kernel(part_conv_ref, conv_ref, to_next_ref, to_prev_ref):
    picks = []
    row = iota((SIDE, CELLS), 0)
    cell = iota((SIDE, CELLS), 1)
    for col in (0, SIDE - 1):
        for p in range(3):
            at = row + 1 - p
            picks.append(one_hot((cell == at * SIDE + col) & (at >= 0) & (at < SIDE)))
    for line in (0, SIDE - 1):
        for q in range(3):
            at = row + 1 - q
            picks.append(one_hot((cell == line * SIDE + at) & (at >= 0) & (at < SIDE)))
    picks = jnp.concatenate(picks, axis=0)
    taps = [0, 3, 6, 2, 5, 8, 0, 1, 2, 6, 7, 8]
    for step in range(STEPS):
        picked = mm(picks, part_conv_ref[step]).astype(BF)
        outside = []
        for side in range(4):
            total = jnp.zeros((SIDE, C), F32)
            for k in range(3 * side, 3 * side + 3):
                total = total + mm_nt(
                    picked[k * SIDE : (k + 1) * SIDE], conv_ref[taps[k] * C : (taps[k] + 1) * C, :]
                )
            outside.append(total.astype(BF))
        to_next_ref[step, 0] = outside[1]
        to_prev_ref[step, 0] = outside[0]
        for ref in (to_next_ref, to_prev_ref):
            ref[step, 1] = outside[2]
            ref[step, 2] = outside[3]


def fields_kernel(
    belt_ref,
    turns_ref,
    part_conv_ref,
    own_ref,
    prev_ref,
    next_ref,
    conv_ref,
    grad_fields_ref,
    shifted,
):
    zero = jnp.zeros((SIDE, C), F32)
    for step in range(STEPS):
        store_shifts(
            shifted,
            step,
            zero,
            zero,
            part_conv_ref[step].astype(F32).reshape(SIDE, SIDE, C),
            zero,
            zero,
        )
        seams = seam_rows(
            belt_ref,
            turns_ref,
            own_ref[step, 1],
            own_ref[step, 2],
            prev_ref[step],
            next_ref[step],
        )
        left = prev_ref[step, 0].astype(F32)
        right = next_ref[step, 0].astype(F32)
        for part in range(4):
            at = part * 8
            grad = jnp.zeros((8 * SIDE, C), F32)
            for p in range(3):
                for q in range(3):
                    lanes = slice((2 - q) * C, (3 - q) * C)
                    window = shifted[step, pl.ds((at + 2 - p) * SIDE, 8 * SIDE), lanes]
                    tap = 3 * p + q
                    grad = grad + mm_nt(window, conv_ref[tap * C : (tap + 1) * C, :])
            grad = grad.reshape(8, SIDE, C)
            col = iota((8, SIDE, C), 1)
            row = iota((8, SIDE, C), 0)
            grad = grad + jnp.where(col == 0, left[at : at + 8][:, None, :], 0.0)
            grad = grad + jnp.where(col == SIDE - 1, right[at : at + 8][:, None, :], 0.0)
            if part == 0:
                grad = grad + jnp.where(row == 0, seams[:SIDE][None], 0.0)
            if part == 3:
                grad = grad + jnp.where(row == 7, seams[SIDE:][None], 0.0)
            grad_fields_ref[step, at : at + 8] = grad.astype(BF)


def in_vmem():
    return pl.BlockSpec(memory_space=pltpu.VMEM)


def in_smem():
    return pl.BlockSpec(memory_space=pltpu.SMEM)


def params(mebibytes=60):
    return pltpu.CompilerParams(vmem_limit_bytes=mebibytes << 20)


def busy():
    return pl.CostEstimate(flops=1 << 33, bytes_accessed=1 << 16, transcendentals=0)


def shape(dims, kind=BF):
    return jax.ShapeDtypeStruct(dims, kind)


EDGE = (STEPS, 3, SIDE, C)


def edges_call(fields):
    return pl.pallas_call(
        edges_kernel,
        out_shape=(shape(EDGE), shape(EDGE)),
        in_specs=[in_vmem()],
        out_specs=(in_vmem(), in_vmem()),
        compiler_params=params(8),
        name="edges",
    )(fields)


def early_call(fields, conv):
    anywhere = pl.BlockSpec(memory_space=pl.ANY)
    raw = (STEPS, CELLS, C)
    return pl.pallas_call(
        early_kernel,
        out_shape=shape(raw, F32),
        in_specs=[anywhere] * 2,
        out_specs=anywhere,
        scratch_shapes=[
            pltpu.VMEM(fields.shape, BF),
            pltpu.VMEM(conv.shape, BF),
            pltpu.VMEM((STEPS, CELLS + 2 * SIDE, 3 * C), BF),
            pltpu.VMEM(raw, F32),
            pltpu.SemaphoreType.DMA((7,)),
        ],
        compiler_params=params(),
        cost_estimate=pl.CostEstimate(
            flops=2 * STEPS * CELLS * C * C * 9, bytes_accessed=5 << 20, transcendentals=0
        ),
        name="early",
    )(fields, conv)


def main_call(*args):
    anywhere = pl.BlockSpec(memory_space=pl.ANY)
    return pl.pallas_call(
        main_kernel,
        out_shape=(
            shape((CELLS, C), F32),
            shape((STEPS, CELLS, C)),
            shape((4, 32, 16, C)),
            shape((4, 32, 16, C)),
        ),
        in_specs=[in_smem()] * 2 + [anywhere] * 12,
        out_specs=(anywhere,) * 4,
        scratch_shapes=[pltpu.VMEM(arg.shape, arg.dtype) for arg in args[2:]]
        + [
            pltpu.VMEM((STEPS, CELLS + 2 * SIDE, 3 * C), BF),
            pltpu.VMEM((STEPS, CELLS, 2 * C), BF),
            pltpu.VMEM((STEPS, CELLS, C), BF),
            pltpu.VMEM((STEPS, 3 * C, CELLS), BF),
            pltpu.VMEM((STEPS, CELLS, C), BF),
            pltpu.VMEM((STEPS, C, CELLS), BF),
            pltpu.VMEM((CELLS, C), BF),
            pltpu.VMEM((CELLS, C), F32),
            pltpu.VMEM((16, 16, 16, C), BF),
            pltpu.SemaphoreType.DMA((12,)),
            pltpu.SemaphoreType.DMA((18,)),
        ],
        compiler_params=params(),
        name="steps",
    )(*args)


def outside_call(part_conv, conv):
    return pl.pallas_call(
        outside_kernel,
        out_shape=(shape(EDGE), shape(EDGE)),
        in_specs=[in_vmem()] * 2,
        out_specs=(in_vmem(), in_vmem()),
        compiler_params=params(16),
        cost_estimate=pl.CostEstimate(flops=1 << 30, bytes_accessed=3 << 20, transcendentals=0),
        name="outside",
    )(part_conv, conv)


def pair_kernel(left_ref, right_ref, out_ref):
    out_ref[...] = (left_ref[...].astype(F32) + right_ref[...].astype(F32)).astype(BF)


def pair_call(left, right):
    block = pl.BlockSpec((1, 32, 16, C), lambda i: (i, 0, 0, 0))
    return pl.pallas_call(
        pair_kernel,
        out_shape=shape(left.shape),
        grid=(4,),
        in_specs=[block, block],
        out_specs=block,
        compiler_params=params(8),
        cost_estimate=busy(),
        name="pair",
    )(left, right)


def added_kernel(pieces_ref, out_ref):
    total = pieces_ref[0].astype(F32)
    for k in range(1, pieces_ref.shape[0]):
        total = total + pieces_ref[k].astype(F32)
    out_ref[...] = total.astype(BF)


def added_call(pieces):
    return pl.pallas_call(
        added_kernel,
        out_shape=shape((32, 16, C)),
        grid=(2,),
        in_specs=[pl.BlockSpec((4, 16, 16, C), lambda i: (0, i, 0, 0))],
        out_specs=pl.BlockSpec((16, 16, C), lambda i: (i, 0, 0)),
        compiler_params=params(8),
        cost_estimate=busy(),
        name="added",
    )(pieces)


def fields_call(*args):
    return pl.pallas_call(
        fields_kernel,
        out_shape=shape((STEPS, SIDE, SIDE, C)),
        in_specs=[in_smem()] * 2 + [in_vmem()] * 5,
        out_specs=in_vmem(),
        scratch_shapes=[pltpu.VMEM((STEPS, CELLS + 2 * SIDE, 3 * C), BF)],
        compiler_params=params(20),
        cost_estimate=pl.CostEstimate(
            flops=2 * STEPS * CELLS * C * C * 9, bytes_accessed=4 << 20, transcendentals=0
        ),
        name="fields",
    )(*args)


RING = [(i, (i + 1) % 16) for i in range(16)]
BACK = [((i + 1) % 16, i) for i in range(16)]


def finish_kernel(whole_ref, conv_ref, update_ref, reset_ref, candidate_ref, head_ref):
    def block(k):
        return whole_ref[((k // 4) % 2) * 8 + (k % 4) * 2 + k // 8].astype(F32)

    for tap in range(9):
        conv_ref[tap] = block(tap)
    for ref, first in ((update_ref, 9), (reset_ref, 11), (candidate_ref, 13)):
        ref[:, 0:C] = block(first)
        ref[:, C : 2 * C] = block(first + 1)
    head_ref[...] = block(15).T[:8]


def finish_call(whole):
    gate = shape((16, 2 * C), F32)
    return pl.pallas_call(
        finish_kernel,
        out_shape=(shape((9, 16, C), F32), gate, gate, gate, shape((8, 16), F32)),
        in_specs=[in_vmem()],
        out_specs=tuple([in_vmem()] * 5),
        compiler_params=params(8),
        name="finish",
    )(whole)


def added(pieces):
    total = pieces[0].astype(F32)
    for k in range(1, pieces.shape[0]):
        total = total + pieces[k].astype(F32)
    return total


EVERY = ("x_hi", "y", "core", "x_lo", "z")


def groups_of(*axes_of_core):
    devices = np.arange(256).reshape(2, 4, 2, 2, 8)
    found = []
    for core, axes in enumerate(axes_of_core):
        inner = [("x_hi", "y", "x_lo", "z").index(axis) for axis in axes]
        outer = [axis for axis in range(4) if axis not in inner]
        here = devices[:, :, core].transpose(outer + inner)
        size = math.prod(here.shape[len(outer) :])
        found += here.reshape(-1, size).tolist()
    return found


FIRST = groups_of(("y",), ("x_hi", "x_lo"))
SECOND = groups_of(("x_hi", "x_lo", "z"), ("y", "z"))


def body(
    fields_in,
    state_start,
    state_adjoint,
    output_grad,
    conv_weight,
    w_update,
    w_reset,
    w_candidate,
    head_weight,
    neighbor_tile,
    seam_turns,
):
    dp = ("x_hi", "y", "core")
    belt = ("x_lo", "z")
    seams = (neighbor_tile.T, seam_turns.T)
    fields = fields_in[0, 0]
    conv = conv_weight.reshape(9 * C, C)
    to_next, to_prev = edges_call(fields)
    prev = lax.ppermute(to_next, belt, RING)
    following = lax.ppermute(to_prev, belt, BACK)
    raw = early_call(fields, conv).reshape(STEPS, SIDE, SIDE, C)
    grad_state, part_conv, keep, send = main_call(
        *seams,
        fields,
        prev,
        following,
        conv,
        raw,
        state_start.reshape(CELLS, C),
        w_update,
        w_reset,
        w_candidate,
        state_adjoint.reshape(CELLS, C),
        output_grad[0, 0],
        head_weight,
    )
    got = lax.ppermute(send, "core", [(0, 1), (1, 0)])
    out_next, out_prev = outside_call(part_conv, conv)
    got, out_next, out_prev = lax.optimization_barrier((got, out_next, out_prev))
    held = pair_call(keep, got)
    held = lax.all_to_all(held, EVERY, 0, 0, axis_index_groups=FIRST, tiled=True)
    prev = lax.ppermute(out_next, belt, RING)
    following = lax.ppermute(out_prev, belt, BACK)
    held, prev, following = lax.optimization_barrier((held, prev, following))
    held = added_call(held)
    grad_fields = fields_call(*seams, part_conv, out_next, prev, following, conv)
    held = lax.all_to_all(held, EVERY, 0, 0, axis_index_groups=SECOND, tiled=True)
    held = added(held).astype(BF)
    held, grad_fields = lax.optimization_barrier((held, grad_fields))
    whole = jnp.broadcast_to(held[None], (16, 16, C))
    whole = lax.all_to_all(whole, dp, 0, 0, tiled=True)
    grad_conv, grad_update, grad_reset, grad_candidate, grad_head = finish_call(whole)
    return (
        grad_fields[None, None],
        grad_state.reshape(1, 1, SIDE, SIDE, C),
        grad_conv,
        grad_update.T,
        grad_reset.T,
        grad_candidate.T,
        grad_head,
    )


def solution(mesh):
    cube = Mesh(mesh.devices.reshape(2, 4, 2, 2, 8), ("x_hi", "y", "core", "x_lo", "z"))
    dp = ("x_hi", "y", "core")
    tile = ("x_lo", "z")
    return jax.shard_map(
        body,
        mesh=cube,
        in_specs=(
            P(dp, tile, None, None, None, None),
            P(dp, tile, None, None, None),
            P(dp, tile, None, None, None),
            P(dp, tile, None, None, None),
            P(),
            P(),
            P(),
            P(),
            P(),
            P(),
            P(),
        ),
        out_specs=(
            P(dp, tile, None, None, None, None),
            P(dp, tile, None, None, None),
            P(None, tile, None),
            P(None, tile),
            P(None, tile),
            P(None, tile),
            P(None, tile),
        ),
        check_vma=False,
    )
```

```python
import math

import jax
import jax.numpy as jnp
import numpy as np
from jax import lax
from jax.experimental import pallas as pl
from jax.experimental.pallas import tpu as pltpu
from jax.sharding import Mesh
from jax.sharding import PartitionSpec as P

CUBIC = 0.044715
ROOT = math.sqrt(2.0 / math.pi)
BF = jnp.bfloat16
F32 = jnp.float32
SIDE = 32
CELLS = SIDE * SIDE
C = 256
STEPS = 2
CHUNK = 512


def mm(a, b):
    return lax.dot_general(a, b, (((1,), (0,)), ((), ())), preferred_element_type=F32)


def mm_nt(a, b):
    return lax.dot_general(a, b, (((1,), (1,)), ((), ())), preferred_element_type=F32)


def mm_tn(a, b):
    return lax.dot_general(a, b, (((0,), (0,)), ((), ())), preferred_element_type=F32)


def one_hot(cond):
    return jnp.where(cond, 1.0, 0.0).astype(BF)


def iota(shape, dim):
    return lax.broadcasted_iota(jnp.int32, shape, dim)


def edges_kernel(fields_ref, to_next_ref, to_prev_ref):
    for step in range(STEPS):
        to_next_ref[step, 0] = fields_ref[step, :, SIDE - 1, :]
        to_prev_ref[step, 0] = fields_ref[step, :, 0, :]
        for ref in (to_next_ref, to_prev_ref):
            ref[step, 1] = fields_ref[step, 0]
            ref[step, 2] = fields_ref[step, SIDE - 1]


def seam_of(belt_ref, turns_ref, side):
    tile = lax.axis_index(("x_lo", "z"))
    partner = belt_ref[side, tile]
    other = lax.rem(side + 2 - turns_ref[side, tile], 4)
    before = lax.rem(tile + 15, 16)
    place = jnp.where(partner == tile, 0, jnp.where(partner == before, 1, 2))
    base = (2 * place + jnp.where(other == 2, 1, 0)) * SIDE
    flip = other == side
    return jnp.where(flip, base + SIDE - 1, base), jnp.where(flip, -1, 1)


def seam_rows(belt_ref, turns_ref, own_top, own_bottom, from_prev, from_next):
    stacked = jnp.concatenate(
        [own_top, own_bottom, from_prev[1], from_prev[2], from_next[1], from_next[2]], axis=0
    )
    rows = iota((2 * SIDE, 6 * SIDE), 0)
    cols = iota((2 * SIDE, 6 * SIDE), 1)
    top_base, top_sign = seam_of(belt_ref, turns_ref, 0)
    bottom_base, bottom_sign = seam_of(belt_ref, turns_ref, 2)
    wanted = jnp.where(
        rows < SIDE, top_base + top_sign * rows, bottom_base + bottom_sign * (rows - SIDE)
    )
    return mm(one_hot(cols == wanted), stacked)


def line_shifts(line):
    at = iota((SIDE, C), 0)
    before = jnp.where(at == 0, 0.0, pltpu.roll(line, 1, axis=0))
    after = jnp.where(at == SIDE - 1, 0.0, pltpu.roll(line, SIDE - 1, axis=0))
    return jnp.concatenate([before, line, after], axis=1).astype(BF)


def store_shifts(ref, step, low, high, middle, left, right):
    col = iota((SIDE, SIDE, C), 1)
    before = jnp.where(col == 0, left[:, None, :], pltpu.roll(middle, 1, axis=1))
    after = jnp.where(col == SIDE - 1, right[:, None, :], pltpu.roll(middle, SIDE - 1, axis=1))
    body = pl.ds(SIDE, CELLS)
    ref[step, body, 0:C] = before.reshape(CELLS, C).astype(BF)
    ref[step, body, C : 2 * C] = middle.reshape(CELLS, C).astype(BF)
    ref[step, body, 2 * C : 3 * C] = after.reshape(CELLS, C).astype(BF)
    ref[step, pl.ds(0, SIDE), :] = line_shifts(low)
    ref[step, pl.ds(SIDE + CELLS, SIDE), :] = line_shifts(high)


def early_kernel(fields_in, conv_in, raw_out, fields_ref, conv_ref, windows, raw_ref, sems):
    loads = [
        pltpu.make_async_copy(fields_in.at[0], fields_ref.at[0], sems.at[0]),
        pltpu.make_async_copy(fields_in.at[1], fields_ref.at[1], sems.at[1]),
        pltpu.make_async_copy(conv_in, conv_ref, sems.at[2]),
    ]
    for load in loads:
        load.start()
    zero = jnp.zeros((SIDE, C), F32)
    stores = []
    loads[0].wait()
    store_shifts(windows, 0, zero, zero, fields_ref[0].astype(F32), zero, zero)
    loads[1].wait()
    loads[2].wait()
    for step in range(STEPS):
        if step == 0:
            store_shifts(windows, 1, zero, zero, fields_ref[1].astype(F32), zero, zero)
        for start in range(0, CELLS, CHUNK):
            raw = jnp.zeros((CHUNK, C), F32)
            for p in range(3):
                window = windows[step, pl.ds(start + p * SIDE, CHUNK), :]
                raw = raw + mm(window, conv_ref[pl.ds(3 * C * p, 3 * C), :])
            rows = pl.ds(start, CHUNK)
            raw_ref[step, rows, :] = raw
            at = (step, rows)
            sem = sems.at[3 + step * (CELLS // CHUNK) + start // CHUNK]
            stores.append(pltpu.make_async_copy(raw_ref.at[at], raw_out.at[at], sem))
            stores[-1].start()
    for store in stores:
        store.wait()


def main_kernel(
    belt_ref,
    turns_ref,
    *refs,
):
    sources, refs = refs[:12], refs[12:]
    grad_state_out, part_conv_out, keep_out, send_out = refs[:4]
    held, refs = refs[4:16], refs[16:]
    (
        windows,
        joined,
        gated_all,
        parts_t,
        part_conv,
        part_conv_t,
        last_state,
        grad_state,
        shares,
        in_sems,
        out_sems,
    ) = refs
    loads = [
        pltpu.make_async_copy(source, target, in_sems.at[k])
        for k, (source, target) in enumerate(zip(sources, held))
    ]
    for load in loads[:9]:
        load.start()
    (
        fields_ref,
        prev_ref,
        next_ref,
        conv_ref,
        raw_ref,
        state_ref,
        update_ref,
        reset_ref,
        candidate_ref,
        adjoint_ref,
        grad_out_ref,
        head_ref,
    ) = held
    for load in loads[:3]:
        load.wait()
    tops, bottoms, lefts, rights = [], [], [], []
    for step in range(STEPS):
        seams = seam_rows(
            belt_ref,
            turns_ref,
            fields_ref[step, 0],
            fields_ref[step, SIDE - 1],
            prev_ref[step],
            next_ref[step],
        )
        left = prev_ref[step, 0].astype(F32)
        right = next_ref[step, 0].astype(F32)
        store_shifts(
            windows,
            step,
            seams[:SIDE],
            seams[SIDE:],
            fields_ref[step].astype(F32),
            left,
            right,
        )
        tops.append(line_shifts(seams[:SIDE]))
        bottoms.append(line_shifts(seams[SIDE:]))
        lefts.append(line_shifts(left))
        rights.append(line_shifts(right))
    for load in loads[3:5]:
        load.wait()

    def taps_of(lines, taps):
        lines = jnp.concatenate(lines, axis=0)
        total = jnp.zeros((STEPS * SIDE, C), F32)
        for k, tap in enumerate(taps):
            total = total + mm(lines[:, k * C : (k + 1) * C], conv_ref[pl.ds(tap * C, C), :])
        return total

    top = taps_of(tops, (0, 1, 2))
    bottom = taps_of(bottoms, (6, 7, 8))
    left = taps_of(lefts, (0, 3, 6))
    right = taps_of(rights, (2, 5, 8))
    place = iota((SIDE, 8, C), 1)
    for step in range(STEPS):
        lines = slice(step * SIDE, (step + 1) * SIDE)
        raw_ref[step, 0, :, :] += top[lines]
        raw_ref[step, SIDE - 1, :, :] += bottom[lines]
        raw_ref[step, :, 0:8, :] += jnp.where(place == 0, left[lines][:, None, :], 0.0)
        raw_ref[step, :, SIDE - 8 : SIDE, :] += jnp.where(place == 7, right[lines][:, None, :], 0.0)
    for load in loads[5:9]:
        load.wait()
    for load in loads[9:]:
        load.start()

    def chunk(start):
        rows = pl.ds(start, CHUNK)
        hidden = state_ref[rows, :]
        saved = []
        for step in range(STEPS):
            raw = raw_ref[step, pl.ds(start // SIDE, CHUNK // SIDE), :, :].reshape(CHUNK, C)
            bend = jnp.tanh(raw * (ROOT + (ROOT * CUBIC) * (raw * raw)))
            feature = (0.5 * raw * (1.0 + bend)).astype(BF)
            joined[step, rows, 0:C] = feature
            joined[step, rows, C : 2 * C] = hidden.astype(BF)
            both = joined[step, rows, :]
            update = 0.5 * jnp.tanh(0.5 * mm(both, update_ref[...])) + 0.5
            reset = 0.5 * jnp.tanh(0.5 * mm(both, reset_ref[...])) + 0.5
            gated = (reset * hidden).astype(BF)
            gated_all[step, rows, :] = gated
            candidate = jnp.tanh(
                mm(feature, candidate_ref[0:C, :]) + mm(gated, candidate_ref[C : 2 * C, :])
            )
            following = hidden + update * (candidate - hidden)
            saved.append((raw, bend, update, reset, candidate, hidden))
            hidden = following
        last_state[rows, :] = hidden.astype(BF)
        if start == 0:
            for load in loads[9:]:
                load.wait()
        carried = adjoint_ref[rows, :]
        for step in reversed(range(STEPS)):
            raw, bend, update, reset, candidate, hidden = saved[step]
            total = carried + mm_tn(grad_out_ref[step, :, rows], head_ref[...])
            keep = 1.0 - update
            scaled = total * update
            part_cand = (scaled * (1.0 - candidate * candidate)).astype(BF)
            part_update = (scaled * (candidate - hidden) * keep).astype(BF)
            grad_gated = mm_nt(part_cand, candidate_ref[C : 2 * C, :])
            part_reset = (grad_gated * hidden * reset * (1.0 - reset)).astype(BF)
            parts_t[step, 0:C, rows] = part_cand.T
            parts_t[step, C : 2 * C, rows] = part_update.T
            parts_t[step, 2 * C : 3 * C, rows] = part_reset.T
            carried = (
                total * keep
                + grad_gated * reset
                + mm_nt(part_update, update_ref[C : 2 * C, :])
                + mm_nt(part_reset, reset_ref[C : 2 * C, :])
            )
            grad_feature = (
                mm_nt(part_cand, candidate_ref[0:C, :])
                + mm_nt(part_update, update_ref[0:C, :])
                + mm_nt(part_reset, reset_ref[0:C, :])
            )
            slope = 0.5 * (1.0 + bend) + (0.5 * ROOT) * raw * (1.0 - bend * bend) * (
                1.0 + (3.0 * CUBIC) * (raw * raw)
            )
            grad_raw = (grad_feature * slope).astype(BF)
            part_conv[step, rows, :] = grad_raw
            part_conv_t[step, :, rows] = grad_raw.T
        grad_state[rows, :] = carried

    for index in range(CELLS // CHUNK):
        chunk(index * CHUNK)
    stores = [
        pltpu.make_async_copy(grad_state, grad_state_out, out_sems.at[16]),
        pltpu.make_async_copy(part_conv, part_conv_out, out_sems.at[17]),
    ]
    for store in stores:
        store.start()

    core = lax.axis_index("core")

    def share(block, value):
        shares[block] = value.reshape(16, 16, C)
        x_hi, y = block % 8 // 4, block % 4
        if block < 8:
            pieces = [(slice(0, 16), y, x_hi * 16)]
        else:
            pieces = [(slice(k * 8, k * 8 + 8), 2 * x_hi + k, y * 8) for k in range(2)]
        for lines, place, first in pieces:
            count = lines.stop - lines.start
            where = (place, pl.ds(first, count))
            sem = out_sems.at[block]
            kept = pltpu.make_async_copy(shares.at[block, lines], keep_out.at[where], sem)
            sent = pltpu.make_async_copy(shares.at[block, lines], send_out.at[where], sem)
            pl.when(core == block // 8)(kept.start)
            pl.when(core != block // 8)(sent.start)
            stores.append(kept)

    def over_steps(one):
        return one(0) + one(1)

    for gate in range(2):
        lanes = slice(C * (gate + 1), C * (gate + 2))
        grad = over_steps(lambda s: mm(parts_t[s, lanes, :], joined[s])).astype(BF)
        share(9 + 2 * gate, grad[:, :C])
        share(10 + 2 * gate, grad[:, C:])
    share(13, over_steps(lambda s: mm(parts_t[s, 0:C, :], joined[s, :, 0:C])).astype(BF))
    share(14, over_steps(lambda s: mm(parts_t[s, 0:C, :], gated_all[s])).astype(BF))
    grad_head = mm(grad_out_ref[0], joined[1, :, C : 2 * C]) + mm(grad_out_ref[1], last_state[...])
    grad_head = jnp.concatenate([grad_head, jnp.zeros((C - 8, C), F32)], axis=0)
    share(15, grad_head.T.astype(BF))
    for p in range(3):
        grad = over_steps(
            lambda s: mm(part_conv_t[s], windows[s, pl.ds(p * SIDE, CELLS), :])
        ).astype(BF)
        for q in range(3):
            share(3 * p + q, grad[:, q * C : (q + 1) * C].T)
    for store in stores:
        store.wait()


def outside_kernel(part_conv_ref, conv_ref, to_next_ref, to_prev_ref):
    lines = [[], [], [], []]
    for step in range(STEPS):
        plane = part_conv_ref.at[step]
        for side, line in enumerate((plane[0], plane[SIDE - 1], plane[:, 0], plane[:, SIDE - 1])):
            lines[side].append(line_shifts(line.astype(F32)))
    taps = ((2, 1, 0), (8, 7, 6), (6, 3, 0), (8, 5, 2))
    outside = []
    for side in range(4):
        line = jnp.concatenate(lines[side], axis=0)
        total = jnp.zeros((STEPS * SIDE, C), F32)
        for k, tap in enumerate(taps[side]):
            total = total + mm_nt(line[:, k * C : (k + 1) * C], conv_ref[pl.ds(tap * C, C), :])
        outside.append(total.astype(BF))
    for step in range(STEPS):
        rows = slice(step * SIDE, (step + 1) * SIDE)
        to_next_ref[step, 0] = outside[3][rows]
        to_prev_ref[step, 0] = outside[2][rows]
        for ref in (to_next_ref, to_prev_ref):
            ref[step, 1] = outside[0][rows]
            ref[step, 2] = outside[1][rows]


def fields_kernel(
    belt_ref,
    turns_ref,
    part_conv_ref,
    own_ref,
    prev_ref,
    next_ref,
    conv_ref,
    grad_fields_ref,
    shifted,
):
    zero = jnp.zeros((SIDE, C), F32)
    for step in range(STEPS):
        store_shifts(
            shifted,
            step,
            zero,
            zero,
            part_conv_ref[step].astype(F32).reshape(SIDE, SIDE, C),
            zero,
            zero,
        )
        seams = seam_rows(
            belt_ref,
            turns_ref,
            own_ref[step, 1],
            own_ref[step, 2],
            prev_ref[step],
            next_ref[step],
        )
        left = prev_ref[step, 0].astype(F32)
        right = next_ref[step, 0].astype(F32)
        for part in range(4):
            at = part * 8
            grad = jnp.zeros((8 * SIDE, C), F32)
            for p in range(3):
                for q in range(3):
                    lanes = slice((2 - q) * C, (3 - q) * C)
                    window = shifted[step, pl.ds((at + 2 - p) * SIDE, 8 * SIDE), lanes]
                    tap = 3 * p + q
                    grad = grad + mm_nt(window, conv_ref[tap * C : (tap + 1) * C, :])
            grad = grad.reshape(8, SIDE, C)
            col = iota((8, SIDE, C), 1)
            row = iota((8, SIDE, C), 0)
            grad = grad + jnp.where(col == 0, left[at : at + 8][:, None, :], 0.0)
            grad = grad + jnp.where(col == SIDE - 1, right[at : at + 8][:, None, :], 0.0)
            if part == 0:
                grad = grad + jnp.where(row == 0, seams[:SIDE][None], 0.0)
            if part == 3:
                grad = grad + jnp.where(row == 7, seams[SIDE:][None], 0.0)
            grad_fields_ref[step, at : at + 8] = grad.astype(BF)


def in_vmem():
    return pl.BlockSpec(memory_space=pltpu.VMEM)


def in_smem():
    return pl.BlockSpec(memory_space=pltpu.SMEM)


def params(mebibytes=60):
    return pltpu.CompilerParams(vmem_limit_bytes=mebibytes << 20)


def shape(dims, kind=BF):
    return jax.ShapeDtypeStruct(dims, kind)


EDGE = (STEPS, 3, SIDE, C)


def edges_call(fields):
    return pl.pallas_call(
        edges_kernel,
        out_shape=(shape(EDGE), shape(EDGE)),
        in_specs=[in_vmem()],
        out_specs=(in_vmem(), in_vmem()),
        compiler_params=params(8),
        name="edges",
    )(fields)


def early_call(fields, conv):
    anywhere = pl.BlockSpec(memory_space=pl.ANY)
    raw = (STEPS, CELLS, C)
    return pl.pallas_call(
        early_kernel,
        out_shape=shape(raw, F32),
        in_specs=[anywhere] * 2,
        out_specs=anywhere,
        scratch_shapes=[
            pltpu.VMEM(fields.shape, BF),
            pltpu.VMEM(conv.shape, BF),
            pltpu.VMEM((STEPS, CELLS + 2 * SIDE, 3 * C), BF),
            pltpu.VMEM(raw, F32),
            pltpu.SemaphoreType.DMA((7,)),
        ],
        compiler_params=params(),
        cost_estimate=pl.CostEstimate(
            flops=2 * STEPS * CELLS * C * C * 9, bytes_accessed=5 << 20, transcendentals=0
        ),
        name="early",
    )(fields, conv)


def main_call(*args):
    anywhere = pl.BlockSpec(memory_space=pl.ANY)
    return pl.pallas_call(
        main_kernel,
        out_shape=(
            shape((CELLS, C), F32),
            shape((STEPS, CELLS, C)),
            shape((4, 32, 16, C)),
            shape((4, 32, 16, C)),
        ),
        in_specs=[in_smem()] * 2 + [anywhere] * 12,
        out_specs=(anywhere,) * 4,
        scratch_shapes=[pltpu.VMEM(arg.shape, arg.dtype) for arg in args[2:]]
        + [
            pltpu.VMEM((STEPS, CELLS + 2 * SIDE, 3 * C), BF),
            pltpu.VMEM((STEPS, CELLS, 2 * C), BF),
            pltpu.VMEM((STEPS, CELLS, C), BF),
            pltpu.VMEM((STEPS, 3 * C, CELLS), BF),
            pltpu.VMEM((STEPS, CELLS, C), BF),
            pltpu.VMEM((STEPS, C, CELLS), BF),
            pltpu.VMEM((CELLS, C), BF),
            pltpu.VMEM((CELLS, C), F32),
            pltpu.VMEM((16, 16, 16, C), BF),
            pltpu.SemaphoreType.DMA((12,)),
            pltpu.SemaphoreType.DMA((18,)),
        ],
        compiler_params=params(),
        name="steps",
    )(*args)


def outside_call(part_conv, conv):
    return pl.pallas_call(
        outside_kernel,
        out_shape=(shape(EDGE), shape(EDGE)),
        in_specs=[in_vmem()] * 2,
        out_specs=(in_vmem(), in_vmem()),
        compiler_params=params(),
        cost_estimate=pl.CostEstimate(flops=1 << 30, bytes_accessed=3 << 20, transcendentals=0),
        name="outside",
    )(part_conv.reshape(STEPS, SIDE, SIDE, C), conv)


def pair_kernel(left_ref, right_ref, out_ref):
    out_ref[...] = (left_ref[...].astype(F32) + right_ref[...].astype(F32)).astype(BF)


def pair_call(left, right):
    return pl.pallas_call(
        pair_kernel,
        out_shape=shape(left.shape),
        in_specs=[in_vmem()] * 2,
        out_specs=in_vmem(),
        compiler_params=params(8),
        name="pair",
    )(left, right)


def added_kernel(pieces_ref, out_ref):
    total = pieces_ref[0].astype(F32)
    for k in range(1, pieces_ref.shape[0]):
        total = total + pieces_ref[k].astype(F32)
    out_ref[...] = total.astype(BF)


def added_call(pieces):
    return pl.pallas_call(
        added_kernel,
        out_shape=shape((32, 16, C)),
        in_specs=[in_vmem()],
        out_specs=in_vmem(),
        compiler_params=params(8),
        name="added",
    )(pieces)


def fields_call(*args):
    return pl.pallas_call(
        fields_kernel,
        out_shape=shape((STEPS, SIDE, SIDE, C)),
        in_specs=[in_smem()] * 2 + [in_vmem()] * 5,
        out_specs=in_vmem(),
        scratch_shapes=[pltpu.VMEM((STEPS, CELLS + 2 * SIDE, 3 * C), BF)],
        compiler_params=params(20),
        cost_estimate=pl.CostEstimate(
            flops=2 * STEPS * CELLS * C * C * 9, bytes_accessed=4 << 20, transcendentals=0
        ),
        name="fields",
    )(*args)


RING = [(i, (i + 1) % 16) for i in range(16)]
BACK = [((i + 1) % 16, i) for i in range(16)]


def finish_kernel(whole_ref, conv_ref, update_ref, reset_ref, candidate_ref, head_ref):
    def block(k):
        return whole_ref[((k // 4) % 2) * 8 + (k % 4) * 2 + k // 8].astype(F32)

    for tap in range(9):
        conv_ref[tap] = block(tap)
    for ref, first in ((update_ref, 9), (reset_ref, 11), (candidate_ref, 13)):
        ref[:, 0:C] = block(first)
        ref[:, C : 2 * C] = block(first + 1)
    head_ref[...] = block(15).T[:8]


def finish_call(whole):
    gate = shape((16, 2 * C), F32)
    return pl.pallas_call(
        finish_kernel,
        out_shape=(shape((9, 16, C), F32), gate, gate, gate, shape((8, 16), F32)),
        in_specs=[in_vmem()],
        out_specs=tuple([in_vmem()] * 5),
        compiler_params=params(8),
        name="finish",
    )(whole)


def added(pieces):
    total = pieces[0].astype(F32)
    for k in range(1, pieces.shape[0]):
        total = total + pieces[k].astype(F32)
    return total


EVERY = ("x_hi", "y", "core", "x_lo", "z")


def groups_of(*axes_of_core):
    devices = np.arange(256).reshape(2, 4, 2, 2, 8)
    found = []
    for core, axes in enumerate(axes_of_core):
        inner = [("x_hi", "y", "x_lo", "z").index(axis) for axis in axes]
        outer = [axis for axis in range(4) if axis not in inner]
        here = devices[:, :, core].transpose(outer + inner)
        size = math.prod(here.shape[len(outer) :])
        found += here.reshape(-1, size).tolist()
    return found


FIRST = groups_of(("y",), ("x_hi", "x_lo"))
SECOND = groups_of(("x_hi", "x_lo", "z"), ("y", "z"))


def body(
    fields_in,
    state_start,
    state_adjoint,
    output_grad,
    conv_weight,
    w_update,
    w_reset,
    w_candidate,
    head_weight,
    neighbor_tile,
    seam_turns,
):
    dp = ("x_hi", "y", "core")
    belt = ("x_lo", "z")
    seams = (neighbor_tile.T, seam_turns.T)
    fields = fields_in[0, 0]
    conv = conv_weight.reshape(9 * C, C)
    to_next, to_prev = edges_call(fields)
    prev = lax.ppermute(to_next, belt, RING)
    following = lax.ppermute(to_prev, belt, BACK)
    raw = early_call(fields, conv).reshape(STEPS, SIDE, SIDE, C)
    grad_state, part_conv, keep, send = main_call(
        *seams,
        fields,
        prev,
        following,
        conv,
        raw,
        state_start.reshape(CELLS, C),
        w_update,
        w_reset,
        w_candidate,
        state_adjoint.reshape(CELLS, C),
        output_grad[0, 0],
        head_weight,
    )
    got = lax.ppermute(send, "core", [(0, 1), (1, 0)])
    out_next, out_prev = outside_call(part_conv, conv)
    got, out_next, out_prev = lax.optimization_barrier((got, out_next, out_prev))
    held = pair_call(keep, got)
    held = lax.all_to_all(held, EVERY, 0, 0, axis_index_groups=FIRST, tiled=True)
    prev = lax.ppermute(out_next, belt, RING)
    following = lax.ppermute(out_prev, belt, BACK)
    held, prev, following = lax.optimization_barrier((held, prev, following))
    held = added_call(held)
    grad_fields = fields_call(*seams, part_conv, out_next, prev, following, conv)
    held = lax.all_to_all(held, EVERY, 0, 0, axis_index_groups=SECOND, tiled=True)
    held = added(held).astype(BF)
    held, grad_fields = lax.optimization_barrier((held, grad_fields))
    whole = jnp.broadcast_to(held[None], (16, 16, C))
    whole = lax.all_to_all(whole, dp, 0, 0, tiled=True)
    grad_conv, grad_update, grad_reset, grad_candidate, grad_head = finish_call(whole)
    return (
        grad_fields[None, None],
        grad_state.reshape(1, 1, SIDE, SIDE, C),
        grad_conv,
        grad_update.T,
        grad_reset.T,
        grad_candidate.T,
        grad_head,
    )


def solution(mesh):
    cube = Mesh(mesh.devices.reshape(2, 4, 2, 2, 8), ("x_hi", "y", "core", "x_lo", "z"))
    dp = ("x_hi", "y", "core")
    tile = ("x_lo", "z")
    return jax.shard_map(
        body,
        mesh=cube,
        in_specs=(
            P(dp, tile, None, None, None, None),
            P(dp, tile, None, None, None),
            P(dp, tile, None, None, None),
            P(dp, tile, None, None, None),
            P(),
            P(),
            P(),
            P(),
            P(),
            P(),
            P(),
        ),
        out_specs=(
            P(dp, tile, None, None, None, None),
            P(dp, tile, None, None, None),
            P(None, tile, None),
            P(None, tile),
            P(None, tile),
            P(None, tile),
            P(None, tile),
        ),
        check_vma=False,
    )
```

```python
import math

import jax
import jax.numpy as jnp
import numpy as np
from jax import lax
from jax.experimental import pallas as pl
from jax.experimental.pallas import tpu as pltpu
from jax.sharding import Mesh
from jax.sharding import PartitionSpec as P

CUBIC = 0.044715
ROOT = math.sqrt(2.0 / math.pi)
BF = jnp.bfloat16
F32 = jnp.float32
SIDE = 32
CELLS = SIDE * SIDE
C = 256
STEPS = 2
CHUNK = 512


def mm(a, b):
    return lax.dot_general(a, b, (((1,), (0,)), ((), ())), preferred_element_type=F32)


def mm_nt(a, b):
    return lax.dot_general(a, b, (((1,), (1,)), ((), ())), preferred_element_type=F32)


def mm_tn(a, b):
    return lax.dot_general(a, b, (((0,), (0,)), ((), ())), preferred_element_type=F32)


def one_hot(cond):
    return jnp.where(cond, 1.0, 0.0).astype(BF)


def iota(shape, dim):
    return lax.broadcasted_iota(jnp.int32, shape, dim)


def edges_kernel(fields_ref, to_next_ref, to_prev_ref):
    for step in range(STEPS):
        to_next_ref[step, 0] = fields_ref[step, :, SIDE - 1, :]
        to_prev_ref[step, 0] = fields_ref[step, :, 0, :]
        for ref in (to_next_ref, to_prev_ref):
            ref[step, 1] = fields_ref[step, 0]
            ref[step, 2] = fields_ref[step, SIDE - 1]


def seam_of(belt_ref, turns_ref, side):
    tile = lax.axis_index(("x_lo", "z"))
    partner = belt_ref[side, tile]
    other = lax.rem(side + 2 - turns_ref[side, tile], 4)
    before = lax.rem(tile + 15, 16)
    place = jnp.where(partner == tile, 0, jnp.where(partner == before, 1, 2))
    base = (2 * place + jnp.where(other == 2, 1, 0)) * SIDE
    flip = other == side
    return jnp.where(flip, base + SIDE - 1, base), jnp.where(flip, -1, 1)


def seam_rows(belt_ref, turns_ref, own_top, own_bottom, from_prev, from_next):
    stacked = jnp.concatenate(
        [own_top, own_bottom, from_prev[1], from_prev[2], from_next[1], from_next[2]], axis=0
    )
    rows = iota((2 * SIDE, 6 * SIDE), 0)
    cols = iota((2 * SIDE, 6 * SIDE), 1)
    top_base, top_sign = seam_of(belt_ref, turns_ref, 0)
    bottom_base, bottom_sign = seam_of(belt_ref, turns_ref, 2)
    wanted = jnp.where(
        rows < SIDE, top_base + top_sign * rows, bottom_base + bottom_sign * (rows - SIDE)
    )
    return mm(one_hot(cols == wanted), stacked)


def line_shifts(line):
    at = iota((SIDE, C), 0)
    before = jnp.where(at == 0, 0.0, pltpu.roll(line, 1, axis=0))
    after = jnp.where(at == SIDE - 1, 0.0, pltpu.roll(line, SIDE - 1, axis=0))
    return jnp.concatenate([before, line, after], axis=1).astype(BF)


def store_shifts(ref, step, low, high, middle, left, right):
    col = iota((SIDE, SIDE, C), 1)
    before = jnp.where(col == 0, left[:, None, :], pltpu.roll(middle, 1, axis=1))
    after = jnp.where(col == SIDE - 1, right[:, None, :], pltpu.roll(middle, SIDE - 1, axis=1))
    body = pl.ds(SIDE, CELLS)
    ref[step, body, 0:C] = before.reshape(CELLS, C).astype(BF)
    ref[step, body, C : 2 * C] = middle.reshape(CELLS, C).astype(BF)
    ref[step, body, 2 * C : 3 * C] = after.reshape(CELLS, C).astype(BF)
    ref[step, pl.ds(0, SIDE), :] = line_shifts(low)
    ref[step, pl.ds(SIDE + CELLS, SIDE), :] = line_shifts(high)


def early_kernel(fields_in, conv_in, raw_out, fields_ref, conv_ref, windows, raw_ref, sems):
    loads = [
        pltpu.make_async_copy(fields_in.at[0], fields_ref.at[0], sems.at[0]),
        pltpu.make_async_copy(fields_in.at[1], fields_ref.at[1], sems.at[1]),
        pltpu.make_async_copy(conv_in, conv_ref, sems.at[2]),
    ]
    for load in loads:
        load.start()
    zero = jnp.zeros((SIDE, C), F32)
    stores = []
    loads[0].wait()
    store_shifts(windows, 0, zero, zero, fields_ref[0].astype(F32), zero, zero)
    loads[1].wait()
    loads[2].wait()
    for step in range(STEPS):
        if step == 0:
            store_shifts(windows, 1, zero, zero, fields_ref[1].astype(F32), zero, zero)
        for start in range(0, CELLS, CHUNK):
            raw = jnp.zeros((CHUNK, C), F32)
            for p in range(3):
                window = windows[step, pl.ds(start + p * SIDE, CHUNK), :]
                raw = raw + mm(window, conv_ref[pl.ds(3 * C * p, 3 * C), :])
            rows = pl.ds(start, CHUNK)
            raw_ref[step, rows, :] = raw
            at = (step, rows)
            sem = sems.at[3 + step * (CELLS // CHUNK) + start // CHUNK]
            stores.append(pltpu.make_async_copy(raw_ref.at[at], raw_out.at[at], sem))
            stores[-1].start()
    for store in stores:
        store.wait()


def main_kernel(
    belt_ref,
    turns_ref,
    *refs,
):
    sources, refs = refs[:12], refs[12:]
    grad_state_out, part_conv_out, keep_out, send_out = refs[:4]
    held, refs = refs[4:16], refs[16:]
    (
        windows,
        joined,
        gated_all,
        parts_t,
        part_conv,
        part_conv_t,
        last_state,
        grad_state,
        shares,
        in_sems,
        out_sems,
    ) = refs
    loads = [
        pltpu.make_async_copy(source, target, in_sems.at[k])
        for k, (source, target) in enumerate(zip(sources, held))
    ]
    for load in loads[:9]:
        load.start()
    (
        fields_ref,
        prev_ref,
        next_ref,
        conv_ref,
        raw_ref,
        state_ref,
        update_ref,
        reset_ref,
        candidate_ref,
        adjoint_ref,
        grad_out_ref,
        head_ref,
    ) = held
    for load in loads[:3]:
        load.wait()
    tops, bottoms, lefts, rights = [], [], [], []
    for step in range(STEPS):
        seams = seam_rows(
            belt_ref,
            turns_ref,
            fields_ref[step, 0],
            fields_ref[step, SIDE - 1],
            prev_ref[step],
            next_ref[step],
        )
        left = prev_ref[step, 0].astype(F32)
        right = next_ref[step, 0].astype(F32)
        store_shifts(
            windows,
            step,
            seams[:SIDE],
            seams[SIDE:],
            fields_ref[step].astype(F32),
            left,
            right,
        )
        tops.append(line_shifts(seams[:SIDE]))
        bottoms.append(line_shifts(seams[SIDE:]))
        lefts.append(line_shifts(left))
        rights.append(line_shifts(right))
    for load in loads[3:5]:
        load.wait()

    def taps_of(lines, taps):
        lines = jnp.concatenate(lines, axis=0)
        total = jnp.zeros((STEPS * SIDE, C), F32)
        for k, tap in enumerate(taps):
            total = total + mm(lines[:, k * C : (k + 1) * C], conv_ref[pl.ds(tap * C, C), :])
        return total

    top = taps_of(tops, (0, 1, 2))
    bottom = taps_of(bottoms, (6, 7, 8))
    left = taps_of(lefts, (0, 3, 6))
    right = taps_of(rights, (2, 5, 8))
    place = iota((SIDE, 8, C), 1)
    for step in range(STEPS):
        lines = slice(step * SIDE, (step + 1) * SIDE)
        raw_ref[step, 0, :, :] += top[lines]
        raw_ref[step, SIDE - 1, :, :] += bottom[lines]
        raw_ref[step, :, 0:8, :] += jnp.where(place == 0, left[lines][:, None, :], 0.0)
        raw_ref[step, :, SIDE - 8 : SIDE, :] += jnp.where(place == 7, right[lines][:, None, :], 0.0)
    for load in loads[5:9]:
        load.wait()
    for load in loads[9:]:
        load.start()

    def chunk(start):
        rows = pl.ds(start, CHUNK)
        hidden = state_ref[rows, :]
        saved = []
        for step in range(STEPS):
            raw = raw_ref[step, pl.ds(start // SIDE, CHUNK // SIDE), :, :].reshape(CHUNK, C)
            bend = jnp.tanh(raw * (ROOT + (ROOT * CUBIC) * (raw * raw)))
            feature = (0.5 * raw * (1.0 + bend)).astype(BF)
            joined[step, rows, 0:C] = feature
            joined[step, rows, C : 2 * C] = hidden.astype(BF)
            both = joined[step, rows, :]
            update = 0.5 * jnp.tanh(0.5 * mm(both, update_ref[...])) + 0.5
            reset = 0.5 * jnp.tanh(0.5 * mm(both, reset_ref[...])) + 0.5
            gated = (reset * hidden).astype(BF)
            gated_all[step, rows, :] = gated
            candidate = jnp.tanh(
                mm(feature, candidate_ref[0:C, :]) + mm(gated, candidate_ref[C : 2 * C, :])
            )
            following = hidden + update * (candidate - hidden)
            saved.append((raw, bend, update, reset, candidate, hidden))
            hidden = following
        last_state[rows, :] = hidden.astype(BF)
        if start == 0:
            for load in loads[9:]:
                load.wait()
        carried = adjoint_ref[rows, :]
        for step in reversed(range(STEPS)):
            raw, bend, update, reset, candidate, hidden = saved[step]
            total = carried + mm_tn(grad_out_ref[step, :, rows], head_ref[...])
            keep = 1.0 - update
            scaled = total * update
            part_cand = (scaled * (1.0 - candidate * candidate)).astype(BF)
            part_update = (scaled * (candidate - hidden) * keep).astype(BF)
            grad_gated = mm_nt(part_cand, candidate_ref[C : 2 * C, :])
            part_reset = (grad_gated * hidden * reset * (1.0 - reset)).astype(BF)
            parts_t[step, 0:C, rows] = part_cand.T
            parts_t[step, C : 2 * C, rows] = part_update.T
            parts_t[step, 2 * C : 3 * C, rows] = part_reset.T
            carried = (
                total * keep
                + grad_gated * reset
                + mm_nt(part_update, update_ref[C : 2 * C, :])
                + mm_nt(part_reset, reset_ref[C : 2 * C, :])
            )
            grad_feature = (
                mm_nt(part_cand, candidate_ref[0:C, :])
                + mm_nt(part_update, update_ref[0:C, :])
                + mm_nt(part_reset, reset_ref[0:C, :])
            )
            slope = 0.5 * (1.0 + bend) + (0.5 * ROOT) * raw * (1.0 - bend * bend) * (
                1.0 + (3.0 * CUBIC) * (raw * raw)
            )
            grad_raw = (grad_feature * slope).astype(BF)
            part_conv[step, rows, :] = grad_raw
            part_conv_t[step, :, rows] = grad_raw.T
        grad_state[rows, :] = carried

    for index in range(CELLS // CHUNK):
        chunk(index * CHUNK)
    stores = [
        pltpu.make_async_copy(grad_state, grad_state_out, out_sems.at[16]),
        pltpu.make_async_copy(part_conv, part_conv_out, out_sems.at[17]),
    ]
    for store in stores:
        store.start()

    core = lax.axis_index("core")

    def share(block, value):
        shares[block] = value.reshape(16, 16, C)
        x_hi, y = block % 8 // 4, block % 4
        if block < 8:
            pieces = [(slice(0, 16), y, x_hi * 16)]
        else:
            pieces = [(slice(k * 8, k * 8 + 8), 2 * x_hi + k, y * 8) for k in range(2)]
        for lines, place, first in pieces:
            count = lines.stop - lines.start
            where = (place, pl.ds(first, count))
            sem = out_sems.at[block]
            kept = pltpu.make_async_copy(shares.at[block, lines], keep_out.at[where], sem)
            sent = pltpu.make_async_copy(shares.at[block, lines], send_out.at[where], sem)
            pl.when(core == block // 8)(kept.start)
            pl.when(core != block // 8)(sent.start)
            stores.append(kept)

    def over_steps(one):
        return one(0) + one(1)

    for gate in range(2):
        lanes = slice(C * (gate + 1), C * (gate + 2))
        grad = over_steps(lambda s: mm(parts_t[s, lanes, :], joined[s])).astype(BF)
        share(9 + 2 * gate, grad[:, :C])
        share(10 + 2 * gate, grad[:, C:])
    share(13, over_steps(lambda s: mm(parts_t[s, 0:C, :], joined[s, :, 0:C])).astype(BF))
    share(14, over_steps(lambda s: mm(parts_t[s, 0:C, :], gated_all[s])).astype(BF))
    grad_head = mm(grad_out_ref[0], joined[1, :, C : 2 * C]) + mm(grad_out_ref[1], last_state[...])
    grad_head = jnp.concatenate([grad_head, jnp.zeros((C - 8, C), F32)], axis=0)
    share(15, grad_head.T.astype(BF))
    for p in range(3):
        grad = over_steps(
            lambda s: mm(part_conv_t[s], windows[s, pl.ds(p * SIDE, CELLS), :])
        ).astype(BF)
        for q in range(3):
            share(3 * p + q, grad[:, q * C : (q + 1) * C].T)
    for store in stores:
        store.wait()


def outside_kernel(part_conv_ref, conv_ref, to_next_ref, to_prev_ref):
    lines = [[], [], [], []]
    for step in range(STEPS):
        plane = part_conv_ref.at[step]
        for side, line in enumerate((plane[0], plane[SIDE - 1], plane[:, 0], plane[:, SIDE - 1])):
            lines[side].append(line_shifts(line.astype(F32)))
    taps = ((2, 1, 0), (8, 7, 6), (6, 3, 0), (8, 5, 2))
    outside = []
    for side in range(4):
        line = jnp.concatenate(lines[side], axis=0)
        total = jnp.zeros((STEPS * SIDE, C), F32)
        for k, tap in enumerate(taps[side]):
            total = total + mm_nt(line[:, k * C : (k + 1) * C], conv_ref[pl.ds(tap * C, C), :])
        outside.append(total.astype(BF))
    for step in range(STEPS):
        rows = slice(step * SIDE, (step + 1) * SIDE)
        to_next_ref[step, 0] = outside[3][rows]
        to_prev_ref[step, 0] = outside[2][rows]
        for ref in (to_next_ref, to_prev_ref):
            ref[step, 1] = outside[0][rows]
            ref[step, 2] = outside[1][rows]


def fields_kernel(
    belt_ref,
    turns_ref,
    part_conv_ref,
    own_ref,
    prev_ref,
    next_ref,
    conv_ref,
    grad_fields_ref,
    shifted,
):
    zero = jnp.zeros((SIDE, C), F32)
    for step in range(STEPS):
        store_shifts(
            shifted,
            step,
            zero,
            zero,
            part_conv_ref[step].astype(F32).reshape(SIDE, SIDE, C),
            zero,
            zero,
        )
        seams = seam_rows(
            belt_ref,
            turns_ref,
            own_ref[step, 1],
            own_ref[step, 2],
            prev_ref[step],
            next_ref[step],
        )
        left = prev_ref[step, 0].astype(F32)
        right = next_ref[step, 0].astype(F32)
        for part in range(4):
            at = part * 8
            grad = jnp.zeros((8 * SIDE, C), F32)
            for p in range(3):
                for q in range(3):
                    lanes = slice((2 - q) * C, (3 - q) * C)
                    window = shifted[step, pl.ds((at + 2 - p) * SIDE, 8 * SIDE), lanes]
                    tap = 3 * p + q
                    grad = grad + mm_nt(window, conv_ref[tap * C : (tap + 1) * C, :])
            grad = grad.reshape(8, SIDE, C)
            col = iota((8, SIDE, C), 1)
            row = iota((8, SIDE, C), 0)
            grad = grad + jnp.where(col == 0, left[at : at + 8][:, None, :], 0.0)
            grad = grad + jnp.where(col == SIDE - 1, right[at : at + 8][:, None, :], 0.0)
            if part == 0:
                grad = grad + jnp.where(row == 0, seams[:SIDE][None], 0.0)
            if part == 3:
                grad = grad + jnp.where(row == 7, seams[SIDE:][None], 0.0)
            grad_fields_ref[step, at : at + 8] = grad.astype(BF)


def in_vmem():
    return pl.BlockSpec(memory_space=pltpu.VMEM)


def in_smem():
    return pl.BlockSpec(memory_space=pltpu.SMEM)


def params(mebibytes=60):
    return pltpu.CompilerParams(vmem_limit_bytes=mebibytes << 20)


def shape(dims, kind=BF):
    return jax.ShapeDtypeStruct(dims, kind)


EDGE = (STEPS, 3, SIDE, C)


def edges_call(fields):
    return pl.pallas_call(
        edges_kernel,
        out_shape=(shape(EDGE), shape(EDGE)),
        in_specs=[in_vmem()],
        out_specs=(in_vmem(), in_vmem()),
        compiler_params=params(8),
        name="edges",
    )(fields)


def early_call(fields, conv):
    anywhere = pl.BlockSpec(memory_space=pl.ANY)
    raw = (STEPS, CELLS, C)
    return pl.pallas_call(
        early_kernel,
        out_shape=shape(raw, F32),
        in_specs=[anywhere] * 2,
        out_specs=anywhere,
        scratch_shapes=[
            pltpu.VMEM(fields.shape, BF),
            pltpu.VMEM(conv.shape, BF),
            pltpu.VMEM((STEPS, CELLS + 2 * SIDE, 3 * C), BF),
            pltpu.VMEM(raw, F32),
            pltpu.SemaphoreType.DMA((7,)),
        ],
        compiler_params=params(),
        cost_estimate=pl.CostEstimate(
            flops=2 * STEPS * CELLS * C * C * 9, bytes_accessed=5 << 20, transcendentals=0
        ),
        name="early",
    )(fields, conv)


def main_call(*args):
    anywhere = pl.BlockSpec(memory_space=pl.ANY)
    return pl.pallas_call(
        main_kernel,
        out_shape=(
            shape((CELLS, C), F32),
            shape((STEPS, CELLS, C)),
            shape((4, 32, 16, C)),
            shape((4, 32, 16, C)),
        ),
        in_specs=[in_smem()] * 2 + [anywhere] * 12,
        out_specs=(anywhere,) * 4,
        scratch_shapes=[pltpu.VMEM(arg.shape, arg.dtype) for arg in args[2:]]
        + [
            pltpu.VMEM((STEPS, CELLS + 2 * SIDE, 3 * C), BF),
            pltpu.VMEM((STEPS, CELLS, 2 * C), BF),
            pltpu.VMEM((STEPS, CELLS, C), BF),
            pltpu.VMEM((STEPS, 3 * C, CELLS), BF),
            pltpu.VMEM((STEPS, CELLS, C), BF),
            pltpu.VMEM((STEPS, C, CELLS), BF),
            pltpu.VMEM((CELLS, C), BF),
            pltpu.VMEM((CELLS, C), F32),
            pltpu.VMEM((16, 16, 16, C), BF),
            pltpu.SemaphoreType.DMA((12,)),
            pltpu.SemaphoreType.DMA((18,)),
        ],
        compiler_params=params(),
        name="steps",
    )(*args)


def outside_call(part_conv, conv):
    return pl.pallas_call(
        outside_kernel,
        out_shape=(shape(EDGE), shape(EDGE)),
        in_specs=[in_vmem()] * 2,
        out_specs=(in_vmem(), in_vmem()),
        compiler_params=params(),
        cost_estimate=pl.CostEstimate(flops=1 << 30, bytes_accessed=3 << 20, transcendentals=0),
        name="outside",
    )(part_conv.reshape(STEPS, SIDE, SIDE, C), conv)


def pair_kernel(left_ref, right_ref, out, out_ref, sems):
    stores = []
    for k in range(left_ref.shape[0]):
        out_ref[k] = (left_ref[k].astype(F32) + right_ref[k].astype(F32)).astype(BF)
        stores.append(pltpu.make_async_copy(out_ref.at[k], out.at[k], sems.at[k]))
        stores[k].start()
    for store in stores:
        store.wait()


def pair_call(left, right):
    return pl.pallas_call(
        pair_kernel,
        out_shape=shape(left.shape),
        in_specs=[in_vmem()] * 2,
        out_specs=pl.BlockSpec(memory_space=pl.ANY),
        scratch_shapes=[
            pltpu.VMEM(left.shape, BF),
            pltpu.SemaphoreType.DMA((left.shape[0],)),
        ],
        compiler_params=params(8),
        name="pair",
    )(left, right)


def added_kernel(pieces_ref, out_ref):
    total = pieces_ref[0].astype(F32)
    for k in range(1, pieces_ref.shape[0]):
        total = total + pieces_ref[k].astype(F32)
    out_ref[...] = total.astype(BF)


def added_call(pieces):
    return pl.pallas_call(
        added_kernel,
        out_shape=shape((32, 16, C)),
        in_specs=[in_vmem()],
        out_specs=in_vmem(),
        compiler_params=params(8),
        name="added",
    )(pieces)


def fields_call(*args):
    return pl.pallas_call(
        fields_kernel,
        out_shape=shape((STEPS, SIDE, SIDE, C)),
        in_specs=[in_smem()] * 2 + [in_vmem()] * 5,
        out_specs=in_vmem(),
        scratch_shapes=[pltpu.VMEM((STEPS, CELLS + 2 * SIDE, 3 * C), BF)],
        compiler_params=params(20),
        cost_estimate=pl.CostEstimate(
            flops=2 * STEPS * CELLS * C * C * 9, bytes_accessed=4 << 20, transcendentals=0
        ),
        name="fields",
    )(*args)


RING = [(i, (i + 1) % 16) for i in range(16)]
BACK = [((i + 1) % 16, i) for i in range(16)]


def finish_kernel(whole_ref, conv_ref, update_ref, reset_ref, candidate_ref, head_ref):
    def block(k):
        return whole_ref[((k // 4) % 2) * 8 + (k % 4) * 2 + k // 8].astype(F32)

    for tap in range(9):
        conv_ref[tap] = block(tap)
    for ref, first in ((update_ref, 9), (reset_ref, 11), (candidate_ref, 13)):
        ref[:, 0:C] = block(first)
        ref[:, C : 2 * C] = block(first + 1)
    head_ref[...] = block(15).T[:8]


def finish_call(whole):
    gate = shape((16, 2 * C), F32)
    return pl.pallas_call(
        finish_kernel,
        out_shape=(shape((9, 16, C), F32), gate, gate, gate, shape((8, 16), F32)),
        in_specs=[in_vmem()],
        out_specs=tuple([in_vmem()] * 5),
        compiler_params=params(8),
        name="finish",
    )(whole)


def added(pieces):
    total = pieces[0].astype(F32)
    for k in range(1, pieces.shape[0]):
        total = total + pieces[k].astype(F32)
    return total


EVERY = ("x_hi", "y", "core", "x_lo", "z")


def groups_of(*axes_of_core):
    devices = np.arange(256).reshape(2, 4, 2, 2, 8)
    found = []
    for core, axes in enumerate(axes_of_core):
        inner = [("x_hi", "y", "x_lo", "z").index(axis) for axis in axes]
        outer = [axis for axis in range(4) if axis not in inner]
        here = devices[:, :, core].transpose(outer + inner)
        size = math.prod(here.shape[len(outer) :])
        found += here.reshape(-1, size).tolist()
    return found


FIRST = groups_of(("y",), ("x_hi", "x_lo"))
SECOND = groups_of(("x_hi", "x_lo", "z"), ("y", "z"))


def body(
    fields_in,
    state_start,
    state_adjoint,
    output_grad,
    conv_weight,
    w_update,
    w_reset,
    w_candidate,
    head_weight,
    neighbor_tile,
    seam_turns,
):
    dp = ("x_hi", "y", "core")
    belt = ("x_lo", "z")
    seams = (neighbor_tile.T, seam_turns.T)
    fields = fields_in[0, 0]
    conv = conv_weight.reshape(9 * C, C)
    to_next, to_prev = edges_call(fields)
    prev = lax.ppermute(to_next, belt, RING)
    following = lax.ppermute(to_prev, belt, BACK)
    raw = early_call(fields, conv).reshape(STEPS, SIDE, SIDE, C)
    grad_state, part_conv, keep, send = main_call(
        *seams,
        fields,
        prev,
        following,
        conv,
        raw,
        state_start.reshape(CELLS, C),
        w_update,
        w_reset,
        w_candidate,
        state_adjoint.reshape(CELLS, C),
        output_grad[0, 0],
        head_weight,
    )
    got = lax.ppermute(send, "core", [(0, 1), (1, 0)])
    out_next, out_prev = outside_call(part_conv, conv)
    got, out_next, out_prev = lax.optimization_barrier((got, out_next, out_prev))
    held = pair_call(keep, got)
    held = lax.all_to_all(held, EVERY, 0, 0, axis_index_groups=FIRST, tiled=True)
    prev = lax.ppermute(out_next, belt, RING)
    following = lax.ppermute(out_prev, belt, BACK)
    held, prev, following = lax.optimization_barrier((held, prev, following))
    held = added_call(held)
    held = lax.all_to_all(held, EVERY, 0, 0, axis_index_groups=SECOND, tiled=True)
    held, prev, following = lax.optimization_barrier((held, prev, following))
    held = added(held).astype(BF)
    grad_fields = fields_call(*seams, part_conv, out_next, prev, following, conv)
    whole = jnp.broadcast_to(held[None], (16, 16, C))
    whole = lax.all_to_all(whole, dp, 0, 0, tiled=True)
    whole, grad_fields = lax.optimization_barrier((whole, grad_fields))
    grad_conv, grad_update, grad_reset, grad_candidate, grad_head = finish_call(whole)
    return (
        grad_fields[None, None],
        grad_state.reshape(1, 1, SIDE, SIDE, C),
        grad_conv,
        grad_update.T,
        grad_reset.T,
        grad_candidate.T,
        grad_head,
    )


def solution(mesh):
    cube = Mesh(mesh.devices.reshape(2, 4, 2, 2, 8), ("x_hi", "y", "core", "x_lo", "z"))
    dp = ("x_hi", "y", "core")
    tile = ("x_lo", "z")
    return jax.shard_map(
        body,
        mesh=cube,
        in_specs=(
            P(dp, tile, None, None, None, None),
            P(dp, tile, None, None, None),
            P(dp, tile, None, None, None),
            P(dp, tile, None, None, None),
            P(),
            P(),
            P(),
            P(),
            P(),
            P(),
            P(),
        ),
        out_specs=(
            P(dp, tile, None, None, None, None),
            P(dp, tile, None, None, None),
            P(None, tile, None),
            P(None, tile),
            P(None, tile),
            P(None, tile),
            P(None, tile),
        ),
        check_vma=False,
    )
```

```python
import math

import jax
import jax.numpy as jnp
import numpy as np
from jax import lax
from jax.experimental import pallas as pl
from jax.experimental.pallas import tpu as pltpu
from jax.sharding import Mesh
from jax.sharding import PartitionSpec as P

CUBIC = 0.044715
ROOT = math.sqrt(2.0 / math.pi)
BF = jnp.bfloat16
F32 = jnp.float32
SIDE = 32
CELLS = SIDE * SIDE
C = 256
STEPS = 2
CHUNK = 512


def mm(a, b):
    return lax.dot_general(a, b, (((1,), (0,)), ((), ())), preferred_element_type=F32)


def mm_nt(a, b):
    return lax.dot_general(a, b, (((1,), (1,)), ((), ())), preferred_element_type=F32)


def mm_tn(a, b):
    return lax.dot_general(a, b, (((0,), (0,)), ((), ())), preferred_element_type=F32)


def one_hot(cond):
    return jnp.where(cond, 1.0, 0.0).astype(BF)


def iota(shape, dim):
    return lax.broadcasted_iota(jnp.int32, shape, dim)


def edges_kernel(fields_ref, to_next_ref, to_prev_ref):
    for step in range(STEPS):
        to_next_ref[step, 0] = fields_ref[step, :, SIDE - 1, :]
        to_prev_ref[step, 0] = fields_ref[step, :, 0, :]
        for ref in (to_next_ref, to_prev_ref):
            ref[step, 1] = fields_ref[step, 0]
            ref[step, 2] = fields_ref[step, SIDE - 1]


def seam_of(belt_ref, turns_ref, side):
    tile = lax.axis_index(("x_lo", "z"))
    partner = belt_ref[side, tile]
    other = lax.rem(side + 2 - turns_ref[side, tile], 4)
    before = lax.rem(tile + 15, 16)
    place = jnp.where(partner == tile, 0, jnp.where(partner == before, 1, 2))
    base = (2 * place + jnp.where(other == 2, 1, 0)) * SIDE
    flip = other == side
    return jnp.where(flip, base + SIDE - 1, base), jnp.where(flip, -1, 1)


def seam_rows(belt_ref, turns_ref, own_top, own_bottom, from_prev, from_next):
    stacked = jnp.concatenate(
        [own_top, own_bottom, from_prev[1], from_prev[2], from_next[1], from_next[2]], axis=0
    )
    rows = iota((2 * SIDE, 6 * SIDE), 0)
    cols = iota((2 * SIDE, 6 * SIDE), 1)
    top_base, top_sign = seam_of(belt_ref, turns_ref, 0)
    bottom_base, bottom_sign = seam_of(belt_ref, turns_ref, 2)
    wanted = jnp.where(
        rows < SIDE, top_base + top_sign * rows, bottom_base + bottom_sign * (rows - SIDE)
    )
    return mm(one_hot(cols == wanted), stacked)


def line_shifts(line):
    at = iota((SIDE, C), 0)
    before = jnp.where(at == 0, 0.0, pltpu.roll(line, 1, axis=0))
    after = jnp.where(at == SIDE - 1, 0.0, pltpu.roll(line, SIDE - 1, axis=0))
    return jnp.concatenate([before, line, after], axis=1).astype(BF)


def store_shifts(ref, step, low, high, middle, left, right):
    col = iota((SIDE, SIDE, C), 1)
    before = jnp.where(col == 0, left[:, None, :], pltpu.roll(middle, 1, axis=1))
    after = jnp.where(col == SIDE - 1, right[:, None, :], pltpu.roll(middle, SIDE - 1, axis=1))
    body = pl.ds(SIDE, CELLS)
    ref[step, body, 0:C] = before.reshape(CELLS, C).astype(BF)
    ref[step, body, C : 2 * C] = middle.reshape(CELLS, C).astype(BF)
    ref[step, body, 2 * C : 3 * C] = after.reshape(CELLS, C).astype(BF)
    ref[step, pl.ds(0, SIDE), :] = line_shifts(low)
    ref[step, pl.ds(SIDE + CELLS, SIDE), :] = line_shifts(high)


def early_kernel(fields_in, conv_in, raw_out, fields_ref, conv_ref, windows, raw_ref, sems):
    loads = [
        pltpu.make_async_copy(fields_in.at[0], fields_ref.at[0], sems.at[0]),
        pltpu.make_async_copy(fields_in.at[1], fields_ref.at[1], sems.at[1]),
        pltpu.make_async_copy(conv_in, conv_ref, sems.at[2]),
    ]
    for load in loads:
        load.start()
    zero = jnp.zeros((SIDE, C), F32)
    stores = []
    loads[0].wait()
    store_shifts(windows, 0, zero, zero, fields_ref[0].astype(F32), zero, zero)
    loads[1].wait()
    loads[2].wait()
    for step in range(STEPS):
        if step == 0:
            store_shifts(windows, 1, zero, zero, fields_ref[1].astype(F32), zero, zero)
        for start in range(0, CELLS, CHUNK):
            raw = jnp.zeros((CHUNK, C), F32)
            for p in range(3):
                window = windows[step, pl.ds(start + p * SIDE, CHUNK), :]
                raw = raw + mm(window, conv_ref[pl.ds(3 * C * p, 3 * C), :])
            rows = pl.ds(start, CHUNK)
            raw_ref[step, rows, :] = raw
            at = (step, rows)
            sem = sems.at[3 + step * (CELLS // CHUNK) + start // CHUNK]
            stores.append(pltpu.make_async_copy(raw_ref.at[at], raw_out.at[at], sem))
            stores[-1].start()
    for store in stores:
        store.wait()


def main_kernel(
    belt_ref,
    turns_ref,
    *refs,
):
    sources, refs = refs[:12], refs[12:]
    grad_state_out, part_conv_out, keep_out, send_out = refs[:4]
    held, refs = refs[4:16], refs[16:]
    (
        windows,
        joined,
        gated_all,
        parts_t,
        part_conv,
        part_conv_t,
        last_state,
        grad_state,
        shares,
        in_sems,
        out_sems,
    ) = refs
    loads = [
        pltpu.make_async_copy(source, target, in_sems.at[k])
        for k, (source, target) in enumerate(zip(sources, held))
    ]
    for load in loads[:9]:
        load.start()
    (
        fields_ref,
        prev_ref,
        next_ref,
        conv_ref,
        raw_ref,
        state_ref,
        update_ref,
        reset_ref,
        candidate_ref,
        adjoint_ref,
        grad_out_ref,
        head_ref,
    ) = held
    for load in loads[:3]:
        load.wait()
    tops, bottoms, lefts, rights = [], [], [], []
    for step in range(STEPS):
        seams = seam_rows(
            belt_ref,
            turns_ref,
            fields_ref[step, 0],
            fields_ref[step, SIDE - 1],
            prev_ref[step],
            next_ref[step],
        )
        left = prev_ref[step, 0].astype(F32)
        right = next_ref[step, 0].astype(F32)
        store_shifts(
            windows,
            step,
            seams[:SIDE],
            seams[SIDE:],
            fields_ref[step].astype(F32),
            left,
            right,
        )
        tops.append(line_shifts(seams[:SIDE]))
        bottoms.append(line_shifts(seams[SIDE:]))
        lefts.append(line_shifts(left))
        rights.append(line_shifts(right))
    for load in loads[3:5]:
        load.wait()

    def taps_of(lines, taps):
        lines = jnp.concatenate(lines, axis=0)
        total = jnp.zeros((STEPS * SIDE, C), F32)
        for k, tap in enumerate(taps):
            total = total + mm(lines[:, k * C : (k + 1) * C], conv_ref[pl.ds(tap * C, C), :])
        return total

    top = taps_of(tops, (0, 1, 2))
    bottom = taps_of(bottoms, (6, 7, 8))
    left = taps_of(lefts, (0, 3, 6))
    right = taps_of(rights, (2, 5, 8))
    place = iota((SIDE, 8, C), 1)
    for step in range(STEPS):
        lines = slice(step * SIDE, (step + 1) * SIDE)
        raw_ref[step, 0, :, :] += top[lines]
        raw_ref[step, SIDE - 1, :, :] += bottom[lines]
        raw_ref[step, :, 0:8, :] += jnp.where(place == 0, left[lines][:, None, :], 0.0)
        raw_ref[step, :, SIDE - 8 : SIDE, :] += jnp.where(place == 7, right[lines][:, None, :], 0.0)
    for load in loads[5:9]:
        load.wait()
    for load in loads[9:]:
        load.start()

    def chunk(start):
        rows = pl.ds(start, CHUNK)
        hidden = state_ref[rows, :]
        saved = []
        for step in range(STEPS):
            raw = raw_ref[step, pl.ds(start // SIDE, CHUNK // SIDE), :, :].reshape(CHUNK, C)
            bend = jnp.tanh(raw * (ROOT + (ROOT * CUBIC) * (raw * raw)))
            feature = (0.5 * raw * (1.0 + bend)).astype(BF)
            joined[step, rows, 0:C] = feature
            joined[step, rows, C : 2 * C] = hidden.astype(BF)
            both = joined[step, rows, :]
            update = 0.5 * jnp.tanh(0.5 * mm(both, update_ref[...])) + 0.5
            reset = 0.5 * jnp.tanh(0.5 * mm(both, reset_ref[...])) + 0.5
            gated = (reset * hidden).astype(BF)
            gated_all[step, rows, :] = gated
            candidate = jnp.tanh(
                mm(feature, candidate_ref[0:C, :]) + mm(gated, candidate_ref[C : 2 * C, :])
            )
            following = hidden + update * (candidate - hidden)
            saved.append((raw, bend, update, reset, candidate, hidden))
            hidden = following
        last_state[rows, :] = hidden.astype(BF)
        if start == 0:
            for load in loads[9:]:
                load.wait()
        carried = adjoint_ref[rows, :]
        for step in reversed(range(STEPS)):
            raw, bend, update, reset, candidate, hidden = saved[step]
            total = carried + mm_tn(grad_out_ref[step, :, rows], head_ref[...])
            keep = 1.0 - update
            scaled = total * update
            part_cand = (scaled * (1.0 - candidate * candidate)).astype(BF)
            part_update = (scaled * (candidate - hidden) * keep).astype(BF)
            grad_gated = mm_nt(part_cand, candidate_ref[C : 2 * C, :])
            part_reset = (grad_gated * hidden * reset * (1.0 - reset)).astype(BF)
            parts_t[step, 0:C, rows] = part_cand.T
            parts_t[step, C : 2 * C, rows] = part_update.T
            parts_t[step, 2 * C : 3 * C, rows] = part_reset.T
            carried = (
                total * keep
                + grad_gated * reset
                + mm_nt(part_update, update_ref[C : 2 * C, :])
                + mm_nt(part_reset, reset_ref[C : 2 * C, :])
            )
            grad_feature = (
                mm_nt(part_cand, candidate_ref[0:C, :])
                + mm_nt(part_update, update_ref[0:C, :])
                + mm_nt(part_reset, reset_ref[0:C, :])
            )
            slope = 0.5 * (1.0 + bend) + (0.5 * ROOT) * raw * (1.0 - bend * bend) * (
                1.0 + (3.0 * CUBIC) * (raw * raw)
            )
            grad_raw = (grad_feature * slope).astype(BF)
            part_conv[step, rows, :] = grad_raw
            part_conv_t[step, :, rows] = grad_raw.T
        grad_state[rows, :] = carried

    for index in range(CELLS // CHUNK):
        chunk(index * CHUNK)
    stores = [
        pltpu.make_async_copy(grad_state, grad_state_out, out_sems.at[16]),
        pltpu.make_async_copy(part_conv, part_conv_out, out_sems.at[17]),
    ]
    for store in stores:
        store.start()

    core = lax.axis_index("core")

    def share(block, value):
        shares[block] = value.reshape(16, 16, C)
        x_hi, y = block % 8 // 4, block % 4
        if block < 8:
            pieces = [(slice(0, 16), y, x_hi * 16)]
        else:
            pieces = [(slice(k * 8, k * 8 + 8), 2 * x_hi + k, y * 8) for k in range(2)]
        for lines, place, first in pieces:
            count = lines.stop - lines.start
            where = (place, pl.ds(first, count))
            sem = out_sems.at[block]
            kept = pltpu.make_async_copy(shares.at[block, lines], keep_out.at[where], sem)
            sent = pltpu.make_async_copy(shares.at[block, lines], send_out.at[where], sem)
            pl.when(core == block // 8)(kept.start)
            pl.when(core != block // 8)(sent.start)
            stores.append(kept)

    def over_steps(one):
        return one(0) + one(1)

    for gate in range(2):
        lanes = slice(C * (gate + 1), C * (gate + 2))
        grad = over_steps(lambda s: mm(parts_t[s, lanes, :], joined[s])).astype(BF)
        share(9 + 2 * gate, grad[:, :C])
        share(10 + 2 * gate, grad[:, C:])
    share(13, over_steps(lambda s: mm(parts_t[s, 0:C, :], joined[s, :, 0:C])).astype(BF))
    share(14, over_steps(lambda s: mm(parts_t[s, 0:C, :], gated_all[s])).astype(BF))
    grad_head = mm(grad_out_ref[0], joined[1, :, C : 2 * C]) + mm(grad_out_ref[1], last_state[...])
    grad_head = jnp.concatenate([grad_head, jnp.zeros((C - 8, C), F32)], axis=0)
    share(15, grad_head.T.astype(BF))
    for p in range(3):
        grad = over_steps(
            lambda s: mm(part_conv_t[s], windows[s, pl.ds(p * SIDE, CELLS), :])
        ).astype(BF)
        for q in range(3):
            share(3 * p + q, grad[:, q * C : (q + 1) * C].T)
    for store in stores:
        store.wait()


def outside_kernel(part_conv_ref, conv_ref, to_next_ref, to_prev_ref):
    lines = [[], [], [], []]
    for step in range(STEPS):
        plane = part_conv_ref.at[step]
        for side, line in enumerate((plane[0], plane[SIDE - 1], plane[:, 0], plane[:, SIDE - 1])):
            lines[side].append(line_shifts(line.astype(F32)))
    taps = ((2, 1, 0), (8, 7, 6), (6, 3, 0), (8, 5, 2))
    outside = []
    for side in range(4):
        line = jnp.concatenate(lines[side], axis=0)
        total = jnp.zeros((STEPS * SIDE, C), F32)
        for k, tap in enumerate(taps[side]):
            total = total + mm_nt(line[:, k * C : (k + 1) * C], conv_ref[pl.ds(tap * C, C), :])
        outside.append(total.astype(BF))
    for step in range(STEPS):
        rows = slice(step * SIDE, (step + 1) * SIDE)
        to_next_ref[step, 0] = outside[3][rows]
        to_prev_ref[step, 0] = outside[2][rows]
        for ref in (to_next_ref, to_prev_ref):
            ref[step, 1] = outside[0][rows]
            ref[step, 2] = outside[1][rows]


def fields_kernel(
    belt_ref,
    turns_ref,
    part_conv_ref,
    own_ref,
    prev_ref,
    next_ref,
    conv_ref,
    grad_fields_ref,
    shifted,
):
    zero = jnp.zeros((SIDE, C), F32)
    for step in range(STEPS):
        store_shifts(
            shifted,
            step,
            zero,
            zero,
            part_conv_ref[step].astype(F32).reshape(SIDE, SIDE, C),
            zero,
            zero,
        )
        seams = seam_rows(
            belt_ref,
            turns_ref,
            own_ref[step, 1],
            own_ref[step, 2],
            prev_ref[step],
            next_ref[step],
        )
        left = prev_ref[step, 0].astype(F32)
        right = next_ref[step, 0].astype(F32)
        for part in range(4):
            at = part * 8
            grad = jnp.zeros((8 * SIDE, C), F32)
            for p in range(3):
                for q in range(3):
                    lanes = slice((2 - q) * C, (3 - q) * C)
                    window = shifted[step, pl.ds((at + 2 - p) * SIDE, 8 * SIDE), lanes]
                    tap = 3 * p + q
                    grad = grad + mm_nt(window, conv_ref[tap * C : (tap + 1) * C, :])
            grad = grad.reshape(8, SIDE, C)
            col = iota((8, SIDE, C), 1)
            row = iota((8, SIDE, C), 0)
            grad = grad + jnp.where(col == 0, left[at : at + 8][:, None, :], 0.0)
            grad = grad + jnp.where(col == SIDE - 1, right[at : at + 8][:, None, :], 0.0)
            if part == 0:
                grad = grad + jnp.where(row == 0, seams[:SIDE][None], 0.0)
            if part == 3:
                grad = grad + jnp.where(row == 7, seams[SIDE:][None], 0.0)
            grad_fields_ref[step, at : at + 8] = grad.astype(BF)


def in_vmem():
    return pl.BlockSpec(memory_space=pltpu.VMEM)


def in_smem():
    return pl.BlockSpec(memory_space=pltpu.SMEM)


def params(mebibytes=60):
    return pltpu.CompilerParams(vmem_limit_bytes=mebibytes << 20)


def shape(dims, kind=BF):
    return jax.ShapeDtypeStruct(dims, kind)


EDGE = (STEPS, 3, SIDE, C)


def edges_call(fields):
    return pl.pallas_call(
        edges_kernel,
        out_shape=(shape(EDGE), shape(EDGE)),
        in_specs=[in_vmem()],
        out_specs=(in_vmem(), in_vmem()),
        compiler_params=params(8),
        name="edges",
    )(fields)


def early_call(fields, conv):
    anywhere = pl.BlockSpec(memory_space=pl.ANY)
    raw = (STEPS, CELLS, C)
    return pl.pallas_call(
        early_kernel,
        out_shape=shape(raw, F32),
        in_specs=[anywhere] * 2,
        out_specs=anywhere,
        scratch_shapes=[
            pltpu.VMEM(fields.shape, BF),
            pltpu.VMEM(conv.shape, BF),
            pltpu.VMEM((STEPS, CELLS + 2 * SIDE, 3 * C), BF),
            pltpu.VMEM(raw, F32),
            pltpu.SemaphoreType.DMA((7,)),
        ],
        compiler_params=params(),
        cost_estimate=pl.CostEstimate(
            flops=2 * STEPS * CELLS * C * C * 9, bytes_accessed=5 << 20, transcendentals=0
        ),
        name="early",
    )(fields, conv)


def main_call(*args):
    anywhere = pl.BlockSpec(memory_space=pl.ANY)
    return pl.pallas_call(
        main_kernel,
        out_shape=(
            shape((CELLS, C), F32),
            shape((STEPS, CELLS, C)),
            shape((4, 32, 16, C)),
            shape((4, 32, 16, C)),
        ),
        in_specs=[in_smem()] * 2 + [anywhere] * 12,
        out_specs=(anywhere,) * 4,
        scratch_shapes=[pltpu.VMEM(arg.shape, arg.dtype) for arg in args[2:]]
        + [
            pltpu.VMEM((STEPS, CELLS + 2 * SIDE, 3 * C), BF),
            pltpu.VMEM((STEPS, CELLS, 2 * C), BF),
            pltpu.VMEM((STEPS, CELLS, C), BF),
            pltpu.VMEM((STEPS, 3 * C, CELLS), BF),
            pltpu.VMEM((STEPS, CELLS, C), BF),
            pltpu.VMEM((STEPS, C, CELLS), BF),
            pltpu.VMEM((CELLS, C), BF),
            pltpu.VMEM((CELLS, C), F32),
            pltpu.VMEM((16, 16, 16, C), BF),
            pltpu.SemaphoreType.DMA((12,)),
            pltpu.SemaphoreType.DMA((18,)),
        ],
        compiler_params=params(),
        name="steps",
    )(*args)


def outside_call(part_conv, conv):
    return pl.pallas_call(
        outside_kernel,
        out_shape=(shape(EDGE), shape(EDGE)),
        in_specs=[in_vmem()] * 2,
        out_specs=(in_vmem(), in_vmem()),
        compiler_params=params(),
        cost_estimate=pl.CostEstimate(flops=1 << 30, bytes_accessed=3 << 20, transcendentals=0),
        name="outside",
    )(part_conv.reshape(STEPS, SIDE, SIDE, C), conv)


def pair_kernel(left_ref, right_ref, out, out_ref, sems):
    stores = []
    for k in range(left_ref.shape[0]):
        out_ref[k] = (left_ref[k].astype(F32) + right_ref[k].astype(F32)).astype(BF)
        stores.append(pltpu.make_async_copy(out_ref.at[k], out.at[k], sems.at[k]))
        stores[k].start()
    for store in stores:
        store.wait()


def pair_call(left, right):
    return pl.pallas_call(
        pair_kernel,
        out_shape=shape(left.shape),
        in_specs=[in_vmem()] * 2,
        out_specs=pl.BlockSpec(memory_space=pl.ANY),
        scratch_shapes=[
            pltpu.VMEM(left.shape, BF),
            pltpu.SemaphoreType.DMA((left.shape[0],)),
        ],
        compiler_params=params(8),
        name="pair",
    )(left, right)


def added_kernel(pieces_ref, out, out_ref, sems):
    stores = []
    for k in range(4):
        rows = pl.ds(8 * k, 8)
        total = pieces_ref[0, rows].astype(F32)
        for piece in range(1, pieces_ref.shape[0]):
            total = total + pieces_ref[piece, rows].astype(F32)
        out_ref[rows] = total.astype(BF)
        stores.append(pltpu.make_async_copy(out_ref.at[rows], out.at[rows], sems.at[k]))
        stores[k].start()
    for store in stores:
        store.wait()


def added_call(pieces):
    return pl.pallas_call(
        added_kernel,
        out_shape=shape(pieces.shape[1:]),
        in_specs=[in_vmem()],
        out_specs=pl.BlockSpec(memory_space=pl.ANY),
        scratch_shapes=[pltpu.VMEM(pieces.shape[1:], BF), pltpu.SemaphoreType.DMA((4,))],
        compiler_params=params(8),
        name="added",
    )(pieces)


def fields_call(*args):
    return pl.pallas_call(
        fields_kernel,
        out_shape=shape((STEPS, SIDE, SIDE, C)),
        in_specs=[in_smem()] * 2 + [in_vmem()] * 5,
        out_specs=in_vmem(),
        scratch_shapes=[pltpu.VMEM((STEPS, CELLS + 2 * SIDE, 3 * C), BF)],
        compiler_params=params(20),
        cost_estimate=pl.CostEstimate(
            flops=2 * STEPS * CELLS * C * C * 9, bytes_accessed=4 << 20, transcendentals=0
        ),
        name="fields",
    )(*args)


RING = [(i, (i + 1) % 16) for i in range(16)]
BACK = [((i + 1) % 16, i) for i in range(16)]


def finish_kernel(whole_ref, conv_ref, update_ref, reset_ref, candidate_ref, head_ref):
    def block(k):
        return whole_ref[((k // 4) % 2) * 8 + (k % 4) * 2 + k // 8].astype(F32)

    for tap in range(9):
        conv_ref[tap] = block(tap)
    for ref, first in ((update_ref, 9), (reset_ref, 11), (candidate_ref, 13)):
        ref[:, 0:C] = block(first)
        ref[:, C : 2 * C] = block(first + 1)
    head_ref[...] = block(15).T[:8]


def finish_call(whole):
    gate = shape((16, 2 * C), F32)
    return pl.pallas_call(
        finish_kernel,
        out_shape=(shape((9, 16, C), F32), gate, gate, gate, shape((8, 16), F32)),
        in_specs=[in_vmem()],
        out_specs=tuple([in_vmem()] * 5),
        compiler_params=params(8),
        name="finish",
    )(whole)


def added(pieces):
    total = pieces[0].astype(F32)
    for k in range(1, pieces.shape[0]):
        total = total + pieces[k].astype(F32)
    return total


EVERY = ("x_hi", "y", "core", "x_lo", "z")


def groups_of(*axes_of_core):
    devices = np.arange(256).reshape(2, 4, 2, 2, 8)
    found = []
    for core, axes in enumerate(axes_of_core):
        inner = [("x_hi", "y", "x_lo", "z").index(axis) for axis in axes]
        outer = [axis for axis in range(4) if axis not in inner]
        here = devices[:, :, core].transpose(outer + inner)
        size = math.prod(here.shape[len(outer) :])
        found += here.reshape(-1, size).tolist()
    return found


FIRST = groups_of(("y",), ("x_hi", "x_lo"))
SECOND = groups_of(("x_hi", "x_lo", "z"), ("y", "z"))


def body(
    fields_in,
    state_start,
    state_adjoint,
    output_grad,
    conv_weight,
    w_update,
    w_reset,
    w_candidate,
    head_weight,
    neighbor_tile,
    seam_turns,
):
    dp = ("x_hi", "y", "core")
    belt = ("x_lo", "z")
    seams = (neighbor_tile.T, seam_turns.T)
    fields = fields_in[0, 0]
    conv = conv_weight.reshape(9 * C, C)
    to_next, to_prev = edges_call(fields)
    prev = lax.ppermute(to_next, belt, RING)
    following = lax.ppermute(to_prev, belt, BACK)
    raw = early_call(fields, conv).reshape(STEPS, SIDE, SIDE, C)
    grad_state, part_conv, keep, send = main_call(
        *seams,
        fields,
        prev,
        following,
        conv,
        raw,
        state_start.reshape(CELLS, C),
        w_update,
        w_reset,
        w_candidate,
        state_adjoint.reshape(CELLS, C),
        output_grad[0, 0],
        head_weight,
    )
    got = lax.ppermute(send, "core", [(0, 1), (1, 0)])
    out_next, out_prev = outside_call(part_conv, conv)
    got, out_next, out_prev = lax.optimization_barrier((got, out_next, out_prev))
    held = pair_call(keep, got)
    held = lax.all_to_all(held, EVERY, 0, 0, axis_index_groups=FIRST, tiled=True)
    prev = lax.ppermute(out_next, belt, RING)
    following = lax.ppermute(out_prev, belt, BACK)
    held, prev, following = lax.optimization_barrier((held, prev, following))
    held = added_call(held)
    grad_fields = fields_call(*seams, part_conv, out_next, prev, following, conv)
    held = lax.all_to_all(held, EVERY, 0, 0, axis_index_groups=SECOND, tiled=True)
    held = added(held).astype(BF)
    held, grad_fields = lax.optimization_barrier((held, grad_fields))
    whole = jnp.broadcast_to(held[None], (16, 16, C))
    whole = lax.all_to_all(whole, dp, 0, 0, tiled=True)
    grad_conv, grad_update, grad_reset, grad_candidate, grad_head = finish_call(whole)
    return (
        grad_fields[None, None],
        grad_state.reshape(1, 1, SIDE, SIDE, C),
        grad_conv,
        grad_update.T,
        grad_reset.T,
        grad_candidate.T,
        grad_head,
    )


def solution(mesh):
    cube = Mesh(mesh.devices.reshape(2, 4, 2, 2, 8), ("x_hi", "y", "core", "x_lo", "z"))
    dp = ("x_hi", "y", "core")
    tile = ("x_lo", "z")
    return jax.shard_map(
        body,
        mesh=cube,
        in_specs=(
            P(dp, tile, None, None, None, None),
            P(dp, tile, None, None, None),
            P(dp, tile, None, None, None),
            P(dp, tile, None, None, None),
            P(),
            P(),
            P(),
            P(),
            P(),
            P(),
            P(),
        ),
        out_specs=(
            P(dp, tile, None, None, None, None),
            P(dp, tile, None, None, None),
            P(None, tile, None),
            P(None, tile),
            P(None, tile),
            P(None, tile),
            P(None, tile),
        ),
        check_vma=False,
    )
```

```python
import math

import jax
import jax.numpy as jnp
import numpy as np
from jax import lax
from jax.experimental import pallas as pl
from jax.experimental.pallas import tpu as pltpu
from jax.sharding import Mesh
from jax.sharding import PartitionSpec as P

CUBIC = 0.044715
ROOT = math.sqrt(2.0 / math.pi)
BF = jnp.bfloat16
F32 = jnp.float32
SIDE = 32
CELLS = SIDE * SIDE
C = 256
STEPS = 2
CHUNK = 512


def mm(a, b):
    return lax.dot_general(a, b, (((1,), (0,)), ((), ())), preferred_element_type=F32)


def mm_nt(a, b):
    return lax.dot_general(a, b, (((1,), (1,)), ((), ())), preferred_element_type=F32)


def mm_tn(a, b):
    return lax.dot_general(a, b, (((0,), (0,)), ((), ())), preferred_element_type=F32)


def one_hot(cond):
    return jnp.where(cond, 1.0, 0.0).astype(BF)


def iota(shape, dim):
    return lax.broadcasted_iota(jnp.int32, shape, dim)


def edges_kernel(fields_ref, to_next_ref, to_prev_ref):
    for step in range(STEPS):
        to_next_ref[step, 0] = fields_ref[step, :, SIDE - 1, :]
        to_prev_ref[step, 0] = fields_ref[step, :, 0, :]
        for ref in (to_next_ref, to_prev_ref):
            ref[step, 1] = fields_ref[step, 0]
            ref[step, 2] = fields_ref[step, SIDE - 1]


def seam_of(belt_ref, turns_ref, side):
    tile = lax.axis_index(("x_lo", "z"))
    partner = belt_ref[side, tile]
    other = lax.rem(side + 2 - turns_ref[side, tile], 4)
    before = lax.rem(tile + 15, 16)
    place = jnp.where(partner == tile, 0, jnp.where(partner == before, 1, 2))
    base = (2 * place + jnp.where(other == 2, 1, 0)) * SIDE
    flip = other == side
    return jnp.where(flip, base + SIDE - 1, base), jnp.where(flip, -1, 1)


def seam_rows(belt_ref, turns_ref, own_top, own_bottom, from_prev, from_next):
    stacked = jnp.concatenate(
        [own_top, own_bottom, from_prev[1], from_prev[2], from_next[1], from_next[2]], axis=0
    )
    rows = iota((2 * SIDE, 6 * SIDE), 0)
    cols = iota((2 * SIDE, 6 * SIDE), 1)
    top_base, top_sign = seam_of(belt_ref, turns_ref, 0)
    bottom_base, bottom_sign = seam_of(belt_ref, turns_ref, 2)
    wanted = jnp.where(
        rows < SIDE, top_base + top_sign * rows, bottom_base + bottom_sign * (rows - SIDE)
    )
    return mm(one_hot(cols == wanted), stacked)


def line_shifts(line):
    at = iota((SIDE, C), 0)
    before = jnp.where(at == 0, 0.0, pltpu.roll(line, 1, axis=0))
    after = jnp.where(at == SIDE - 1, 0.0, pltpu.roll(line, SIDE - 1, axis=0))
    return jnp.concatenate([before, line, after], axis=1).astype(BF)


def store_shifts(ref, step, low, high, middle, left, right):
    col = iota((SIDE, SIDE, C), 1)
    before = jnp.where(col == 0, left[:, None, :], pltpu.roll(middle, 1, axis=1))
    after = jnp.where(col == SIDE - 1, right[:, None, :], pltpu.roll(middle, SIDE - 1, axis=1))
    body = pl.ds(SIDE, CELLS)
    ref[step, body, 0:C] = before.reshape(CELLS, C).astype(BF)
    ref[step, body, C : 2 * C] = middle.reshape(CELLS, C).astype(BF)
    ref[step, body, 2 * C : 3 * C] = after.reshape(CELLS, C).astype(BF)
    ref[step, pl.ds(0, SIDE), :] = line_shifts(low)
    ref[step, pl.ds(SIDE + CELLS, SIDE), :] = line_shifts(high)


def early_kernel(fields_in, conv_in, raw_out, fields_ref, conv_ref, windows, raw_ref, sems):
    loads = [
        pltpu.make_async_copy(fields_in.at[0], fields_ref.at[0], sems.at[0]),
        pltpu.make_async_copy(fields_in.at[1], fields_ref.at[1], sems.at[1]),
        pltpu.make_async_copy(conv_in, conv_ref, sems.at[2]),
    ]
    for load in loads:
        load.start()
    zero = jnp.zeros((SIDE, C), F32)
    stores = []
    loads[0].wait()
    store_shifts(windows, 0, zero, zero, fields_ref[0].astype(F32), zero, zero)
    loads[1].wait()
    loads[2].wait()
    for step in range(STEPS):
        if step == 0:
            store_shifts(windows, 1, zero, zero, fields_ref[1].astype(F32), zero, zero)
        for start in range(0, CELLS, CHUNK):
            raw = jnp.zeros((CHUNK, C), F32)
            for p in range(3):
                window = windows[step, pl.ds(start + p * SIDE, CHUNK), :]
                raw = raw + mm(window, conv_ref[pl.ds(3 * C * p, 3 * C), :])
            rows = pl.ds(start, CHUNK)
            raw_ref[step, rows, :] = raw
            at = (step, rows)
            sem = sems.at[3 + step * (CELLS // CHUNK) + start // CHUNK]
            stores.append(pltpu.make_async_copy(raw_ref.at[at], raw_out.at[at], sem))
            stores[-1].start()
    for store in stores:
        store.wait()


def main_kernel(
    belt_ref,
    turns_ref,
    *refs,
):
    sources, refs = refs[:12], refs[12:]
    grad_state_out, part_conv_out, keep_out, send_out = refs[:4]
    held, refs = refs[4:16], refs[16:]
    (
        windows,
        joined,
        gated_all,
        parts_t,
        part_conv,
        part_conv_t,
        last_state,
        grad_state,
        shares,
        in_sems,
        out_sems,
    ) = refs
    loads = [
        pltpu.make_async_copy(source, target, in_sems.at[k])
        for k, (source, target) in enumerate(zip(sources, held))
    ]
    for load in loads[:9]:
        load.start()
    (
        fields_ref,
        prev_ref,
        next_ref,
        conv_ref,
        raw_ref,
        state_ref,
        update_ref,
        reset_ref,
        candidate_ref,
        adjoint_ref,
        grad_out_ref,
        head_ref,
    ) = held
    for load in loads[:3]:
        load.wait()
    tops, bottoms, lefts, rights = [], [], [], []
    for step in range(STEPS):
        seams = seam_rows(
            belt_ref,
            turns_ref,
            fields_ref[step, 0],
            fields_ref[step, SIDE - 1],
            prev_ref[step],
            next_ref[step],
        )
        left = prev_ref[step, 0].astype(F32)
        right = next_ref[step, 0].astype(F32)
        store_shifts(
            windows,
            step,
            seams[:SIDE],
            seams[SIDE:],
            fields_ref[step].astype(F32),
            left,
            right,
        )
        tops.append(line_shifts(seams[:SIDE]))
        bottoms.append(line_shifts(seams[SIDE:]))
        lefts.append(line_shifts(left))
        rights.append(line_shifts(right))
    for load in loads[3:5]:
        load.wait()

    def taps_of(lines, taps):
        lines = jnp.concatenate(lines, axis=0)
        total = jnp.zeros((STEPS * SIDE, C), F32)
        for k, tap in enumerate(taps):
            total = total + mm(lines[:, k * C : (k + 1) * C], conv_ref[pl.ds(tap * C, C), :])
        return total

    top = taps_of(tops, (0, 1, 2))
    bottom = taps_of(bottoms, (6, 7, 8))
    left = taps_of(lefts, (0, 3, 6))
    right = taps_of(rights, (2, 5, 8))
    place = iota((SIDE, 8, C), 1)
    for step in range(STEPS):
        lines = slice(step * SIDE, (step + 1) * SIDE)
        raw_ref[step, 0, :, :] += top[lines]
        raw_ref[step, SIDE - 1, :, :] += bottom[lines]
        raw_ref[step, :, 0:8, :] += jnp.where(place == 0, left[lines][:, None, :], 0.0)
        raw_ref[step, :, SIDE - 8 : SIDE, :] += jnp.where(place == 7, right[lines][:, None, :], 0.0)
    for load in loads[5:9]:
        load.wait()
    for load in loads[9:]:
        load.start()

    def chunk(start):
        rows = pl.ds(start, CHUNK)
        hidden = state_ref[rows, :]
        saved = []
        for step in range(STEPS):
            raw = raw_ref[step, pl.ds(start // SIDE, CHUNK // SIDE), :, :].reshape(CHUNK, C)
            bend = jnp.tanh(raw * (ROOT + (ROOT * CUBIC) * (raw * raw)))
            feature = (0.5 * raw * (1.0 + bend)).astype(BF)
            joined[step, rows, 0:C] = feature
            joined[step, rows, C : 2 * C] = hidden.astype(BF)
            both = joined[step, rows, :]
            update = 0.5 * jnp.tanh(0.5 * mm(both, update_ref[...])) + 0.5
            reset = 0.5 * jnp.tanh(0.5 * mm(both, reset_ref[...])) + 0.5
            gated = (reset * hidden).astype(BF)
            gated_all[step, rows, :] = gated
            candidate = jnp.tanh(
                mm(feature, candidate_ref[0:C, :]) + mm(gated, candidate_ref[C : 2 * C, :])
            )
            following = hidden + update * (candidate - hidden)
            saved.append((raw, bend, update, reset, candidate, hidden))
            hidden = following
        last_state[rows, :] = hidden.astype(BF)
        if start == 0:
            for load in loads[9:]:
                load.wait()
        carried = adjoint_ref[rows, :]
        for step in reversed(range(STEPS)):
            raw, bend, update, reset, candidate, hidden = saved[step]
            total = carried + mm_tn(grad_out_ref[step, :, rows], head_ref[...])
            keep = 1.0 - update
            scaled = total * update
            part_cand = (scaled * (1.0 - candidate * candidate)).astype(BF)
            part_update = (scaled * (candidate - hidden) * keep).astype(BF)
            grad_gated = mm_nt(part_cand, candidate_ref[C : 2 * C, :])
            part_reset = (grad_gated * hidden * reset * (1.0 - reset)).astype(BF)
            parts_t[step, 0:C, rows] = part_cand.T
            parts_t[step, C : 2 * C, rows] = part_update.T
            parts_t[step, 2 * C : 3 * C, rows] = part_reset.T
            carried = (
                total * keep
                + grad_gated * reset
                + mm_nt(part_update, update_ref[C : 2 * C, :])
                + mm_nt(part_reset, reset_ref[C : 2 * C, :])
            )
            grad_feature = (
                mm_nt(part_cand, candidate_ref[0:C, :])
                + mm_nt(part_update, update_ref[0:C, :])
                + mm_nt(part_reset, reset_ref[0:C, :])
            )
            slope = 0.5 * (1.0 + bend) + (0.5 * ROOT) * raw * (1.0 - bend * bend) * (
                1.0 + (3.0 * CUBIC) * (raw * raw)
            )
            grad_raw = (grad_feature * slope).astype(BF)
            part_conv[step, rows, :] = grad_raw
            part_conv_t[step, :, rows] = grad_raw.T
        grad_state[rows, :] = carried

    for index in range(CELLS // CHUNK):
        chunk(index * CHUNK)
    stores = [
        pltpu.make_async_copy(grad_state, grad_state_out, out_sems.at[16]),
        pltpu.make_async_copy(part_conv, part_conv_out, out_sems.at[17]),
    ]
    for store in stores:
        store.start()

    core = lax.axis_index("core")

    def share(block, value):
        shares[block] = value.reshape(16, 16, C)
        x_hi, y = block % 8 // 4, block % 4
        if block < 8:
            pieces = [(slice(0, 16), y, x_hi * 16)]
        else:
            pieces = [(slice(k * 8, k * 8 + 8), 2 * x_hi + k, y * 8) for k in range(2)]
        for lines, place, first in pieces:
            count = lines.stop - lines.start
            where = (place, pl.ds(first, count))
            sem = out_sems.at[block]
            kept = pltpu.make_async_copy(shares.at[block, lines], keep_out.at[where], sem)
            sent = pltpu.make_async_copy(shares.at[block, lines], send_out.at[where], sem)
            pl.when(core == block // 8)(kept.start)
            pl.when(core != block // 8)(sent.start)
            stores.append(kept)

    def over_steps(one):
        return one(0) + one(1)

    for gate in range(2):
        lanes = slice(C * (gate + 1), C * (gate + 2))
        grad = over_steps(lambda s: mm(parts_t[s, lanes, :], joined[s])).astype(BF)
        share(9 + 2 * gate, grad[:, :C])
        share(10 + 2 * gate, grad[:, C:])
    share(13, over_steps(lambda s: mm(parts_t[s, 0:C, :], joined[s, :, 0:C])).astype(BF))
    share(14, over_steps(lambda s: mm(parts_t[s, 0:C, :], gated_all[s])).astype(BF))
    grad_head = mm(grad_out_ref[0], joined[1, :, C : 2 * C]) + mm(grad_out_ref[1], last_state[...])
    grad_head = jnp.concatenate([grad_head, jnp.zeros((C - 8, C), F32)], axis=0)
    share(15, grad_head.T.astype(BF))
    for p in range(3):
        grad = over_steps(
            lambda s: mm(part_conv_t[s], windows[s, pl.ds(p * SIDE, CELLS), :])
        ).astype(BF)
        for q in range(3):
            share(3 * p + q, grad[:, q * C : (q + 1) * C].T)
    for store in stores:
        store.wait()


def outside_kernel(part_conv_ref, conv_ref, to_next_ref, to_prev_ref):
    lines = [[], [], [], []]
    for step in range(STEPS):
        plane = part_conv_ref.at[step]
        for side, line in enumerate((plane[0], plane[SIDE - 1], plane[:, 0], plane[:, SIDE - 1])):
            lines[side].append(line_shifts(line.astype(F32)))
    taps = ((2, 1, 0), (8, 7, 6), (6, 3, 0), (8, 5, 2))
    outside = []
    for side in range(4):
        line = jnp.concatenate(lines[side], axis=0)
        total = jnp.zeros((STEPS * SIDE, C), F32)
        for k, tap in enumerate(taps[side]):
            total = total + mm_nt(line[:, k * C : (k + 1) * C], conv_ref[pl.ds(tap * C, C), :])
        outside.append(total.astype(BF))
    for step in range(STEPS):
        rows = slice(step * SIDE, (step + 1) * SIDE)
        to_next_ref[step, 0] = outside[3][rows]
        to_prev_ref[step, 0] = outside[2][rows]
        for ref in (to_next_ref, to_prev_ref):
            ref[step, 1] = outside[0][rows]
            ref[step, 2] = outside[1][rows]


def fields_kernel(
    belt_ref,
    turns_ref,
    part_conv_ref,
    own_ref,
    prev_ref,
    next_ref,
    conv_ref,
    grad_fields_ref,
    shifted,
):
    zero = jnp.zeros((SIDE, C), F32)
    for step in range(STEPS):
        store_shifts(
            shifted,
            step,
            zero,
            zero,
            part_conv_ref[step].astype(F32).reshape(SIDE, SIDE, C),
            zero,
            zero,
        )
        seams = seam_rows(
            belt_ref,
            turns_ref,
            own_ref[step, 1],
            own_ref[step, 2],
            prev_ref[step],
            next_ref[step],
        )
        left = prev_ref[step, 0].astype(F32)
        right = next_ref[step, 0].astype(F32)
        for part in range(4):
            at = part * 8
            grad = jnp.zeros((8 * SIDE, C), F32)
            for p in range(3):
                for q in range(3):
                    lanes = slice((2 - q) * C, (3 - q) * C)
                    window = shifted[step, pl.ds((at + 2 - p) * SIDE, 8 * SIDE), lanes]
                    tap = 3 * p + q
                    grad = grad + mm_nt(window, conv_ref[tap * C : (tap + 1) * C, :])
            grad = grad.reshape(8, SIDE, C)
            col = iota((8, SIDE, C), 1)
            row = iota((8, SIDE, C), 0)
            grad = grad + jnp.where(col == 0, left[at : at + 8][:, None, :], 0.0)
            grad = grad + jnp.where(col == SIDE - 1, right[at : at + 8][:, None, :], 0.0)
            if part == 0:
                grad = grad + jnp.where(row == 0, seams[:SIDE][None], 0.0)
            if part == 3:
                grad = grad + jnp.where(row == 7, seams[SIDE:][None], 0.0)
            grad_fields_ref[step, at : at + 8] = grad.astype(BF)


def in_vmem():
    return pl.BlockSpec(memory_space=pltpu.VMEM)


def in_smem():
    return pl.BlockSpec(memory_space=pltpu.SMEM)


def params(mebibytes=60):
    return pltpu.CompilerParams(vmem_limit_bytes=mebibytes << 20)


def shape(dims, kind=BF):
    return jax.ShapeDtypeStruct(dims, kind)


EDGE = (STEPS, 3, SIDE, C)


def edges_call(fields):
    return pl.pallas_call(
        edges_kernel,
        out_shape=(shape(EDGE), shape(EDGE)),
        in_specs=[in_vmem()],
        out_specs=(in_vmem(), in_vmem()),
        compiler_params=params(8),
        name="edges",
    )(fields)


def early_call(fields, conv):
    anywhere = pl.BlockSpec(memory_space=pl.ANY)
    raw = (STEPS, CELLS, C)
    return pl.pallas_call(
        early_kernel,
        out_shape=shape(raw, F32),
        in_specs=[anywhere] * 2,
        out_specs=anywhere,
        scratch_shapes=[
            pltpu.VMEM(fields.shape, BF),
            pltpu.VMEM(conv.shape, BF),
            pltpu.VMEM((STEPS, CELLS + 2 * SIDE, 3 * C), BF),
            pltpu.VMEM(raw, F32),
            pltpu.SemaphoreType.DMA((7,)),
        ],
        compiler_params=params(),
        cost_estimate=pl.CostEstimate(
            flops=2 * STEPS * CELLS * C * C * 9, bytes_accessed=5 << 20, transcendentals=0
        ),
        name="early",
    )(fields, conv)


def main_call(*args):
    anywhere = pl.BlockSpec(memory_space=pl.ANY)
    return pl.pallas_call(
        main_kernel,
        out_shape=(
            shape((CELLS, C), F32),
            shape((STEPS, CELLS, C)),
            shape((4, 32, 16, C)),
            shape((4, 32, 16, C)),
        ),
        in_specs=[in_smem()] * 2 + [anywhere] * 12,
        out_specs=(anywhere,) * 4,
        scratch_shapes=[pltpu.VMEM(arg.shape, arg.dtype) for arg in args[2:]]
        + [
            pltpu.VMEM((STEPS, CELLS + 2 * SIDE, 3 * C), BF),
            pltpu.VMEM((STEPS, CELLS, 2 * C), BF),
            pltpu.VMEM((STEPS, CELLS, C), BF),
            pltpu.VMEM((STEPS, 3 * C, CELLS), BF),
            pltpu.VMEM((STEPS, CELLS, C), BF),
            pltpu.VMEM((STEPS, C, CELLS), BF),
            pltpu.VMEM((CELLS, C), BF),
            pltpu.VMEM((CELLS, C), F32),
            pltpu.VMEM((16, 16, 16, C), BF),
            pltpu.SemaphoreType.DMA((12,)),
            pltpu.SemaphoreType.DMA((18,)),
        ],
        compiler_params=params(),
        name="steps",
    )(*args)


def outside_call(part_conv, conv):
    return pl.pallas_call(
        outside_kernel,
        out_shape=(shape(EDGE), shape(EDGE)),
        in_specs=[in_vmem()] * 2,
        out_specs=(in_vmem(), in_vmem()),
        compiler_params=params(),
        cost_estimate=pl.CostEstimate(flops=1 << 30, bytes_accessed=3 << 20, transcendentals=0),
        name="outside",
    )(part_conv.reshape(STEPS, SIDE, SIDE, C), conv)


def pair_kernel(left_ref, right_ref, out, out_ref, sems):
    stores = []
    for k in range(left_ref.shape[0]):
        out_ref[k] = (left_ref[k].astype(F32) + right_ref[k].astype(F32)).astype(BF)
        stores.append(pltpu.make_async_copy(out_ref.at[k], out.at[k], sems.at[k]))
        stores[k].start()
    for store in stores:
        store.wait()


def pair_call(left, right):
    return pl.pallas_call(
        pair_kernel,
        out_shape=shape(left.shape),
        in_specs=[in_vmem()] * 2,
        out_specs=pl.BlockSpec(memory_space=pl.ANY),
        scratch_shapes=[
            pltpu.VMEM(left.shape, BF),
            pltpu.SemaphoreType.DMA((left.shape[0],)),
        ],
        compiler_params=params(8),
        name="pair",
    )(left, right)


def added_kernel(pieces_ref, out_ref):
    total = pieces_ref[0].astype(F32)
    for k in range(1, pieces_ref.shape[0]):
        total = total + pieces_ref[k].astype(F32)
    out_ref[...] = total.astype(BF)


def added_call(pieces):
    return pl.pallas_call(
        added_kernel,
        out_shape=shape((32, 16, C)),
        in_specs=[in_vmem()],
        out_specs=in_vmem(),
        compiler_params=params(8),
        name="added",
    )(pieces)


def spread_kernel(pieces_ref, out, total_ref, sems):
    total = pieces_ref[0].astype(F32)
    for k in range(1, pieces_ref.shape[0]):
        total = total + pieces_ref[k].astype(F32)
    total_ref[...] = total.astype(BF)
    stores = [pltpu.make_async_copy(total_ref, out.at[k], sems.at[k]) for k in range(16)]
    for store in stores:
        store.start()
    for store in stores:
        store.wait()


def spread_call(pieces):
    return pl.pallas_call(
        spread_kernel,
        out_shape=shape((16, 16, C)),
        in_specs=[in_vmem()],
        out_specs=pl.BlockSpec(memory_space=pl.ANY),
        scratch_shapes=[pltpu.VMEM((16, C), BF), pltpu.SemaphoreType.DMA((16,))],
        compiler_params=params(8),
        name="spread",
    )(pieces)


def fields_call(*args):
    return pl.pallas_call(
        fields_kernel,
        out_shape=shape((STEPS, SIDE, SIDE, C)),
        in_specs=[in_smem()] * 2 + [in_vmem()] * 5,
        out_specs=in_vmem(),
        scratch_shapes=[pltpu.VMEM((STEPS, CELLS + 2 * SIDE, 3 * C), BF)],
        compiler_params=params(20),
        cost_estimate=pl.CostEstimate(
            flops=2 * STEPS * CELLS * C * C * 9, bytes_accessed=4 << 20, transcendentals=0
        ),
        name="fields",
    )(*args)


RING = [(i, (i + 1) % 16) for i in range(16)]
BACK = [((i + 1) % 16, i) for i in range(16)]


def finish_kernel(whole_ref, conv_ref, update_ref, reset_ref, candidate_ref, head_ref):
    def block(k):
        return whole_ref[((k // 4) % 2) * 8 + (k % 4) * 2 + k // 8].astype(F32)

    for tap in range(9):
        conv_ref[tap] = block(tap)
    for ref, first in ((update_ref, 9), (reset_ref, 11), (candidate_ref, 13)):
        ref[:, 0:C] = block(first)
        ref[:, C : 2 * C] = block(first + 1)
    head_ref[...] = block(15).T[:8]


def finish_call(whole):
    gate = shape((16, 2 * C), F32)
    return pl.pallas_call(
        finish_kernel,
        out_shape=(shape((9, 16, C), F32), gate, gate, gate, shape((8, 16), F32)),
        in_specs=[in_vmem()],
        out_specs=tuple([in_vmem()] * 5),
        compiler_params=params(8),
        name="finish",
    )(whole)


EVERY = ("x_hi", "y", "core", "x_lo", "z")


def groups_of(*axes_of_core):
    devices = np.arange(256).reshape(2, 4, 2, 2, 8)
    found = []
    for core, axes in enumerate(axes_of_core):
        inner = [("x_hi", "y", "x_lo", "z").index(axis) for axis in axes]
        outer = [axis for axis in range(4) if axis not in inner]
        here = devices[:, :, core].transpose(outer + inner)
        size = math.prod(here.shape[len(outer) :])
        found += here.reshape(-1, size).tolist()
    return found


FIRST = groups_of(("y",), ("x_hi", "x_lo"))
SECOND = groups_of(("x_hi", "x_lo", "z"), ("y", "z"))


def body(
    fields_in,
    state_start,
    state_adjoint,
    output_grad,
    conv_weight,
    w_update,
    w_reset,
    w_candidate,
    head_weight,
    neighbor_tile,
    seam_turns,
):
    dp = ("x_hi", "y", "core")
    belt = ("x_lo", "z")
    seams = (neighbor_tile.T, seam_turns.T)
    fields = fields_in[0, 0]
    conv = conv_weight.reshape(9 * C, C)
    to_next, to_prev = edges_call(fields)
    prev = lax.ppermute(to_next, belt, RING)
    following = lax.ppermute(to_prev, belt, BACK)
    raw = early_call(fields, conv).reshape(STEPS, SIDE, SIDE, C)
    grad_state, part_conv, keep, send = main_call(
        *seams,
        fields,
        prev,
        following,
        conv,
        raw,
        state_start.reshape(CELLS, C),
        w_update,
        w_reset,
        w_candidate,
        state_adjoint.reshape(CELLS, C),
        output_grad[0, 0],
        head_weight,
    )
    got = lax.ppermute(send, "core", [(0, 1), (1, 0)])
    out_next, out_prev = outside_call(part_conv, conv)
    got, out_next, out_prev = lax.optimization_barrier((got, out_next, out_prev))
    held = pair_call(keep, got)
    held = lax.all_to_all(held, EVERY, 0, 0, axis_index_groups=FIRST, tiled=True)
    prev = lax.ppermute(out_next, belt, RING)
    following = lax.ppermute(out_prev, belt, BACK)
    held, prev, following = lax.optimization_barrier((held, prev, following))
    held = added_call(held)
    held = lax.all_to_all(held, EVERY, 0, 0, axis_index_groups=SECOND, tiled=True)
    held, prev, following = lax.optimization_barrier((held, prev, following))
    grad_fields = fields_call(*seams, part_conv, out_next, prev, following, conv)
    whole = spread_call(held)
    whole = lax.all_to_all(whole, dp, 0, 0, tiled=True)
    whole, grad_fields = lax.optimization_barrier((whole, grad_fields))
    grad_conv, grad_update, grad_reset, grad_candidate, grad_head = finish_call(whole)
    return (
        grad_fields[None, None],
        grad_state.reshape(1, 1, SIDE, SIDE, C),
        grad_conv,
        grad_update.T,
        grad_reset.T,
        grad_candidate.T,
        grad_head,
    )


def solution(mesh):
    cube = Mesh(mesh.devices.reshape(2, 4, 2, 2, 8), ("x_hi", "y", "core", "x_lo", "z"))
    dp = ("x_hi", "y", "core")
    tile = ("x_lo", "z")
    return jax.shard_map(
        body,
        mesh=cube,
        in_specs=(
            P(dp, tile, None, None, None, None),
            P(dp, tile, None, None, None),
            P(dp, tile, None, None, None),
            P(dp, tile, None, None, None),
            P(),
            P(),
            P(),
            P(),
            P(),
            P(),
            P(),
        ),
        out_specs=(
            P(dp, tile, None, None, None, None),
            P(dp, tile, None, None, None),
            P(None, tile, None),
            P(None, tile),
            P(None, tile),
            P(None, tile),
            P(None, tile),
        ),
        check_vma=False,
    )
```
